32 devices in a mesh: dp: 4 (over x, core), chan: 8 (over z, y).
Axes of the slice: x: 2, y: 2, z: 4, core: 2. Of those that a mesh axis runs over, the one named last changes fastest.
Arguments:
- canvas: float32 [8, 3, 64, 64], P('dp'), may hold values from -6 to 6
- crop_boxes: int32 [8, 3], P('dp'), may hold values from 0 to 48, as said below
- time_steps: int32 [8], P('dp'), may hold values from 0 to 999
- noise_field: float32 [3, 8, 256], P(None, 'dp'), may hold values from -6 to 6
- step_count: int32 [1], replicated, may hold values from 1 to 20
- w_in: float32 [256, 27], P('chan'), may hold values from -1.25 to 1.25
- m_in: float32 [256, 27], P('chan'), may hold values from -0.03125 to 0.03125
- v_in: float32 [256, 27], P('chan'), may hold values from 2.4414062e-06 to 9.765625e-06
- conv_w: float32 [4, 256, 2304], P(None, 'chan'), may hold values from -0.125 to 0.125
- conv_m: float32 [4, 256, 2304], P(None, 'chan'), may hold values from -0.03125 to 0.03125
- conv_v: float32 [4, 256, 2304], P(None, 'chan'), may hold values from 2.4414062e-06 to 9.765625e-06
- temb_w: float32 [2, 256, 512], P(None, 'chan'), may hold values from -0.25 to 0.25
- temb_m: float32 [2, 256, 512], P(None, 'chan'), may hold values from -0.03125 to 0.03125
- temb_v: float32 [2, 256, 512], P(None, 'chan'), may hold values from 2.4414062e-06 to 9.765625e-06
- attn_w: float32 [4, 256, 256], P(None, 'chan'), may hold values from -0.5 to 0.5
- attn_m: float32 [4, 256, 256], P(None, 'chan'), may hold values from -0.03125 to 0.03125
- attn_v: float32 [4, 256, 256], P(None, 'chan'), may hold values from 2.4414062e-06 to 9.765625e-06
- out_w: float32 [3, 2304], replicated, may hold values from -0.125 to 0.125
- out_m: float32 [3, 2304], replicated, may hold values from -0.03125 to 0.03125
- out_v: float32 [3, 2304], replicated, may hold values from 2.4414062e-06 to 9.765625e-06
- vectors: float32 [22, 256], P(None, 'chan')
- vec_m: float32 [22, 256], P(None, 'chan'), may hold values from -0.03125 to 0.03125
- vec_v: float32 [22, 256], P(None, 'chan'), may hold values from 2.4414062e-06 to 9.765625e-06
Outputs:
- loss: float32 [], replicated
- matrix_norms: float32 [12, 2], replicated
- w_in_new: float32 [256, 27], P('chan')
- m_in_new: float32 [256, 27], P('chan')
- v_in_new: float32 [256, 27], P('chan')
- conv_new: float32 [4, 256, 2304], P(None, 'chan')
- conv_m_new: float32 [4, 256, 2304], P(None, 'chan')
- conv_v_new: float32 [4, 256, 2304], P(None, 'chan')
- conv_low: bfloat16 [4, 256, 2304], P(None, 'chan')
- temb_new: float32 [2, 256, 512], P(None, 'chan')
- temb_m_new: float32 [2, 256, 512], P(None, 'chan')
- temb_v_new: float32 [2, 256, 512], P(None, 'chan')
- temb_low: bfloat16 [2, 256, 512], P(None, 'chan')
- attn_new: float32 [4, 256, 256], P(None, 'chan')
- attn_m_new: float32 [4, 256, 256], P(None, 'chan')
- attn_v_new: float32 [4, 256, 256], P(None, 'chan')
- attn_low: bfloat16 [4, 256, 256], P(None, 'chan')
- out_new: float32 [3, 2304], replicated
- out_m_new: float32 [3, 2304], replicated
- out_v_new: float32 [3, 2304], replicated
- vec_new: float32 [22, 256], P(None, 'chan')
- vec_m_new: float32 [22, 256], P(None, 'chan')
- vec_v_new: float32 [22, 256], P(None, 'chan')
- attn_grad_sum: float32 [4, 256, 256], P(None, 'chan')
The draws below stay inside these ranges and needn't reach their ends.
Inputs may be any that keep to these rules, and one draw needn't show every extreme that they name: `crop_boxes`: row b holds the window's top row and left column, each from 0 to 48, and the side of the counted square, 4 + 12 * b // max(7, 1) plus 0 or 1, at most 16; the last image's side is 16, the first image's window is at row 48, column 0.
All inputs are finite; a program needn't handle non-finite values.
Results may differ from the reference program's by a relative error of at most 0.0092.
Values may be sent and summed in bfloat16 or wider, within the bound.
A program may use at most 192 MiB of HBM per device.

```python
import math
import jax
import jax.numpy as jnp
from jax import lax

C = 256
TEMB = 512
HW = 16
CANVAS = 64
GSIZE = 8
IMAGES = 8


def draw_crop_boxes(key, part):
    first_key, second_key, third_key = jax.random.split(key, 3)
    ladder = jnp.arange(IMAGES, dtype=jnp.int32)
    top_rows = jax.random.randint(first_key, (IMAGES,), 0, CANVAS - HW + 1)
    left_cols = jax.random.randint(second_key, (IMAGES,), 0, CANVAS - HW + 1)
    top_rows = jnp.where(ladder == 0, CANVAS - HW, top_rows)
    left_cols = jnp.where(ladder == 0, 0, left_cols)
    least_side = HW // 4
    extent = least_side + (HW - least_side) * ladder // max(IMAGES - 1, 1) + jax.random.randint(third_key, (IMAGES,), 0, 2)
    extent = jnp.minimum(extent, HW)
    return jnp.stack([top_rows, left_cols, extent], axis=1).astype(jnp.int32)


def draw_vectors(key, part):
    gain_key, shift_key = jax.random.split(key)
    row_index = jnp.arange(22)[:, None]
    gains = jax.random.uniform(gain_key, (22, C), jnp.float32, 0.6, 1.4)
    shifts = 0.3 * jax.random.normal(shift_key, (22, C), jnp.float32)
    return jnp.where(row_index < 6, gains, shifts).astype(jnp.float32)


def touch_ends(result, key, smallest, top_value):
    spot = [jax.random.randint(jax.random.fold_in(key, axis), (), 0, length) for axis, length in enumerate(result.shape)]
    widest = result.shape.index(max(result.shape))
    beside = spot[:widest] + [(spot[widest] + 1) % result.shape[widest]] + spot[widest + 1:]
    return result.at[tuple(spot)].set(smallest).at[tuple(beside)].set(top_value)


def block_levels(own_key, dims, pieces, low, largest):
    loudness = 1.0
    for dim, shards_of in pieces:
        heights = jax.random.uniform(jax.random.fold_in(jax.random.fold_in(own_key, 6), dim), (shards_of,), jnp.float32, low / len(pieces), largest / len(pieces))
        loudness = loudness * jnp.repeat(jnp.exp(heights), dims[dim] // shards_of).reshape((-1,) + (1,) * (len(dims) - 1 - dim))
    return loudness


def normal_values(stream_key, dims, width, reach, cuts=(), kind=jnp.bfloat16):
    factor_of = block_levels(stream_key, dims, cuts, -0.22, 0.18) if cuts else 1.0
    array = jax.random.normal(stream_key, dims, jnp.float32) * width * factor_of
    return jnp.minimum(jnp.maximum(array, -reach), reach).astype(kind)


def setup_inputs(seed: int = 0) -> dict:
    streams_of = jax.random.split(jax.random.key(seed), 24)
    canvas = normal_values(streams_of[0], (IMAGES, 3, CANVAS, CANVAS), 1.0, 6.0, ((0, 4),), jnp.float32)
    crop_boxes = draw_crop_boxes(jax.random.fold_in(streams_of[23], 71), 0)
    time_steps = touch_ends(jax.random.randint(streams_of[2], (IMAGES,), 0, 1000), jax.random.fold_in(streams_of[2], 1), 0, 999).astype(jnp.int32)
    noise_field = normal_values(streams_of[3], (3, IMAGES, HW * HW), 1.0, 6.0, ((1, 4),), jnp.float32)
    step_count = jax.random.randint(streams_of[4], (1,), 1, 21).astype(jnp.int32)
    w_in = normal_values(streams_of[5], (C, 27), 27 ** -0.5, 1.25, ((0, 8),), jnp.float32)
    m_in = normal_values(streams_of[6], (C, 27), (0.11 * (IMAGES * HW * HW) ** -0.5), 0.03125, ((0, 8),), jnp.float32)
    v_in = jnp.clip(jnp.exp(math.log(9.765624781721272e-06) - 1.3862944 * jax.random.uniform(streams_of[7], (C, 27), jnp.float32) ** block_levels(streams_of[7], (C, 27), ((0, 8),), -0.2, 0.2)), 2.441406195430318e-06, 9.765624781721272e-06)
    conv_w = normal_values(streams_of[8], (4, C, 9 * C), (9 * C) ** -0.5, 0.125, ((1, 8),), jnp.float32)
    conv_m = normal_values(streams_of[9], (4, C, 9 * C), (0.11 * (IMAGES * HW * HW) ** -0.5), 0.03125, ((1, 8),), jnp.float32)
    conv_v = jnp.clip(jnp.exp(math.log(9.765624781721272e-06) - 1.3862944 * jax.random.uniform(streams_of[10], (4, C, 9 * C), jnp.float32) ** block_levels(streams_of[10], (4, C, 9 * C), ((1, 8),), -0.2, 0.2)), 2.441406195430318e-06, 9.765624781721272e-06)
    temb_w = normal_values(streams_of[11], (2, C, TEMB), TEMB ** -0.5, 0.25, ((1, 8),), jnp.float32)
    temb_m = normal_values(streams_of[12], (2, C, TEMB), (0.11 * (IMAGES * HW * HW) ** -0.5), 0.03125, ((1, 8),), jnp.float32)
    temb_v = jnp.clip(jnp.exp(math.log(9.765624781721272e-06) - 1.3862944 * jax.random.uniform(streams_of[13], (2, C, TEMB), jnp.float32) ** block_levels(streams_of[13], (2, C, TEMB), ((1, 8),), -0.2, 0.2)), 2.441406195430318e-06, 9.765624781721272e-06)
    attn_w = normal_values(streams_of[14], (4, C, C), (C // 2) ** -0.5, 0.5, ((1, 8),), jnp.float32)
    attn_m = normal_values(streams_of[15], (4, C, C), (0.11 * (IMAGES * HW * HW) ** -0.5), 0.03125, ((1, 8),), jnp.float32)
    attn_v = jnp.clip(jnp.exp(math.log(9.765624781721272e-06) - 1.3862944 * jax.random.uniform(streams_of[16], (4, C, C), jnp.float32) ** block_levels(streams_of[16], (4, C, C), ((1, 8),), -0.2, 0.2)), 2.441406195430318e-06, 9.765624781721272e-06)
    out_w = normal_values(streams_of[17], (3, 9 * C), (9 * C) ** -0.5, 0.125, (), jnp.float32)
    out_m = normal_values(streams_of[18], (3, 9 * C), (0.11 * (IMAGES * HW * HW) ** -0.5), 0.03125, (), jnp.float32)
    out_v = jnp.clip(jnp.exp(jax.random.uniform(streams_of[19], (3, 9 * C), jnp.float32, math.log(2.441406195430318e-06), math.log(9.765624781721272e-06))), 2.441406195430318e-06, 9.765624781721272e-06)
    vectors = draw_vectors(jax.random.fold_in(streams_of[23], 71), 0)
    vec_m = normal_values(streams_of[21], (22, C), (0.11 * (IMAGES * HW * HW) ** -0.5), 0.03125, ((1, 8),), jnp.float32)
    vec_v = jnp.clip(jnp.exp(math.log(9.765624781721272e-06) - 1.3862944 * jax.random.uniform(streams_of[22], (22, C), jnp.float32) ** block_levels(streams_of[22], (22, C), ((1, 8),), -0.2, 0.2)), 2.441406195430318e-06, 9.765624781721272e-06)
    return {"canvas": canvas, "crop_boxes": crop_boxes, "time_steps": time_steps, "noise_field": noise_field, "step_count": step_count, "w_in": w_in, "m_in": m_in, "v_in": v_in, "conv_w": conv_w, "conv_m": conv_m, "conv_v": conv_v, "temb_w": temb_w, "temb_m": temb_m, "temb_v": temb_v, "attn_w": attn_w, "attn_m": attn_m, "attn_v": attn_v, "out_w": out_w, "out_m": out_m, "out_v": out_v, "vectors": vectors, "vec_m": vec_m, "vec_v": vec_v}


@jax.custom_vjp
def low(v):
    return lax.optimization_barrier(v.astype(jnp.bfloat16)).astype(jnp.float32)

@jax.custom_vjp
def low_back(v):
    return v

def low_keep(v):
    return (low(v), None)

def low_pass(kept, grad):
    return (grad,)

def back_keep(v):
    return (v, None)

def back_low(kept, grad):
    return (low(grad),)
low.defvjp(low_keep, low_pass)
low_back.defvjp(back_keep, back_low)
HIGH = lax.Precision.HIGHEST
NORM_EPS = 1e-05
BETA_ONE = 0.9
BETA_TWO = 0.95
ADAM_EPS = 1e-06
DECAY = 0.01
RATE = 0.3

def product(weight, field):
    return jnp.dot(weight, field, precision=HIGH, preferred_element_type=jnp.float32)

def to_columns(field, images):
    field_depth = field.shape[0]
    square = field.reshape(field_depth, images, HW, HW)
    padded = jnp.pad(square, ((0, 0), (0, 0), (1, 1), (1, 1)))
    shifted = [padded[:, :, row_off:row_off + HW, col_off:col_off + HW] for row_off in range(3) for col_off in range(3)]
    return jnp.stack(shifted, axis=1).reshape(field_depth * 9, images * HW * HW)

def group_act(field, gain, shift):
    field_depth, rows_all = field.shape
    images = rows_all // (HW * HW)
    grouped = field.reshape(field_depth // GSIZE, GSIZE, images, HW * HW)
    centre = lax.optimization_barrier(jnp.mean(grouped, axis=(1, 3), keepdims=True))
    spread = lax.optimization_barrier(jnp.mean((grouped - centre) ** 2, axis=(1, 3), keepdims=True))
    scaled = ((grouped - centre) * lax.rsqrt(spread + NORM_EPS)).reshape(field_depth, rows_all)
    return jax.nn.silu(scaled * gain[:, None] + shift[:, None])

def prepare(canvas, crop_boxes, time_steps):
    images = canvas.shape[0]

    def crop_one(picture, box_row):
        return lax.dynamic_slice(picture, (jnp.int32(0), box_row[0], box_row[1]), (3, HW, HW))
    windows = jax.vmap(crop_one)(canvas, crop_boxes)
    clean = jnp.transpose(windows, (1, 0, 2, 3)).reshape(3, images * HW * HW).astype(jnp.float32)
    ladder = jnp.arange(HW, dtype=jnp.int32)
    inside = ladder[None, :] < crop_boxes[:, 2:3]
    mask_rows = (inside[:, :, None] & inside[:, None, :]).astype(jnp.float32).reshape(images * HW * HW)
    phase = (time_steps.astype(jnp.float32) / 1000.0 + 0.008) / 1.008
    alpha_bar = jnp.cos(phase * (math.pi / 2)) ** 2
    abar_rows = jnp.repeat(alpha_bar, HW * HW)
    frequency = jnp.exp(-math.log(10000.0) * jnp.arange(TEMB // 2, dtype=jnp.float32) / (TEMB // 2))
    angles = time_steps.astype(jnp.float32)[None, :] * frequency[:, None]
    embedding = jnp.concatenate([jnp.sin(angles), jnp.cos(angles)], axis=0)
    return (clean, mask_rows, abar_rows, embedding)

def per_image_add(field, shift):
    field_depth, rows_all = field.shape
    images = shift.shape[1]
    return (field.reshape(field_depth, images, HW * HW) + shift[:, :, None]).reshape(field_depth, rows_all)

def res_block(hidden, block, conv_w, temb_w, vectors, temb_act):
    images = temb_act.shape[1]
    first_act = low(group_act(hidden, vectors[3 * block], vectors[6 + 3 * block]))
    middle = low_back(product(low(conv_w[2 * block]), to_columns(first_act, images))) + vectors[13 + 2 * block][:, None]
    shift = low_back(product(low(temb_w[block]), temb_act)) + vectors[17 + block][:, None]
    middle = per_image_add(middle, shift)
    second_act = low(group_act(middle, vectors[1 + 3 * block], vectors[7 + 3 * block]))
    branch = low_back(product(low(conv_w[2 * block + 1]), to_columns(second_act, images))) + vectors[14 + 2 * block][:, None]
    return hidden + branch

def attention(hidden, attn_w, vectors, images):
    normed = low(group_act(hidden, vectors[2], vectors[8]))
    triple = low_back(product(low(attn_w[:3].reshape(3 * C, C)), normed))
    query = low(triple[:C] + vectors[19][:, None]).reshape(C, images, HW * HW)
    key_part = low(triple[C:2 * C]).reshape(C, images, HW * HW)
    value = low(triple[2 * C:] + vectors[20][:, None]).reshape(C, images, HW * HW)
    scores = low_back(jnp.einsum('cbi,cbj->bij', query, key_part, precision=HIGH) * C ** (-0.5))
    probs = low(jax.nn.softmax(scores, axis=-1))
    mixed = jnp.einsum('bij,cbj->cbi', probs, value, precision=HIGH).reshape(C, images * HW * HW)
    mixed = low(low_back(mixed))
    return hidden + (low_back(product(low(attn_w[3]), mixed)) + vectors[21][:, None])

def forward_loss(w_in, conv_w, temb_w, attn_w, out_w, vectors, noisy, temb_act, noise_rows, mask_rows, count_total):
    images = temb_act.shape[1]
    hidden = low_back(product(low(w_in), to_columns(low(noisy), images))) + vectors[12][:, None]
    hidden = res_block(hidden, 0, conv_w, temb_w, vectors, temb_act)
    hidden = attention(hidden, attn_w, vectors, images)
    hidden = res_block(hidden, 1, conv_w, temb_w, vectors, temb_act)
    final_act = low(group_act(hidden, vectors[5], vectors[11]))
    pred = low_back(product(low(out_w), to_columns(final_act, images)))
    error = pred - noise_rows
    return jnp.sum(mask_rows * error * error) / count_total

def adapt(grad, first, second, count_step):
    first_new = BETA_ONE * first + (1.0 - BETA_ONE) * grad
    second_new = BETA_TWO * second + (1.0 - BETA_TWO) * grad * grad
    direction = first_new / (1.0 - BETA_ONE ** count_step) / (jnp.sqrt(second_new / (1.0 - BETA_TWO ** count_step)) + ADAM_EPS)
    return (first_new, second_new, direction)

def matrix_step(weight, first, second, grad, count_step):
    first_new, second_new, direction = adapt(grad, first, second, count_step)
    update = direction + DECAY * weight
    stacked_w = weight.reshape((-1,) + weight.shape[-2:])
    stacked_u = update.reshape(stacked_w.shape)
    weight_sq = lax.optimization_barrier(jnp.sum(stacked_w * stacked_w, axis=(1, 2)))
    update_sq = lax.optimization_barrier(jnp.sum(stacked_u * stacked_u, axis=(1, 2)))
    ratio = jnp.sqrt(weight_sq / (update_sq + 1e-06))
    new_weight = (stacked_w - RATE * ratio[:, None, None] * stacked_u).reshape(weight.shape)
    norms = jnp.stack([jnp.sqrt(weight_sq), jnp.sqrt(update_sq)], axis=1)
    return (new_weight, first_new, second_new, norms)

def reference(canvas, crop_boxes, time_steps, noise_field, step_count, w_in, m_in, v_in, conv_w, conv_m, conv_v, temb_w, temb_m, temb_v, attn_w, attn_m, attn_v, out_w, out_m, out_v, vectors, vec_m, vec_v):
    clean, mask_rows, abar_rows, embedding = prepare(canvas, crop_boxes, time_steps)
    images = canvas.shape[0]
    noise_rows = noise_field.reshape(3, images * HW * HW)
    count_total = 3.0 * jnp.sum(mask_rows)
    noisy = jnp.sqrt(abar_rows) * clean + jnp.sqrt(1.0 - abar_rows) * noise_rows
    temb_act = low(jax.nn.silu(embedding))

    def loss_only(w_one, w_two, w_three, w_four, w_five, w_six):
        return forward_loss(w_one, w_two, w_three, w_four, w_five, w_six, noisy, temb_act, noise_rows, mask_rows, count_total)
    loss, pull_back = jax.vjp(loss_only, w_in, conv_w, temb_w, attn_w, out_w, vectors)
    grad_in, grad_conv, grad_temb, grad_attn, grad_out, grad_vec = pull_back(jnp.ones_like(loss))
    count_step = step_count[0].astype(jnp.float32)
    in_new, in_first, in_second, in_norms = matrix_step(w_in, m_in, v_in, grad_in, count_step)
    conv_new, conv_first, conv_second, conv_norms = matrix_step(conv_w, conv_m, conv_v, grad_conv, count_step)
    temb_new, temb_first, temb_second, temb_norms = matrix_step(temb_w, temb_m, temb_v, grad_temb, count_step)
    attn_new, attn_first, attn_second, attn_norms = matrix_step(attn_w, attn_m, attn_v, grad_attn, count_step)
    out_new, out_first, out_second, out_norms = matrix_step(out_w, out_m, out_v, grad_out, count_step)
    vec_first, vec_second, vec_dir = adapt(grad_vec, vec_m, vec_v, count_step)
    vec_new = vectors - RATE * vec_dir
    matrix_norms = jnp.concatenate([in_norms, conv_norms, temb_norms, attn_norms, out_norms], axis=0)
    return (loss, matrix_norms, in_new, in_first, in_second, conv_new, conv_first, conv_second, conv_new.astype(jnp.bfloat16), temb_new, temb_first, temb_second, temb_new.astype(jnp.bfloat16), attn_new, attn_first, attn_second, attn_new.astype(jnp.bfloat16), out_new, out_first, out_second, vec_new, vec_first, vec_second, grad_attn)
```

```python
import functools
import math

import jax
import jax.numpy as jnp
from jax import lax
from jax.experimental import pallas as pl
from jax.experimental.pallas import tpu as pltpu
from jax.sharding import PartitionSpec as P

TEMB = 512
HW = 16
PIX = HW * HW
GSIZE = 8
C = 256
TAPS = 9
KW = C * TAPS
HALF = 128 * TAPS
LANES = KW + C

NORM_EPS = 1e-05
BETA_ONE = 0.9
BETA_TWO = 0.95
ADAM_EPS = 1e-06
DECAY = 0.01
RATE = 0.3
F32 = jnp.float32
BF16 = jnp.bfloat16
HIGH = lax.Precision.HIGHEST
MESH = pl.DeviceIdType.MESH
NN = (((1,), (0,)), ((), ()))
NT = (((1,), (1,)), ((), ()))
TN = (((0,), (0,)), ((), ()))
MIB = 1024 * 1024

VEC_ROWS = 22
LOSS_ROW = 24
MAIN = HALF + 128 + 128
SUM_ROWS = 16


def dot(a, b, dims, precision=None):
    return lax.dot_general(a, b, dims, precision=precision, preferred_element_type=F32)


def iota(shape, axis):
    return lax.broadcasted_iota(jnp.int32, shape, axis)


def tap_order():
    wanted = (iota((1, HALF), 1) & 127) * TAPS + (iota((1, HALF), 1) >> 7)
    return jnp.where(iota((HALF, 1), 0) == wanted, 1.0, 0.0).astype(BF16)


def prep_kernel(lr, images, crop, conv_w, attn_w, w_in, temb_w, temb_act, vectors, out_w,
                shard, small, count, out_taps, rows_scr, in_scr, out_scr):
    order = tap_order()
    for k in range(4):
        weight = conv_w[k].astype(BF16)
        both = jnp.concatenate([weight[:, :HALF], weight[:, HALF:]], axis=0)
        mixed = dot(both, order, NN).astype(BF16)
        for tap in range(TAPS):
            for h in range(2):
                lanes = slice(tap * C + h * 128, tap * C + h * 128 + 128)
                shard[k * lr:(k + 1) * lr, lanes] = mixed[h * lr:(h + 1) * lr, tap * 128:(tap + 1) * 128]
        shard[k * lr:(k + 1) * lr, KW:LANES] = attn_w[k].astype(BF16)

    out_scr[...] = jnp.zeros_like(out_scr)
    for h in range(2):
        out_scr[h * 8:h * 8 + 3, :] = out_w[:, h * HALF:(h + 1) * HALF]
    out_mixed = dot(out_scr[...].astype(BF16), order, NN)
    for tap in range(TAPS):
        for h in range(2):
            out_taps[tap * 8:tap * 8 + 8, h * 128:(h + 1) * 128] = out_mixed[
                h * 8:h * 8 + 8, tap * 128:(tap + 1) * 128
            ]

    rows_scr[...] = jnp.zeros_like(rows_scr)
    rows_scr[0:VEC_ROWS, 0:lr] = vectors[...]
    for block in range(2):
        shift = dot(temb_act[...], temb_w[block].astype(BF16), NT)
        for b in range(images):
            row = VEC_ROWS + block * images + b
            rows_scr[row:row + 1, 0:lr] = (
                shift[b:b + 1, :] + vectors[17 + block:18 + block, :]
            ) + vectors[13 + 2 * block:14 + 2 * block, :]
    in_scr[...] = jnp.zeros_like(in_scr)
    in_scr[0:lr, 0:27] = w_in[...]
    turned = in_scr[...].T
    packed = [jnp.zeros((8, 128), F32), jnp.zeros((8, 128), F32)]
    for g in range(4):
        for i, rows in enumerate((rows_scr[g * 8:g * 8 + 8, :], turned[g * 8:g * 8 + 8, :])):
            packed[i] += rows if g == 0 else pltpu.roll(rows, g * lr, 1)
    small[0:8, :] = packed[0]
    small[8:16, :] = packed[1]

    total = jnp.int32(0)
    for b in range(images):
        side = jnp.minimum(jnp.maximum(crop[b, 2], 0), HW)
        total += 3 * side * side
    count[...] = jnp.full((8, 128), total, jnp.int32).astype(F32)


def gather_kernel(n, ny, nz, nx, dp, width, shard, small, count, whole, smalls, counts,
                  own_sem, near_send, near_recv, x_send, x_recv, core_send, core_recv,
                  small_send, small_recv, count_send, count_recv):
    me = lax.axis_index("chan")
    part = lax.axis_index("dp")
    z, y = me // ny, me % ny
    x, core = part // 2, part % 2

    def chan_of(k, l):
        return lax.rem(z + k + nz, nz) * ny + lax.rem(y + l + ny, ny)

    def part_of(m, c):
        return lax.rem(x + m + nx, nx) * 2 + c

    def lanes_of(p):
        return pl.ds(pl.multiple_of(p * width, 128), width)

    barrier = pltpu.get_barrier_semaphore()
    for k in range(1, n):
        pl.semaphore_signal(barrier, inc=1, device_id=(part, lax.rem(me + k, n)), device_id_type=MESH)
    for k in range(1, dp):
        pl.semaphore_signal(barrier, inc=1, device_id=(lax.rem(part + k, dp), me), device_id_type=MESH)

    own = [
        pltpu.make_async_copy(shard, whole.at[me], own_sem.at[0]),
        pltpu.make_async_copy(small, smalls.at[me], own_sem.at[1]),
        pltpu.make_async_copy(count, counts.at[part], own_sem.at[2]),
    ]
    for copy in own:
        copy.start()
    pl.semaphore_wait(barrier, n + dp - 2)

    sends = []

    def remote(src, dst, send_sem, recv_sem, target):
        return pltpu.make_async_remote_copy(
            src_ref=src, dst_ref=dst, send_sem=send_sem, recv_sem=recv_sem,
            device_id=target, device_id_type=MESH,
        )

    def send(*args):
        copy = remote(*args)
        copy.start()
        sends.append(copy)

    mine = lanes_of(part)
    order = [(k, l) for k in range(nz) for l in range(ny)][1:]
    place = {kl: o for o, kl in enumerate(order)}

    def slot(src, p):
        return whole.at[src, :, lanes_of(p)]

    for k in range(1, nz):
        send(shard.at[:, mine], slot(me, part), near_send.at[place[(k, 0)]],
             near_recv.at[place[(k, 0)]], (part, chan_of(k, 0)))
    for l in range(1, ny):
        send(shard.at[:, mine], slot(me, part), near_send.at[place[(0, l)]],
             near_recv.at[place[(0, l)]], (part, chan_of(0, l)))
    for k in range(1, n):
        target = lax.rem(me + k, n)
        send(small, smalls.at[me], small_send.at[k - 1], small_recv.at[k - 1], (part, target))
    for k in range(1, dp):
        target = lax.rem(part + k, dp)
        send(count, counts.at[part], count_send.at[k - 1], count_recv.at[k - 1], (target, me))

    def forward(kl):
        o = place[kl]
        src = chan_of(-kl[0], -kl[1])
        remote(shard.at[:, mine], slot(src, part), near_send.at[o], near_recv.at[o],
               (part, src)).wait_recv()
        for m in range(1, nx):
            send(slot(src, part), slot(src, part), x_send.at[m - 1, o], x_recv.at[m - 1, o],
                 (part_of(m, core), me))
        send(slot(src, part), slot(src, part), core_send.at[0, o], core_recv.at[0, o],
             (part_of(0, 1 - core), me))

    for k in range(1, nz):
        src = chan_of(-k, 0)
        o = place[(k, 0)]
        forward((k, 0))
        for l in range(1, ny):
            send(slot(src, part), slot(src, part), near_send.at[place[(k, l)]],
                 near_recv.at[place[(k, l)]], (part, chan_of(0, l)))
    for l in range(1, ny):
        forward((0, l))
    for k in range(1, nz):
        for l in range(1, ny):
            forward((k, l))
    for o, (k, l) in enumerate(order):
        src = chan_of(-k, -l)
        for m in range(1, nx):
            p = part_of(-m, core)
            remote(slot(src, p), slot(src, p), x_send.at[m - 1, o], x_recv.at[m - 1, o],
                   (p, me)).wait_recv()
            send(slot(src, p), slot(src, p), core_send.at[m, o], core_recv.at[m, o],
                 (part_of(0, 1 - core), me))
    for k in range(1, n):
        src = lax.rem(me - k + n, n)
        remote(small, smalls.at[src], small_send.at[k - 1], small_recv.at[k - 1],
               (part, src)).wait_recv()
    for k in range(1, dp):
        p = lax.rem(part - k + dp, dp)
        remote(count, counts.at[p], count_send.at[k - 1], count_recv.at[k - 1], (p, me)).wait_recv()
    for o, (k, l) in enumerate(order):
        src = chan_of(-k, -l)
        for m in range(nx):
            p = part_of(-m, 1 - core)
            remote(slot(src, p), slot(src, p), core_send.at[m, o], core_recv.at[m, o],
                   (part_of(0, 1 - core), me)).wait_recv()
    for copy in sends:
        copy.wait_send()
    for copy in own:
        copy.wait()


def group_sum(row):
    lane = iota(row.shape, 1)
    step = 1
    while step < GSIZE:
        up = pltpu.roll(row, C - step, 1)
        down = pltpu.roll(row, step, 1)
        row = row + jnp.where((lane & step) == 0, up, down)
        step *= 2
    return row


def row_sum(value):
    return jnp.sum(value, axis=0, keepdims=True)


def group_mean(row):
    wide = jnp.broadcast_to(row, (8, C))
    return group_sum(wide)[0:1] * (1.0 / (GSIZE * PIX))


def compute_kernel(n, lr, dp, images, crop, coefs, whole, smalls, counts, out_taps, temb_act,
                   canvas, noise, main, misc_out, misc_vec,
                   vec, w_in, hidden, xhat, dact, rstd, col0, col1, col2, col3, taps0, rows_scr, acts,
                   q_scr, k_scr, v_scr, probs, mixed_scr, gvec, gconv, gsum):
    cols = (col0, col1, col2, col3)
    d = lax.axis_index("chan")
    rows_all = images * PIX
    scale = C ** -0.5

    def span(b):
        return slice(b * PIX, (b + 1) * PIX)

    def conv_weight(k):
        return whole[:, k * lr:(k + 1) * lr, 0:KW].reshape(C, KW)

    def attn_weight(k):
        return whole[:, k * lr:(k + 1) * lr, KW:LANES].reshape(C, C)

    vec[...] = jnp.zeros_like(vec)
    w_in[...] = jnp.zeros_like(w_in)
    lane_wide = iota((16, C), 1)
    for j in range(n):
        block = jnp.concatenate([smalls[j], jnp.zeros((16, 128), F32)], axis=1)
        for g in range(4):
            piece = jnp.where((lane_wide >= g * lr) & (lane_wide < (g + 1) * lr), block, 0.0)
            move = (j - g) * lr % C
            if move:
                piece = pltpu.roll(piece, move, 1)
            vec[g * 8:g * 8 + 8, :] += piece[0:8]
            w_in[g * 8:g * 8 + 8, :] += piece[8:16]

    def vrow(i):
        return vec[i:i + 1, :]

    total = counts[0, 0:1, 0:1]
    for k in range(1, dp):
        total = total + counts[k, 0:1, 0:1]

    lane = iota((1, PIX), 1)
    pix_x, pix_y = lane & (HW - 1), lane >> 4
    size = canvas.shape[2]
    noise_rows = []
    mask_rows = []
    noisy_rows = []
    for b in range(images):
        pick = jnp.where(iota((size, PIX), 0) == crop[b, 1] + pix_x, 1.0, 0.0)
        flat = canvas[b].reshape(3 * size, size)
        spread = dot(flat, pick, NN, HIGH).reshape(3, size, PIX)
        chosen = iota((size, PIX), 0) == crop[b, 0] + pix_y
        clean = jnp.sum(jnp.where(chosen[None], spread, 0.0), axis=1)
        noise_b = noise[:, b, :]
        noisy_rows.append(coefs[0, b] * clean + coefs[1, b] * noise_b)
        noise_rows.append(noise_b)
        side = crop[b, 2]
        mask_rows.append(jnp.where((pix_x < side) & (pix_y < side), 1.0, 0.0))
    zeros5 = jnp.zeros((5, rows_all), F32)
    noisy = jnp.concatenate([jnp.concatenate(noisy_rows, axis=1), zeros5], axis=0)
    noise_all = jnp.concatenate([jnp.concatenate(noise_rows, axis=1), zeros5], axis=0)
    mask_all = jnp.concatenate(mask_rows, axis=1)

    lane_all = iota((8, rows_all), 1)
    px, py = lane_all & (HW - 1), (lane_all >> 4) & (HW - 1)

    def tap_shift(field, tap):
        dy, dx = tap // 3 - 1, tap % 3 - 1
        move = -(dy * HW + dx) % rows_all
        out = pltpu.roll(field, move, 1) if move else field
        inside = (px + dx >= 0) & (px + dx < HW) & (py + dy >= 0) & (py + dy < HW)
        return jnp.where(inside, out, 0.0)

    noisy = noisy.astype(BF16).astype(F32)
    rows_scr[...] = jnp.zeros_like(rows_scr)
    for tap in range(TAPS):
        moved = tap_shift(noisy, tap)
        for colour in range(3):
            rows_scr[colour * TAPS + tap:colour * TAPS + tap + 1, :] = moved[colour:colour + 1]
    taps0[...] = rows_scr[...].astype(BF16)
    hidden[0] = dot(taps0[...], w_in[...].astype(BF16), TN) + vrow(12)

    col_x = iota((PIX, C), 0) & (HW - 1)

    def norm_fwd(i, value, gain, shift, store):
        for b in range(images):
            part = value[span(b)]
            centred = part - group_mean(row_sum(part))
            inv = lax.rsqrt(group_mean(row_sum(centred * centred)) + NORM_EPS)
            normed = centred * inv
            scaled = normed * gain + shift
            gate = 0.5 * jnp.tanh(0.5 * scaled) + 0.5
            act = scaled * gate
            xhat[i, span(b), :] = normed
            dact[i, span(b), :] = gate + act * (1.0 - gate)
            rstd[i * images + b:i * images + b + 1, :] = inv
            store(b, act)

    def norm_back(i, grad, gain_row):
        outs = []
        gain = vrow(gain_row)
        gain_sum = jnp.zeros((1, C), F32)
        shift_sum = jnp.zeros((1, C), F32)
        for b in range(images):
            slope = grad[span(b)] * dact[i, span(b), :]
            normed = xhat[i, span(b), :]
            shift_b = row_sum(slope)
            gain_b = row_sum(slope * normed)
            mean_one = group_mean(shift_b * gain)
            mean_two = group_mean(gain_b * gain)
            inv = rstd[i * images + b:i * images + b + 1, :]
            outs.append(inv * (slope * gain - mean_one - normed * mean_two))
            gain_sum += gain_b
            shift_sum += shift_b
        gvec[gain_row:gain_row + 1, :] = gain_sum
        gvec[6 + gain_row:7 + gain_row, :] = shift_sum
        return jnp.concatenate(outs, axis=0)

    blank = jnp.zeros((HW, C), BF16)

    def store_cols(ref, b, act):
        left = jnp.where(col_x > 0, pltpu.roll(act, 1, 0), 0.0)
        right = jnp.where(col_x < HW - 1, pltpu.roll(act, PIX - 1, 0), 0.0)
        for dx, moved in enumerate((left, act, right)):
            low = moved.astype(BF16)
            for dy in range(3):
                lanes = slice((3 * dy + dx) * C, (3 * dy + dx + 1) * C)
                base = b * PIX
                if dy == 0:
                    ref[base:base + HW, lanes] = blank
                    ref[base + HW:base + PIX, lanes] = low[:PIX - HW]
                elif dy == 1:
                    ref[base:base + PIX, lanes] = low
                else:
                    ref[base:base + PIX - HW, lanes] = low[HW:]
                    ref[base + PIX - HW:base + PIX, lanes] = blank

    def add_rows(value, first):
        return jnp.concatenate(
            [value[span(b)] + vrow(first + b) for b in range(images)], axis=0
        )

    def block_fwd(block, source, target):
        norm_fwd(3 * block, hidden[source], vrow(3 * block), vrow(6 + 3 * block),
                 functools.partial(store_cols, cols[2 * block]))
        middle = dot(cols[2 * block][...], conv_weight(2 * block), NT)
        middle = add_rows(middle, VEC_ROWS + block * images)
        norm_fwd(3 * block + 1, middle, vrow(3 * block + 1), vrow(7 + 3 * block),
                 functools.partial(store_cols, cols[2 * block + 1]))
        branch = dot(cols[2 * block + 1][...], conv_weight(2 * block + 1), NT)
        hidden[target] = hidden[source] + (branch + vrow(14 + 2 * block))

    def store_act(index):
        def store(b, act):
            acts[index, span(b), :] = act.astype(BF16)
        return store

    block_fwd(0, 0, 1)

    norm_fwd(2, hidden[1], vrow(2), vrow(8), store_act(0))
    q_scr[...] = (dot(acts[0], attn_weight(0), NT) + vrow(19)).astype(BF16)
    k_scr[...] = dot(acts[0], attn_weight(1), NT).astype(BF16)
    v_scr[...] = (dot(acts[0], attn_weight(2), NT) + vrow(20)).astype(BF16)
    for b in range(images):
        scores = dot(q_scr[span(b), :], k_scr[span(b), :], NT) * scale
        raised = jnp.exp(scores - jnp.max(scores, axis=1, keepdims=True))
        soft = raised / jnp.sum(raised, axis=1, keepdims=True)
        probs[b] = soft
        mixed_scr[span(b), :] = dot(soft.astype(BF16), v_scr[span(b), :], NN).astype(BF16)
    hidden[0] = hidden[1] + (dot(mixed_scr[...], attn_weight(3), NT) + vrow(21))

    block_fwd(1, 0, 1)
    norm_fwd(5, hidden[1], vrow(5), vrow(11), store_act(1))

    out_low = out_taps[...].astype(BF16)
    fanned = dot(out_low, acts[1], NT)
    pred = jnp.zeros((8, rows_all), F32)
    for tap in range(TAPS):
        pred += tap_shift(fanned[tap * 8:tap * 8 + 8], tap)
    error = pred - noise_all
    masked = mask_all * error
    inverse = 1.0 / total
    loss = jnp.sum(jnp.sum(masked * error, axis=1, keepdims=True), axis=0, keepdims=True) * inverse
    grad_pred = (2.0 * masked * inverse).astype(BF16).astype(F32)
    spread_pred = jnp.concatenate(
        [tap_shift(grad_pred, TAPS - 1 - tap) for tap in range(TAPS)], axis=0
    ).astype(BF16)
    out_grad = dot(spread_pred, acts[1], NN)
    grad = dot(spread_pred, out_low, TN)

    gvec[...] = jnp.zeros_like(gvec)
    pick_own = jnp.where(
        iota((lr, C), 1) == iota((lr, C), 0) + d * lr, 1.0, 0.0
    ).astype(BF16)

    def own_rows(low):
        return dot(pick_own, low, NT).astype(BF16)

    def conv_back(k, low):
        gconv[k * lr:(k + 1) * lr, 0:KW] = dot(own_rows(low), cols[k][...], NN)
        parts = dot(low, conv_weight(k), NN)
        outs = []
        hole = jnp.zeros((HW, C), F32)
        for b in range(images):
            sides = []
            for dx in range(3):
                up = parts[span(b), dx * C:(dx + 1) * C]
                mid = parts[span(b), (3 + dx) * C:(4 + dx) * C]
                down = parts[span(b), (6 + dx) * C:(7 + dx) * C]
                sides.append(
                    mid
                    + jnp.concatenate([up[HW:], hole], axis=0)
                    + jnp.concatenate([hole, down[:PIX - HW]], axis=0)
                )
            left = pltpu.roll(jnp.where(col_x > 0, sides[0], 0.0), PIX - 1, 0)
            right = pltpu.roll(jnp.where(col_x < HW - 1, sides[2], 0.0), 1, 0)
            outs.append(sides[1] + left + right)
        return jnp.concatenate(outs, axis=0)

    def block_back(block, grad):
        gvec[14 + 2 * block:15 + 2 * block, :] = row_sum(grad)
        back = conv_back(2 * block + 1, grad.astype(BF16))
        middle = norm_back(3 * block + 1, back, 3 * block + 1)
        gsum[...] = jnp.zeros_like(gsum)
        for b in range(images):
            gsum[b:b + 1, :] = row_sum(middle[span(b)])
        whole_sum = row_sum(gsum[...])
        gvec[13 + 2 * block:14 + 2 * block, :] = whole_sum
        gvec[17 + block:18 + block, :] = whole_sum
        own = dot(pick_own, gsum[...].astype(BF16), NT).astype(BF16)
        temb = dot(own, temb_act[...], NN)
        for j in range(4):
            top = (j % 2) * 2 * lr + block * lr
            gconv[top:top + lr, LANES + (j // 2) * 128:LANES + (j // 2) * 128 + 128] = (
                temb[:, j * 128:(j + 1) * 128]
            )
        back = conv_back(2 * block, middle.astype(BF16))
        return grad + norm_back(3 * block, back, 3 * block)

    grad = norm_back(5, grad, 5)
    grad = block_back(1, grad)

    gvec[21:22, :] = row_sum(grad)
    low = grad.astype(BF16)
    gconv[3 * lr:4 * lr, KW:LANES] = dot(own_rows(low), mixed_scr[...], NN)
    mixed_low = dot(low, attn_weight(3), NN).astype(BF16)
    grads_q, grads_k, grads_v = [], [], []
    for b in range(images):
        part = mixed_low[span(b)]
        soft = probs[b]
        grad_soft = dot(part, v_scr[span(b), :], NT)
        grads_v.append(dot(soft.astype(BF16), part, TN))
        weighed = soft * grad_soft
        slope = (weighed - soft * jnp.sum(weighed, axis=1, keepdims=True)).astype(BF16)
        grads_q.append(scale * dot(slope, k_scr[span(b), :], NN))
        grads_k.append(scale * dot(slope, q_scr[span(b), :], TN))
    back = jnp.zeros((rows_all, C), F32)
    for i, grads in enumerate((grads_q, grads_k, grads_v)):
        full = jnp.concatenate(grads, axis=0)
        if i != 1:
            gvec[19 + i // 2:20 + i // 2, :] = row_sum(full)
        low = full.astype(BF16)
        gconv[i * lr:(i + 1) * lr, KW:LANES] = dot(own_rows(low), acts[0], NN)
        back += dot(low, attn_weight(i), NN)
    grad = grad + norm_back(2, back, 2)

    grad = block_back(0, grad)
    gvec[12:13, :] = row_sum(grad)
    in_grad = dot(own_rows(grad.astype(BF16)), taps0[...], NT)

    order = tap_order()
    shaped = []
    for h in range(2):
        shaped.append(jnp.concatenate(
            [gconv[:, tap * C + h * 128:tap * C + h * 128 + 128] for tap in range(TAPS)], axis=1
        ).astype(BF16))
    for h in range(2):
        shaped.append(jnp.concatenate(
            [
                jnp.concatenate(
                    [out_grad[tap * 8:tap * 8 + 8, h * 128:(h + 1) * 128] for tap in range(TAPS)], axis=1
                ),
                jnp.zeros((8, HALF), F32),
            ], axis=0,
        ).astype(BF16))
    natural = dot(jnp.concatenate(shaped, axis=0), order, NT)
    for h in range(2):
        main[h, :, 0:HALF] = natural[h * 4 * lr:(h + 1) * 4 * lr].astype(BF16)
        main[h, :, HALF:HALF + 128] = gconv[:, KW + h * 128:KW + h * 128 + 128].astype(BF16)
        main[h, :, HALF + 128:MAIN] = gconv[:, LANES + h * 128:LANES + h * 128 + 128].astype(BF16)
        misc_out[h] = natural[8 * lr + h * 16:8 * lr + h * 16 + 8]
    own_vec = pltpu.roll(gvec[...], lax.rem(C - d * lr, C), 1)
    misc_vec[0] = own_vec[:, 0:128]
    misc_vec[0, LOSS_ROW:LOSS_ROW + 1, :] = jnp.broadcast_to(loss, (1, 128))
    misc_vec[1] = jnp.zeros((32, 128), F32)
    misc_vec[1, 0:lr, 0:32] = in_grad


def adapt(grad, first, second, fix_one, fix_two):
    first_new = BETA_ONE * first + (1.0 - BETA_ONE) * grad
    second_new = BETA_TWO * second + (1.0 - BETA_TWO) * grad * grad
    direction = first_new * fix_one / (jnp.sqrt(second_new * fix_two) + ADAM_EPS)
    return first_new, second_new, direction


def update_of(grad, first, second, weight, fix_one, fix_two):
    first_new, second_new, direction = adapt(grad, first, second, fix_one, fix_two)
    return first_new, second_new, direction + DECAY * weight


def matrix_parts(lr):
    parts = []
    for k in range(4):
        for h in range(2):
            parts.append((1 + k, "conv", k, slice(h * HALF, (h + 1) * HALF), h,
                          slice(k * lr, (k + 1) * lr), slice(0, HALF)))
    for k in range(2):
        for j in range(4):
            top = (j % 2) * 2 * lr + k * lr
            parts.append((5 + k, "temb", k, slice(j * 128, (j + 1) * 128), j // 2,
                          slice(top, top + lr), slice(HALF + 128, MAIN)))
    for k in range(4):
        for h in range(2):
            parts.append((7 + k, "attn", k, slice(h * 128, (h + 1) * 128), h,
                          slice(k * lr, (k + 1) * lr), slice(HALF, HALF + 128)))
    return parts


def reduce_kernel(n, lr, dp, nx, fixes, main, misc_out, misc_vec, w_in, m_in, v_in, conv_w, conv_m, conv_v,
                  temb_w, temb_m, temb_v, attn_w, attn_m, attn_v, out_w, out_m, out_v,
                  gmain, gout, gvec, norms,
                  one_main, one_out, one_vec, two_main, two_out, two_vec, last_main, last_out, last_vec,
                  mine, others, send_one, recv_one, send_two, recv_two, send_three, recv_three,
                  sum_send, sum_recv):
    me = lax.axis_index("chan")
    part = lax.axis_index("dp")
    x, core = part // 2, part % 2
    sibling = (x * 2 + 1 - core, me)

    barrier = pltpu.get_barrier_semaphore()
    for k in range(1, n):
        pl.semaphore_signal(barrier, inc=1, device_id=(part, lax.rem(me + k, n)), device_id_type=MESH)
    for m in range(1, nx):
        pl.semaphore_signal(barrier, inc=1, device_id=(lax.rem(x + m, nx) * 2 + core, me), device_id_type=MESH)
    pl.semaphore_signal(barrier, inc=1, device_id=sibling, device_id_type=MESH)
    pl.semaphore_wait(barrier, n + nx - 1)

    def remote(src, dst, send_sem, recv_sem, target):
        return pltpu.make_async_remote_copy(
            src_ref=src, dst_ref=dst, send_sem=send_sem, recv_sem=recv_sem,
            device_id=target, device_id_type=MESH,
        )

    trio = ((main, one_main, two_main, last_main), (misc_out, one_out, two_out, last_out),
            (misc_vec, one_vec, two_vec, last_vec))
    first = []
    for i, (source, landed, slots, last) in enumerate(trio):
        copy = remote(source.at[1 - core], landed, send_one.at[i], recv_one.at[i], sibling)
        copy.start()
        first.append(copy)
    second = []
    for i, (source, landed, slots, last) in enumerate(trio):
        first[i].wait_recv()
        slots[x] = (source[core].astype(F32) + landed[...].astype(F32)).astype(slots.dtype)
        for m in range(1, nx):
            copy = remote(slots.at[x], slots.at[x], send_two.at[i, m - 1], recv_two.at[i, m - 1],
                          (lax.rem(x + m, nx) * 2 + core, me))
            copy.start()
            second.append(copy)
    third = []
    for i, (source, landed, slots, last) in enumerate(trio):
        for m in range(1, nx):
            sender = lax.rem(x - m + nx, nx)
            remote(slots.at[sender], slots.at[sender], send_two.at[i, m - 1], recv_two.at[i, m - 1],
                   (sender * 2 + core, me)).wait_recv()
        summed = slots[0].astype(F32)
        for m in range(1, nx):
            summed = summed + slots[m].astype(F32)
        last[core] = summed.astype(last.dtype)
        copy = remote(last.at[core], last.at[core], send_three.at[i], recv_three.at[i], sibling)
        copy.start()
        third.append(copy)
    for i, (source, landed, slots, last) in enumerate(trio):
        remote(last.at[1 - core], last.at[1 - core], send_three.at[i], recv_three.at[i], sibling).wait_recv()
    gmain[...] = last_main[...].astype(F32)
    gout[...] = last_out[...]
    gvec[...] = last_vec[...]

    fix_one, fix_two = fixes[0], fixes[1]
    arrays = {"conv": (conv_w, conv_m, conv_v), "temb": (temb_w, temb_m, temb_v), "attn": (attn_w, attn_m, attn_v)}

    def squares(value):
        return jnp.sum(jnp.sum(value * value, axis=1, keepdims=True), axis=0, keepdims=True)

    sums = {}

    def note(number, weight, update):
        pair = (squares(weight), squares(update))
        if number in sums:
            pair = (sums[number][0] + pair[0], sums[number][1] + pair[1])
        sums[number] = pair

    for number, name, k, lanes, h, rows, held in matrix_parts(lr):
        w_ref, m_ref, v_ref = arrays[name]
        weight = w_ref[k, :, lanes]
        update = update_of(gmain[h, rows, held], m_ref[k, :, lanes], v_ref[k, :, lanes], weight, fix_one, fix_two)[2]
        note(number, weight, update)
    weight = w_in[...]
    note(0, weight, update_of(gvec[1, 0:lr, 0:27], m_in[...], v_in[...], weight, fix_one, fix_two)[2])
    for h in range(2):
        lanes = slice(h * HALF, (h + 1) * HALF)
        weight = out_w[:, lanes]
        note(11, weight, update_of(gout[h, 0:3, :], out_m[:, lanes], out_v[:, lanes], weight, fix_one, fix_two)[2])

    row = iota((SUM_ROWS, 128), 0)
    lane = iota((SUM_ROWS, 128), 1)
    table = jnp.zeros((SUM_ROWS, 128), F32)
    for number in range(11):
        for side in range(2):
            table = jnp.where((row == number) & (lane == side), sums[number][side], table)
    mine[...] = table
    copies = []
    for k in range(1, n):
        copy = remote(mine, others.at[me], sum_send.at[k - 1], sum_recv.at[k - 1], (part, lax.rem(me + k, n)))
        copy.start()
        copies.append(copy)
    others[me] = table
    for k in range(1, n):
        src = lax.rem(me - k + n, n)
        remote(mine, others.at[src], sum_send.at[k - 1], sum_recv.at[k - 1], (part, src)).wait_recv()
    total = others[0]
    for k in range(1, n):
        total = total + others[k]
    for side in range(2):
        total = jnp.where((row == 11) & (lane == side), sums[11][side], total)
    norms[...] = total
    for copy in first + second + third + copies:
        copy.wait_send()


def update_kernel(lr, fixes, gmain, gout, gvec, norms, w_in, m_in, v_in, conv_w, conv_m, conv_v,
                  temb_w, temb_m, temb_v, attn_w, attn_m, attn_v, out_w, out_m, out_v, vectors, vec_m, vec_v,
                  norms_new, in_new, in_first, in_second, conv_new, conv_first, conv_second, conv_low,
                  temb_new, temb_first, temb_second, temb_low, attn_new, attn_first, attn_second, attn_low,
                  out_new, out_first, out_second, vec_new, vec_first, vec_second, attn_grad):
    fix_one, fix_two = fixes[0], fixes[1]
    norms_new[...] = jnp.sqrt(norms[0:12, 0:2])

    def ratio(number):
        squares = norms[number:number + 1, 0:2]
        return RATE * jnp.sqrt(squares[:, 0:1] / (squares[:, 1:2] + 1e-06))

    arrays = {
        "conv": (conv_w, conv_m, conv_v, conv_new, conv_first, conv_second, conv_low),
        "temb": (temb_w, temb_m, temb_v, temb_new, temb_first, temb_second, temb_low),
        "attn": (attn_w, attn_m, attn_v, attn_new, attn_first, attn_second, attn_low),
    }
    for number, name, k, lanes, h, rows, held in matrix_parts(lr):
        w_ref, m_ref, v_ref, new_ref, first_ref, second_ref, low_ref = arrays[name]
        weight = w_ref[k, :, lanes]
        grad = gmain[h, rows, held]
        first, second, update = update_of(grad, m_ref[k, :, lanes], v_ref[k, :, lanes], weight, fix_one, fix_two)
        new = weight - ratio(number) * update
        first_ref[k, :, lanes] = first
        second_ref[k, :, lanes] = second
        new_ref[k, :, lanes] = new
        low_ref[k, :, lanes] = new.astype(BF16)
        if name == "attn":
            attn_grad[k, :, lanes] = grad
    weight = w_in[...]
    first, second, update = update_of(gvec[1, 0:lr, 0:27], m_in[...], v_in[...], weight, fix_one, fix_two)
    in_new[...] = weight - ratio(0) * update
    in_first[...] = first
    in_second[...] = second
    for h in range(2):
        lanes = slice(h * HALF, (h + 1) * HALF)
        weight = out_w[:, lanes]
        first, second, update = update_of(gout[h, 0:3, :], out_m[:, lanes], out_v[:, lanes], weight, fix_one, fix_two)
        out_new[:, lanes] = weight - ratio(11) * update
        out_first[:, lanes] = first
        out_second[:, lanes] = second
    first, second, direction = adapt(gvec[0, 0:VEC_ROWS, 0:lr], vec_m[...], vec_v[...], fix_one, fix_two)
    vec_new[...] = vectors[...] - RATE * direction
    vec_first[...] = first
    vec_second[...] = second


def vmem(count):
    return [pl.BlockSpec(memory_space=pltpu.VMEM)] * count


def smem(count):
    return [pl.BlockSpec(memory_space=pltpu.SMEM)] * count


def anywhere(count):
    return [pl.BlockSpec(memory_space=pl.ANY)] * count


def shape(dims, kind=F32):
    return jax.ShapeDtypeStruct(dims, kind)


def per_device(n, dp, canvas, crop_boxes, time_steps, noise_field, step_count, w_in, m_in, v_in,
               conv_w, conv_m, conv_v, temb_w, temb_m, temb_v, attn_w, attn_m, attn_v,
               out_w, out_m, out_v, vectors, vec_m, vec_v):
    images = canvas.shape[0]
    rows_all = images * PIX
    lr = conv_w.shape[1]
    nx = dp // 2
    ny = 1 << ((n.bit_length() - 2) // 2)
    nz = n // ny
    width = 128 * -(-(LANES // 128) // dp)

    steps = time_steps.astype(F32)
    phase = (steps / 1000.0 + 0.008) / 1.008
    alpha_bar = jnp.cos(phase * (math.pi / 2)) ** 2
    coefs = jnp.stack([jnp.sqrt(alpha_bar), jnp.sqrt(1.0 - alpha_bar)])
    frequency = jnp.exp(-math.log(10000.0) * jnp.arange(TEMB // 2, dtype=F32) / (TEMB // 2))
    angles = steps[:, None] * frequency[None, :]
    embedding = jnp.concatenate([jnp.sin(angles), jnp.cos(angles)], axis=1)
    temb_act = jnp.pad(jax.nn.silu(embedding), ((0, 16 - images), (0, 0))).astype(BF16)
    count_step = step_count[0].astype(F32)
    fixes = jnp.stack([1.0 / (1.0 - BETA_ONE ** count_step), 1.0 / (1.0 - BETA_TWO ** count_step)])

    shard, small, count, out_taps = pl.pallas_call(
        functools.partial(prep_kernel, lr, images),
        out_shape=(shape((4 * lr, dp * width), BF16), shape((16, 128)), shape((8, 128)), shape((72, C))),
        in_specs=smem(1) + vmem(7),
        out_specs=vmem(4),
        scratch_shapes=[pltpu.VMEM((32, 128), F32), pltpu.VMEM((128, 128), F32), pltpu.VMEM((16, HALF), F32)],
        compiler_params=pltpu.CompilerParams(vmem_limit_bytes=32 * MIB),
        name="prep",
    )(crop_boxes, conv_w, attn_w, w_in, temb_w, temb_act, vectors, out_w)

    dma = pltpu.SemaphoreType.DMA
    whole, smalls, counts = pl.pallas_call(
        functools.partial(gather_kernel, n, ny, nz, nx, dp, width),
        out_shape=(shape((n, 4 * lr, dp * width), BF16), shape((n, 16, 128)), shape((dp, 8, 128))),
        in_specs=anywhere(3),
        out_specs=anywhere(3),
        scratch_shapes=[
            dma((3,)), dma((n - 1,)), dma((n - 1,)),
            dma((max(nx - 1, 1), n - 1)), dma((max(nx - 1, 1), n - 1)), dma((nx, n - 1)), dma((nx, n - 1)),
            dma((n - 1,)), dma((n - 1,)), dma((dp - 1,)), dma((dp - 1,)),
        ],
        compiler_params=pltpu.CompilerParams(collective_id=1, has_side_effects=True),
        name="gather",
    )(shard, small, count)

    main, misc_out, misc_vec = pl.pallas_call(
        functools.partial(compute_kernel, n, lr, dp, images),
        out_shape=(shape((2, 4 * lr, MAIN), BF16), shape((2, 8, HALF)), shape((2, 32, 128))),
        in_specs=smem(2) + vmem(7),
        out_specs=vmem(3),
        scratch_shapes=[
            pltpu.VMEM((32, C), F32), pltpu.VMEM((32, C), F32), pltpu.VMEM((2, rows_all, C), F32),
            pltpu.VMEM((6, rows_all, C), F32), pltpu.VMEM((6, rows_all, C), F32),
            pltpu.VMEM((-(-6 * images // 8) * 8, C), F32),
            pltpu.VMEM((rows_all, KW), BF16), pltpu.VMEM((rows_all, KW), BF16),
            pltpu.VMEM((rows_all, KW), BF16), pltpu.VMEM((rows_all, KW), BF16),
            pltpu.VMEM((32, rows_all), BF16), pltpu.VMEM((32, rows_all), F32),
            pltpu.VMEM((2, rows_all, C), BF16),
            pltpu.VMEM((rows_all, C), BF16), pltpu.VMEM((rows_all, C), BF16), pltpu.VMEM((rows_all, C), BF16),
            pltpu.VMEM((images, PIX, PIX), F32), pltpu.VMEM((rows_all, C), BF16),
            pltpu.VMEM((32, C), F32), pltpu.VMEM((4 * lr, LANES + C), F32), pltpu.VMEM((16, C), F32),
        ],
        compiler_params=pltpu.CompilerParams(vmem_limit_bytes=56 * MIB),
        name="compute",
    )(crop_boxes, coefs, whole, smalls, counts, out_taps, temb_act, canvas, noise_field)

    state = (w_in, m_in, v_in, conv_w, conv_m, conv_v, temb_w, temb_m, temb_v, attn_w, attn_m, attn_v,
             out_w, out_m, out_v)
    half_main, half_out, half_vec = (4 * lr, MAIN), (8, HALF), (32, 128)
    gmain, gout, gvec, norms = pl.pallas_call(
        functools.partial(reduce_kernel, n, lr, dp, nx),
        out_shape=(shape((2,) + half_main), shape((2,) + half_out), shape((2,) + half_vec),
                   shape((SUM_ROWS, 128))),
        in_specs=smem(1) + vmem(3 + len(state)),
        out_specs=vmem(4),
        scratch_shapes=[
            pltpu.VMEM(half_main, BF16), pltpu.VMEM(half_out, F32), pltpu.VMEM(half_vec, F32),
            pltpu.VMEM((nx,) + half_main, BF16), pltpu.VMEM((nx,) + half_out, F32), pltpu.VMEM((nx,) + half_vec, F32),
            pltpu.VMEM((2,) + half_main, BF16), pltpu.VMEM((2,) + half_out, F32), pltpu.VMEM((2,) + half_vec, F32),
            pltpu.VMEM((SUM_ROWS, 128), F32), pltpu.VMEM((n, SUM_ROWS, 128), F32),
            dma((3,)), dma((3,)), dma((3, max(nx - 1, 1))), dma((3, max(nx - 1, 1))), dma((3,)), dma((3,)),
            dma((n - 1,)), dma((n - 1,)),
        ],
        compiler_params=pltpu.CompilerParams(
            collective_id=2, has_side_effects=True, vmem_limit_bytes=40 * MIB
        ),
        name="reduce",
    )(fixes, main, misc_out, misc_vec, *state)

    outs = [shape((12, 2))]
    for array, low in ((w_in, False), (conv_w, True), (temb_w, True), (attn_w, True), (out_w, False), (vectors, False)):
        outs += [shape(array.shape)] * 3
        if low:
            outs.append(shape(array.shape, BF16))
    outs.append(shape(attn_w.shape))
    updated = pl.pallas_call(
        functools.partial(update_kernel, lr),
        out_shape=tuple(outs),
        in_specs=smem(1) + vmem(4 + len(state) + 3),
        out_specs=vmem(len(outs)),
        compiler_params=pltpu.CompilerParams(vmem_limit_bytes=40 * MIB),
        name="update",
    )(fixes, gmain, gout, gvec, norms, *state, vectors, vec_m, vec_v)
    return (gvec[0, LOSS_ROW, 0],) + tuple(updated)


def solution(mesh):
    chan_row = P("chan", None)
    chan_mid = P(None, "chan", None)
    chan_vec = P(None, "chan")
    return jax.shard_map(
        functools.partial(per_device, mesh.shape["chan"], mesh.shape["dp"]),
        mesh=mesh,
        in_specs=(P("dp", None, None, None), P("dp", None), P("dp"), P(None, "dp", None), P())
        + (chan_row,) * 3 + (chan_mid,) * 9 + (P(),) * 3 + (chan_vec,) * 3,
        out_specs=(P(), P()) + (chan_row,) * 3 + (chan_mid,) * 12 + (P(),) * 3 + (chan_vec,) * 3 + (chan_mid,),
        check_vma=False,
    )
```

```python
import functools
import math

import jax
import jax.numpy as jnp
from jax import lax
from jax.experimental import pallas as pl
from jax.experimental.pallas import tpu as pltpu
from jax.sharding import PartitionSpec as P

TEMB = 512
HW = 16
PIX = HW * HW
GSIZE = 8
C = 256
TAPS = 9
KW = C * TAPS
HALF = 128 * TAPS
LANES = KW + C

NORM_EPS = 1e-05
BETA_ONE = 0.9
BETA_TWO = 0.95
ADAM_EPS = 1e-06
DECAY = 0.01
RATE = 0.3
F32 = jnp.float32
BF16 = jnp.bfloat16
HIGH = lax.Precision.HIGHEST
MESH = pl.DeviceIdType.MESH
NN = (((1,), (0,)), ((), ()))
NT = (((1,), (1,)), ((), ()))
TN = (((0,), (0,)), ((), ()))
MIB = 1024 * 1024

VEC_ROWS = 22
LOSS_ROW = 24
MAIN = HALF + 128 + 128
SUM_ROWS = 16


def dot(a, b, dims, precision=None):
    return lax.dot_general(a, b, dims, precision=precision, preferred_element_type=F32)


def iota(shape, axis):
    return lax.broadcasted_iota(jnp.int32, shape, axis)


def tap_order():
    wanted = (iota((1, HALF), 1) & 127) * TAPS + (iota((1, HALF), 1) >> 7)
    return jnp.where(iota((HALF, 1), 0) == wanted, 1.0, 0.0).astype(BF16)


def group_sum(row):
    lane = iota(row.shape, 1)
    step = 1
    while step < GSIZE:
        up = pltpu.roll(row, C - step, 1)
        down = pltpu.roll(row, step, 1)
        row = row + jnp.where((lane & step) == 0, up, down)
        step *= 2
    return row


def row_sum(value):
    return jnp.sum(value, axis=0, keepdims=True)


def group_mean(row):
    wide = jnp.broadcast_to(row, (8, C))
    return group_sum(wide)[0:1] * (1.0 / (GSIZE * PIX))


def compute(n, lr, dp, images, crop, coefs, whole, attn_all, smalls, counts, out_taps, temb_act,
                   canvas, noise, main, misc_out, misc_vec,
                   vec, w_in, hidden, xhat, dact, rstd, col0, col1, col2, col3, taps0, rows_scr, acts,
                   q_scr, k_scr, v_scr, probs, mixed_scr, gvec, gconv, gsum):
    cols = (col0, col1, col2, col3)
    d = lax.axis_index("chan")
    rows_all = images * PIX
    scale = C ** -0.5

    def span(b):
        return slice(b * PIX, (b + 1) * PIX)

    def conv_weight(k):
        return whole[:, k * lr:(k + 1) * lr, :].reshape(C, KW)

    def attn_weight(k):
        return attn_all[:, k * lr:(k + 1) * lr, :].reshape(C, C)

    vec[...] = jnp.zeros_like(vec)
    w_in[...] = jnp.zeros_like(w_in)
    lane_wide = iota((16, C), 1)
    for j in range(n):
        block = jnp.concatenate([smalls[j], jnp.zeros((16, 128), F32)], axis=1)
        for g in range(4):
            piece = jnp.where((lane_wide >= g * lr) & (lane_wide < (g + 1) * lr), block, 0.0)
            move = (j - g) * lr % C
            if move:
                piece = pltpu.roll(piece, move, 1)
            vec[g * 8:g * 8 + 8, :] += piece[0:8]
            w_in[g * 8:g * 8 + 8, :] += piece[8:16]

    def vrow(i):
        return vec[i:i + 1, :]

    total = counts[0, 0:1, 0:1]
    for k in range(1, dp):
        total = total + counts[k, 0:1, 0:1]

    lane = iota((1, PIX), 1)
    pix_x, pix_y = lane & (HW - 1), lane >> 4
    size = canvas.shape[2]
    noise_rows = []
    mask_rows = []
    noisy_rows = []
    for b in range(images):
        pick = jnp.where(iota((size, PIX), 0) == crop[b, 1] + pix_x, 1.0, 0.0)
        flat = canvas[b].reshape(3 * size, size)
        spread = dot(flat, pick, NN, HIGH).reshape(3, size, PIX)
        chosen = iota((size, PIX), 0) == crop[b, 0] + pix_y
        clean = jnp.sum(jnp.where(chosen[None], spread, 0.0), axis=1)
        noise_b = noise[:, b, :]
        noisy_rows.append(coefs[0, b] * clean + coefs[1, b] * noise_b)
        noise_rows.append(noise_b)
        side = crop[b, 2]
        mask_rows.append(jnp.where((pix_x < side) & (pix_y < side), 1.0, 0.0))
    zeros5 = jnp.zeros((5, rows_all), F32)
    noisy = jnp.concatenate([jnp.concatenate(noisy_rows, axis=1), zeros5], axis=0)
    noise_all = jnp.concatenate([jnp.concatenate(noise_rows, axis=1), zeros5], axis=0)
    mask_all = jnp.concatenate(mask_rows, axis=1)

    lane_all = iota((8, rows_all), 1)
    px, py = lane_all & (HW - 1), (lane_all >> 4) & (HW - 1)

    def tap_shift(field, tap):
        dy, dx = tap // 3 - 1, tap % 3 - 1
        move = -(dy * HW + dx) % rows_all
        out = pltpu.roll(field, move, 1) if move else field
        inside = (px + dx >= 0) & (px + dx < HW) & (py + dy >= 0) & (py + dy < HW)
        return jnp.where(inside, out, 0.0)

    noisy = noisy.astype(BF16).astype(F32)
    rows_scr[...] = jnp.zeros_like(rows_scr)
    for tap in range(TAPS):
        moved = tap_shift(noisy, tap)
        for colour in range(3):
            rows_scr[colour * TAPS + tap:colour * TAPS + tap + 1, :] = moved[colour:colour + 1]
    taps0[...] = rows_scr[...].astype(BF16)
    hidden[0] = dot(taps0[...], w_in[...].astype(BF16), TN) + vrow(12)

    col_x = iota((PIX, C), 0) & (HW - 1)

    def norm_fwd(i, value, gain, shift, store):
        for b in range(images):
            part = value[span(b)]
            centred = part - group_mean(row_sum(part))
            inv = lax.rsqrt(group_mean(row_sum(centred * centred)) + NORM_EPS)
            normed = centred * inv
            scaled = normed * gain + shift
            gate = 0.5 * jnp.tanh(0.5 * scaled) + 0.5
            act = scaled * gate
            xhat[i, span(b), :] = normed
            dact[i, span(b), :] = gate + act * (1.0 - gate)
            rstd[i * images + b:i * images + b + 1, :] = inv
            store(b, act)

    def norm_back(i, grad, gain_row):
        outs = []
        gain = vrow(gain_row)
        gain_sum = jnp.zeros((1, C), F32)
        shift_sum = jnp.zeros((1, C), F32)
        for b in range(images):
            slope = grad[span(b)] * dact[i, span(b), :]
            normed = xhat[i, span(b), :]
            shift_b = row_sum(slope)
            gain_b = row_sum(slope * normed)
            mean_one = group_mean(shift_b * gain)
            mean_two = group_mean(gain_b * gain)
            inv = rstd[i * images + b:i * images + b + 1, :]
            outs.append(inv * (slope * gain - mean_one - normed * mean_two))
            gain_sum += gain_b
            shift_sum += shift_b
        gvec[gain_row:gain_row + 1, :] = gain_sum
        gvec[6 + gain_row:7 + gain_row, :] = shift_sum
        return jnp.concatenate(outs, axis=0)

    blank = jnp.zeros((HW, C), BF16)

    def store_cols(ref, b, act):
        left = jnp.where(col_x > 0, pltpu.roll(act, 1, 0), 0.0)
        right = jnp.where(col_x < HW - 1, pltpu.roll(act, PIX - 1, 0), 0.0)
        for dx, moved in enumerate((left, act, right)):
            low = moved.astype(BF16)
            for dy in range(3):
                lanes = slice((3 * dy + dx) * C, (3 * dy + dx + 1) * C)
                base = b * PIX
                if dy == 0:
                    ref[base:base + HW, lanes] = blank
                    ref[base + HW:base + PIX, lanes] = low[:PIX - HW]
                elif dy == 1:
                    ref[base:base + PIX, lanes] = low
                else:
                    ref[base:base + PIX - HW, lanes] = low[HW:]
                    ref[base + PIX - HW:base + PIX, lanes] = blank

    def add_rows(value, first):
        return jnp.concatenate(
            [value[span(b)] + vrow(first + b) for b in range(images)], axis=0
        )

    def block_fwd(block, source, target):
        norm_fwd(3 * block, hidden[source], vrow(3 * block), vrow(6 + 3 * block),
                 functools.partial(store_cols, cols[2 * block]))
        middle = dot(cols[2 * block][...], conv_weight(2 * block), NT)
        middle = add_rows(middle, VEC_ROWS + block * images)
        norm_fwd(3 * block + 1, middle, vrow(3 * block + 1), vrow(7 + 3 * block),
                 functools.partial(store_cols, cols[2 * block + 1]))
        branch = dot(cols[2 * block + 1][...], conv_weight(2 * block + 1), NT)
        hidden[target] = hidden[source] + (branch + vrow(14 + 2 * block))

    def store_act(index):
        def store(b, act):
            acts[index, span(b), :] = act.astype(BF16)
        return store

    block_fwd(0, 0, 1)

    norm_fwd(2, hidden[1], vrow(2), vrow(8), store_act(0))
    q_scr[...] = (dot(acts[0], attn_weight(0), NT) + vrow(19)).astype(BF16)
    k_scr[...] = dot(acts[0], attn_weight(1), NT).astype(BF16)
    v_scr[...] = (dot(acts[0], attn_weight(2), NT) + vrow(20)).astype(BF16)
    for b in range(images):
        scores = dot(q_scr[span(b), :], k_scr[span(b), :], NT) * scale
        raised = jnp.exp(scores - jnp.max(scores, axis=1, keepdims=True))
        soft = raised / jnp.sum(raised, axis=1, keepdims=True)
        probs[b] = soft
        mixed_scr[span(b), :] = dot(soft.astype(BF16), v_scr[span(b), :], NN).astype(BF16)
    hidden[0] = hidden[1] + (dot(mixed_scr[...], attn_weight(3), NT) + vrow(21))

    block_fwd(1, 0, 1)
    norm_fwd(5, hidden[1], vrow(5), vrow(11), store_act(1))

    out_low = out_taps[...].astype(BF16)
    fanned = dot(out_low, acts[1], NT)
    pred = jnp.zeros((8, rows_all), F32)
    for tap in range(TAPS):
        pred += tap_shift(fanned[tap * 8:tap * 8 + 8], tap)
    error = pred - noise_all
    masked = mask_all * error
    inverse = 1.0 / total
    loss = jnp.sum(jnp.sum(masked * error, axis=1, keepdims=True), axis=0, keepdims=True) * inverse
    grad_pred = (2.0 * masked * inverse).astype(BF16).astype(F32)
    spread_pred = jnp.concatenate(
        [tap_shift(grad_pred, TAPS - 1 - tap) for tap in range(TAPS)], axis=0
    ).astype(BF16)
    out_grad = dot(spread_pred, acts[1], NN)
    grad = dot(spread_pred, out_low, TN)

    gvec[...] = jnp.zeros_like(gvec)
    pick_own = jnp.where(
        iota((lr, C), 1) == iota((lr, C), 0) + d * lr, 1.0, 0.0
    ).astype(BF16)

    def own_rows(low):
        return dot(pick_own, low, NT).astype(BF16)

    def conv_back(k, low):
        gconv[k * lr:(k + 1) * lr, 0:KW] = dot(own_rows(low), cols[k][...], NN)
        parts = dot(low, conv_weight(k), NN)
        outs = []
        hole = jnp.zeros((HW, C), F32)
        for b in range(images):
            sides = []
            for dx in range(3):
                up = parts[span(b), dx * C:(dx + 1) * C]
                mid = parts[span(b), (3 + dx) * C:(4 + dx) * C]
                down = parts[span(b), (6 + dx) * C:(7 + dx) * C]
                sides.append(
                    mid
                    + jnp.concatenate([up[HW:], hole], axis=0)
                    + jnp.concatenate([hole, down[:PIX - HW]], axis=0)
                )
            left = pltpu.roll(jnp.where(col_x > 0, sides[0], 0.0), PIX - 1, 0)
            right = pltpu.roll(jnp.where(col_x < HW - 1, sides[2], 0.0), 1, 0)
            outs.append(sides[1] + left + right)
        return jnp.concatenate(outs, axis=0)

    def block_back(block, grad):
        gvec[14 + 2 * block:15 + 2 * block, :] = row_sum(grad)
        back = conv_back(2 * block + 1, grad.astype(BF16))
        middle = norm_back(3 * block + 1, back, 3 * block + 1)
        gsum[...] = jnp.zeros_like(gsum)
        for b in range(images):
            gsum[b:b + 1, :] = row_sum(middle[span(b)])
        whole_sum = row_sum(gsum[...])
        gvec[13 + 2 * block:14 + 2 * block, :] = whole_sum
        gvec[17 + block:18 + block, :] = whole_sum
        own = dot(pick_own, gsum[...].astype(BF16), NT).astype(BF16)
        temb = dot(own, temb_act[...], NN)
        for j in range(4):
            top = (j % 2) * 2 * lr + block * lr
            gconv[top:top + lr, LANES + (j // 2) * 128:LANES + (j // 2) * 128 + 128] = (
                temb[:, j * 128:(j + 1) * 128]
            )
        back = conv_back(2 * block, middle.astype(BF16))
        return grad + norm_back(3 * block, back, 3 * block)

    grad = norm_back(5, grad, 5)
    grad = block_back(1, grad)

    gvec[21:22, :] = row_sum(grad)
    low = grad.astype(BF16)
    gconv[3 * lr:4 * lr, KW:LANES] = dot(own_rows(low), mixed_scr[...], NN)
    mixed_low = dot(low, attn_weight(3), NN).astype(BF16)
    grads_q, grads_k, grads_v = [], [], []
    for b in range(images):
        part = mixed_low[span(b)]
        soft = probs[b]
        grad_soft = dot(part, v_scr[span(b), :], NT)
        grads_v.append(dot(soft.astype(BF16), part, TN))
        weighed = soft * grad_soft
        slope = (weighed - soft * jnp.sum(weighed, axis=1, keepdims=True)).astype(BF16)
        grads_q.append(scale * dot(slope, k_scr[span(b), :], NN))
        grads_k.append(scale * dot(slope, q_scr[span(b), :], TN))
    back = jnp.zeros((rows_all, C), F32)
    for i, grads in enumerate((grads_q, grads_k, grads_v)):
        full = jnp.concatenate(grads, axis=0)
        if i != 1:
            gvec[19 + i // 2:20 + i // 2, :] = row_sum(full)
        low = full.astype(BF16)
        gconv[i * lr:(i + 1) * lr, KW:LANES] = dot(own_rows(low), acts[0], NN)
        back += dot(low, attn_weight(i), NN)
    grad = grad + norm_back(2, back, 2)

    grad = block_back(0, grad)
    gvec[12:13, :] = row_sum(grad)
    in_grad = dot(own_rows(grad.astype(BF16)), taps0[...], NT)

    order = tap_order()
    shaped = []
    for h in range(2):
        shaped.append(jnp.concatenate(
            [gconv[:, tap * C + h * 128:tap * C + h * 128 + 128] for tap in range(TAPS)], axis=1
        ).astype(BF16))
    for h in range(2):
        shaped.append(jnp.concatenate(
            [
                jnp.concatenate(
                    [out_grad[tap * 8:tap * 8 + 8, h * 128:(h + 1) * 128] for tap in range(TAPS)], axis=1
                ),
                jnp.zeros((8, HALF), F32),
            ], axis=0,
        ).astype(BF16))
    natural = dot(jnp.concatenate(shaped, axis=0), order, NT)
    for h in range(2):
        main[h, :, 0:HALF] = natural[h * 4 * lr:(h + 1) * 4 * lr].astype(BF16)
        main[h, :, HALF:HALF + 128] = gconv[:, KW + h * 128:KW + h * 128 + 128].astype(BF16)
        main[h, :, HALF + 128:MAIN] = gconv[:, LANES + h * 128:LANES + h * 128 + 128].astype(BF16)
        misc_out[h] = natural[8 * lr + h * 16:8 * lr + h * 16 + 8]
    own_vec = pltpu.roll(gvec[...], lax.rem(C - d * lr, C), 1)
    misc_vec[0] = own_vec[:, 0:128]
    misc_vec[0, LOSS_ROW:LOSS_ROW + 1, :] = jnp.broadcast_to(loss, (1, 128))
    misc_vec[1] = jnp.zeros((32, 128), F32)
    misc_vec[1, 0:lr, 0:32] = in_grad


def flip(value, mask):
    bit = 1
    while bit <= mask:
        if mask & bit:
            value = value + bit * (1 - 2 * ((value // bit) % 2))
        bit *= 2
    return value


def remote(src, dst, send_sem, recv_sem, target):
    return pltpu.make_async_remote_copy(
        src_ref=src, dst_ref=dst, send_sem=send_sem, recv_sem=recv_sem,
        device_id=target, device_id_type=MESH,
    )


def step_kernel(n, ny, nz, nx, dp, lr, images, crop, coefs, conv_hbm, attn_hbm, temb_hbm, in_hbm, out_hbm,
                vec_hbm, temb_act, canvas, noise, main, misc_out, misc_vec,
                conv_w, attn_w, temb_w, w_in_own, out_w, vectors,
                whole, attn_all, smalls, counts, load_sem,
                near_send, near_recv, x_send, x_recv, core_send, core_recv,
                small_send, small_recv, count_send, count_recv,
                own_rows_scr, in_scr, out_scr, out_taps, *rest):
    me = lax.axis_index("chan")
    part = lax.axis_index("dp")
    z, y = me // ny, me % ny
    x, core = part // 2, part % 2
    sibling = (x * 2 + 1 - core, me)

    loads = [
        pltpu.make_async_copy(conv_hbm.at[k], conv_w.at[k], load_sem.at[k]) for k in range(4)
    ] + [
        pltpu.make_async_copy(src, dst, load_sem.at[4 + i])
        for i, (src, dst) in enumerate(
            ((attn_hbm, attn_w), (temb_hbm, temb_w), (in_hbm, w_in_own), (out_hbm, out_w), (vec_hbm, vectors))
        )
    ]
    for load in loads:
        load.start()

    offsets = [(i, j) for i in range(nz) for j in range(ny)][1:]
    place = {o: i for i, o in enumerate(offsets)}

    def chan_at(o):
        return flip(z, o[0]) * ny + flip(y, o[1])

    barrier = pltpu.get_barrier_semaphore()
    for o in offsets:
        pl.semaphore_signal(barrier, inc=1, device_id=(part, chan_at(o)), device_id_type=MESH)
    for k in range(1, dp):
        pl.semaphore_signal(barrier, inc=1, device_id=(lax.rem(part + k, dp), me), device_id_type=MESH)

    core_lanes = KW // 2
    x_lanes = 3 * 128 if nx == 2 else 0
    near_lanes = core_lanes - x_lanes
    chunk_rows = max(lr, 16)
    conv_chunks = 4 * lr // chunk_rows
    chunks = list(range(conv_chunks)) + [None]

    def rows_of(chunk):
        return pl.ds(chunk * chunk_rows, chunk_rows)

    def near_ref(chunk, src, c):
        if chunk is None:
            return attn_all.at[src, pl.ds(pl.multiple_of(c * 2 * lr, 16), 2 * lr), :]
        start = c * core_lanes + x * x_lanes if x_lanes else c * core_lanes
        return whole.at[src, rows_of(chunk), pl.ds(pl.multiple_of(start, 128), near_lanes)]

    def x_ref(chunk, src, c, side):
        start = c * core_lanes + side * near_lanes
        return whole.at[src, rows_of(chunk), pl.ds(pl.multiple_of(start, 128), x_lanes)]

    sends = []

    def send(*args):
        copy = remote(*args)
        copy.start()
        sends.append(copy)

    def index(chunk):
        return conv_chunks if chunk is None else chunk

    def send_near(chunk, src, o, target):
        i = index(chunk)
        ref = near_ref(chunk, src, core)
        send(ref, ref, near_send.at[i, place[o]], near_recv.at[i, place[o]], target)

    def send_core(chunk, src, o, piece):
        i = index(chunk)
        ref = near_ref(chunk, src, core) if piece == 0 else x_ref(chunk, src, core, 1 - x)
        send(ref, ref, core_send.at[piece, i, place[o]], core_recv.at[piece, i, place[o]], sibling)

    def begin(chunk):
        for i in range(1, nz):
            send_near(chunk, me, (i, 0), (part, chan_at((i, 0))))
        for j in range(1, ny):
            send_near(chunk, me, (0, j), (part, chan_at((0, j))))

    def near_in(chunk, o):
        i = index(chunk)
        src = chan_at(o)
        ref = near_ref(chunk, src, core)
        remote(ref, ref, near_send.at[i, place[o]], near_recv.at[i, place[o]], (part, src)).wait_recv()
        if o[1] == 0:
            for j in range(1, ny):
                send_near(chunk, src, (o[0], j), (part, chan_at((0, j))))
        if x_lanes and chunk is not None:
            ref = x_ref(chunk, src, core, x)
            send(ref, ref, x_send.at[i, place[o]], x_recv.at[i, place[o]], ((1 - x) * 2 + core, me))
        send_core(chunk, src, o, 0)

    def x_in(chunk, o):
        if x_lanes and chunk is not None:
            i = index(chunk)
            src = chan_at(o)
            ref = x_ref(chunk, src, core, 1 - x)
            remote(ref, ref, x_send.at[i, place[o]], x_recv.at[i, place[o]], ((1 - x) * 2 + core, me)).wait_recv()
            send_core(chunk, src, o, 1)

    def core_in(chunk, o):
        i = index(chunk)
        src = chan_at(o)
        pieces = [near_ref(chunk, src, 1 - core)]
        if x_lanes and chunk is not None:
            pieces.append(x_ref(chunk, src, 1 - core, 1 - x))
        for piece, ref in enumerate(pieces):
            remote(ref, ref, core_send.at[piece, i, place[o]], core_recv.at[piece, i, place[o]], sibling).wait_recv()

    def stage_one(chunk):
        for i in range(1, nz):
            near_in(chunk, (i, 0))

    def stage_two(chunk):
        for j in range(1, ny):
            near_in(chunk, (0, j))
        for i in range(1, nz):
            for j in range(1, ny):
                near_in(chunk, (i, j))

    def stage_three(chunk):
        for o in offsets:
            x_in(chunk, o)

    def stage_four(chunk):
        for o in offsets:
            core_in(chunk, o)

    order = tap_order()
    pl.semaphore_wait(barrier, n + dp - 2)
    begun = 0
    for k in range(4):
        loads[k].wait()
        weight = conv_w[k].astype(BF16)
        both = jnp.concatenate([weight[:, :HALF], weight[:, HALF:]], axis=0)
        mixed = dot(both, order, NN).astype(BF16)
        for tap in range(TAPS):
            for h in range(2):
                lanes = slice(tap * C + h * 128, tap * C + h * 128 + 128)
                whole[me, k * lr:(k + 1) * lr, lanes] = mixed[h * lr:(h + 1) * lr, tap * 128:(tap + 1) * 128]
        if (k + 1) * lr >= (begun + 1) * chunk_rows:
            if begun < 2:
                begin(begun)
            begun += 1
        if k == 0:
            for load in loads[5:]:
                load.wait()
            own_rows_scr[...] = jnp.zeros_like(own_rows_scr)
            own_rows_scr[0:VEC_ROWS, 0:lr] = vectors[...]
            for block in range(2):
                shift = dot(temb_act[...], temb_w[block].astype(BF16), NT)
                for b in range(images):
                    row = VEC_ROWS + block * images + b
                    own_rows_scr[row:row + 1, 0:lr] = (
                        shift[b:b + 1, :] + vectors[17 + block:18 + block, :]
                    ) + vectors[13 + 2 * block:14 + 2 * block, :]
            in_scr[...] = jnp.zeros_like(in_scr)
            in_scr[0:lr, 0:27] = w_in_own[...]
            turned = in_scr[...].T
            packed = [jnp.zeros((8, 128), F32), jnp.zeros((8, 128), F32)]
            for g in range(4):
                for i, rows in enumerate((own_rows_scr[g * 8:g * 8 + 8, :], turned[g * 8:g * 8 + 8, :])):
                    packed[i] += rows if g == 0 else pltpu.roll(rows, g * lr, 1)
            smalls[me, 0:8, :] = packed[0]
            smalls[me, 8:16, :] = packed[1]
            total = jnp.int32(0)
            for b in range(images):
                side = jnp.minimum(jnp.maximum(crop[b, 2], 0), HW)
                total += 3 * side * side
            counts[part] = jnp.full((8, 128), total, jnp.int32).astype(F32)
            for o in offsets:
                i = place[o]
                send(smalls.at[me], smalls.at[me], small_send.at[i], small_recv.at[i], (part, chan_at(o)))
            for i in range(1, dp):
                send(counts.at[part], counts.at[part], count_send.at[i - 1], count_recv.at[i - 1],
                     (lax.rem(part + i, dp), me))
    loads[4].wait()
    for k in range(4):
        attn_all[me, k * lr:(k + 1) * lr, :] = attn_w[k].astype(BF16)

    out_scr[...] = jnp.zeros_like(out_scr)
    for h in range(2):
        out_scr[h * 8:h * 8 + 3, :] = out_w[:, h * HALF:(h + 1) * HALF]
    out_mixed = dot(out_scr[...].astype(BF16), order, NN)
    for tap in range(TAPS):
        for h in range(2):
            out_taps[tap * 8:tap * 8 + 8, h * 128:(h + 1) * 128] = out_mixed[
                h * 8:h * 8 + 8, tap * 128:(tap + 1) * 128
            ]

    for i in range(len(chunks) + 3):
        for stage, delay in ((stage_one, 0), (stage_two, 1), (stage_three, 2), (stage_four, 3)):
            if 0 <= i - delay < len(chunks):
                stage(chunks[i - delay])
            if delay == 0 and 2 <= i + 2 < len(chunks):
                begin(chunks[i + 2])
    for o in offsets:
        src = chan_at(o)
        remote(smalls.at[src], smalls.at[src], small_send.at[place[o]], small_recv.at[place[o]],
               (part, src)).wait_recv()
    for i in range(1, dp):
        p = lax.rem(part - i + dp, dp)
        remote(counts.at[p], counts.at[p], count_send.at[i - 1], count_recv.at[i - 1], (p, me)).wait_recv()
    for copy in sends:
        copy.wait_send()

    compute(n, lr, dp, images, crop, coefs, whole, attn_all, smalls, counts, out_taps, temb_act,
            canvas, noise, main, misc_out, misc_vec, *rest)


def adapt(grad, first, second, fix_one, fix_two):
    first_new = BETA_ONE * first + (1.0 - BETA_ONE) * grad
    second_new = BETA_TWO * second + (1.0 - BETA_TWO) * grad * grad
    direction = first_new * fix_one / (jnp.sqrt(second_new * fix_two) + ADAM_EPS)
    return first_new, second_new, direction


def update_of(grad, first, second, weight, fix_one, fix_two):
    first_new, second_new, direction = adapt(grad, first, second, fix_one, fix_two)
    return first_new, second_new, direction + DECAY * weight


def matrix_parts(lr):
    parts = []
    for k in range(4):
        for h in range(2):
            parts.append((1 + k, "conv", k, slice(h * HALF, (h + 1) * HALF), h,
                          slice(k * lr, (k + 1) * lr), slice(0, HALF)))
    for k in range(2):
        for j in range(4):
            top = (j % 2) * 2 * lr + k * lr
            parts.append((5 + k, "temb", k, slice(j * 128, (j + 1) * 128), j // 2,
                          slice(top, top + lr), slice(HALF + 128, MAIN)))
    for k in range(4):
        for h in range(2):
            parts.append((7 + k, "attn", k, slice(h * 128, (h + 1) * 128), h,
                          slice(k * lr, (k + 1) * lr), slice(HALF, HALF + 128)))
    return parts


def reduce_kernel(n, lr, dp, nx, fixes, main, misc_out, misc_vec, *refs):
    state_hbm, refs = refs[:15], refs[15:]
    (gmain, gout, gvec, norms), refs = refs[:4], refs[4:]
    state, refs = refs[:15], refs[15:]
    loads = [
        pltpu.make_async_copy(src, dst, refs[-1].at[i]) for i, (src, dst) in enumerate(zip(state_hbm, state))
    ]
    for load in loads:
        load.start()
    reduce_body(n, lr, dp, nx, loads, fixes, main, misc_out, misc_vec, *state, gmain, gout, gvec, norms, *refs[:-1])


def reduce_body(n, lr, dp, nx, loads, fixes, main, misc_out, misc_vec, w_in, m_in, v_in, conv_w, conv_m, conv_v,
                  temb_w, temb_m, temb_v, attn_w, attn_m, attn_v, out_w, out_m, out_v,
                  gmain, gout, gvec, norms,
                  one_main, one_out, one_vec, two_main, two_out, two_vec, last_main, last_out, last_vec,
                  mine, others, send_one, recv_one, send_two, recv_two, send_three, recv_three,
                  sum_send, sum_recv):
    me = lax.axis_index("chan")
    part = lax.axis_index("dp")
    x, core = part // 2, part % 2
    sibling = (x * 2 + 1 - core, me)

    barrier = pltpu.get_barrier_semaphore()
    for k in range(1, n):
        pl.semaphore_signal(barrier, inc=1, device_id=(part, lax.rem(me + k, n)), device_id_type=MESH)
    for m in range(1, nx):
        pl.semaphore_signal(barrier, inc=1, device_id=(lax.rem(x + m, nx) * 2 + core, me), device_id_type=MESH)
    pl.semaphore_signal(barrier, inc=1, device_id=sibling, device_id_type=MESH)
    pl.semaphore_wait(barrier, n + nx - 1)

    trio = ((main, one_main, two_main, last_main), (misc_out, one_out, two_out, last_out),
            (misc_vec, one_vec, two_vec, last_vec))
    first = []
    for i, (source, landed, slots, last) in enumerate(trio):
        copy = remote(source.at[1 - core], landed, send_one.at[i], recv_one.at[i], sibling)
        copy.start()
        first.append(copy)
    second = []
    for i, (source, landed, slots, last) in enumerate(trio):
        first[i].wait_recv()
        slots[x] = (source[core].astype(F32) + landed[...].astype(F32)).astype(slots.dtype)
        for m in range(1, nx):
            copy = remote(slots.at[x], slots.at[x], send_two.at[i, m - 1], recv_two.at[i, m - 1],
                          (lax.rem(x + m, nx) * 2 + core, me))
            copy.start()
            second.append(copy)
    third = []
    for i, (source, landed, slots, last) in enumerate(trio):
        for m in range(1, nx):
            sender = lax.rem(x - m + nx, nx)
            remote(slots.at[sender], slots.at[sender], send_two.at[i, m - 1], recv_two.at[i, m - 1],
                   (sender * 2 + core, me)).wait_recv()
        summed = slots[0].astype(F32)
        for m in range(1, nx):
            summed = summed + slots[m].astype(F32)
        last[core] = summed.astype(last.dtype)
        copy = remote(last.at[core], last.at[core], send_three.at[i], recv_three.at[i], sibling)
        copy.start()
        third.append(copy)
    for i, (source, landed, slots, last) in enumerate(trio):
        remote(last.at[1 - core], last.at[1 - core], send_three.at[i], recv_three.at[i], sibling).wait_recv()
    gmain[...] = last_main[...].astype(F32)
    gout[...] = last_out[...]
    gvec[...] = last_vec[...]

    for load in loads:
        load.wait()
    fix_one, fix_two = fixes[0], fixes[1]
    arrays = {"conv": (conv_w, conv_m, conv_v), "temb": (temb_w, temb_m, temb_v), "attn": (attn_w, attn_m, attn_v)}

    def squares(value):
        return jnp.sum(jnp.sum(value * value, axis=1, keepdims=True), axis=0, keepdims=True)

    sums = {}

    def note(number, weight, update):
        pair = (squares(weight), squares(update))
        if number in sums:
            pair = (sums[number][0] + pair[0], sums[number][1] + pair[1])
        sums[number] = pair

    for number, name, k, lanes, h, rows, held in matrix_parts(lr):
        w_ref, m_ref, v_ref = arrays[name]
        weight = w_ref[k, :, lanes]
        update = update_of(gmain[h, rows, held], m_ref[k, :, lanes], v_ref[k, :, lanes], weight, fix_one, fix_two)[2]
        note(number, weight, update)
    weight = w_in[...]
    note(0, weight, update_of(gvec[1, 0:lr, 0:27], m_in[...], v_in[...], weight, fix_one, fix_two)[2])
    for h in range(2):
        lanes = slice(h * HALF, (h + 1) * HALF)
        weight = out_w[:, lanes]
        note(11, weight, update_of(gout[h, 0:3, :], out_m[:, lanes], out_v[:, lanes], weight, fix_one, fix_two)[2])

    row = iota((SUM_ROWS, 128), 0)
    lane = iota((SUM_ROWS, 128), 1)
    table = jnp.zeros((SUM_ROWS, 128), F32)
    for number in range(11):
        for side in range(2):
            table = jnp.where((row == number) & (lane == side), sums[number][side], table)
    mine[...] = table
    copies = []
    for k in range(1, n):
        copy = remote(mine, others.at[me], sum_send.at[k - 1], sum_recv.at[k - 1], (part, lax.rem(me + k, n)))
        copy.start()
        copies.append(copy)
    others[me] = table
    for k in range(1, n):
        src = lax.rem(me - k + n, n)
        remote(mine, others.at[src], sum_send.at[k - 1], sum_recv.at[k - 1], (part, src)).wait_recv()
    total = others[0]
    for k in range(1, n):
        total = total + others[k]
    for side in range(2):
        total = jnp.where((row == 11) & (lane == side), sums[11][side], total)
    norms[...] = total
    for copy in first + second + third + copies:
        copy.wait_send()


def update_kernel(lr, fixes, gmain, gout, gvec, norms, w_in, m_in, v_in, conv_w, conv_m, conv_v,
                  temb_w, temb_m, temb_v, attn_w, attn_m, attn_v, out_w, out_m, out_v, vectors, vec_m, vec_v,
                  norms_new, in_new, in_first, in_second, conv_new, conv_first, conv_second, conv_low,
                  temb_new, temb_first, temb_second, temb_low, attn_new, attn_first, attn_second, attn_low,
                  out_new, out_first, out_second, vec_new, vec_first, vec_second, attn_grad):
    fix_one, fix_two = fixes[0], fixes[1]
    norms_new[...] = jnp.sqrt(norms[0:12, 0:2])

    def ratio(number):
        squares = norms[number:number + 1, 0:2]
        return RATE * jnp.sqrt(squares[:, 0:1] / (squares[:, 1:2] + 1e-06))

    arrays = {
        "conv": (conv_w, conv_m, conv_v, conv_new, conv_first, conv_second, conv_low),
        "temb": (temb_w, temb_m, temb_v, temb_new, temb_first, temb_second, temb_low),
        "attn": (attn_w, attn_m, attn_v, attn_new, attn_first, attn_second, attn_low),
    }
    for number, name, k, lanes, h, rows, held in matrix_parts(lr):
        w_ref, m_ref, v_ref, new_ref, first_ref, second_ref, low_ref = arrays[name]
        weight = w_ref[k, :, lanes]
        grad = gmain[h, rows, held]
        first, second, update = update_of(grad, m_ref[k, :, lanes], v_ref[k, :, lanes], weight, fix_one, fix_two)
        new = weight - ratio(number) * update
        first_ref[k, :, lanes] = first
        second_ref[k, :, lanes] = second
        new_ref[k, :, lanes] = new
        low_ref[k, :, lanes] = new.astype(BF16)
        if name == "attn":
            attn_grad[k, :, lanes] = grad
    weight = w_in[...]
    first, second, update = update_of(gvec[1, 0:lr, 0:27], m_in[...], v_in[...], weight, fix_one, fix_two)
    in_new[...] = weight - ratio(0) * update
    in_first[...] = first
    in_second[...] = second
    for h in range(2):
        lanes = slice(h * HALF, (h + 1) * HALF)
        weight = out_w[:, lanes]
        first, second, update = update_of(gout[h, 0:3, :], out_m[:, lanes], out_v[:, lanes], weight, fix_one, fix_two)
        out_new[:, lanes] = weight - ratio(11) * update
        out_first[:, lanes] = first
        out_second[:, lanes] = second
    first, second, direction = adapt(gvec[0, 0:VEC_ROWS, 0:lr], vec_m[...], vec_v[...], fix_one, fix_two)
    vec_new[...] = vectors[...] - RATE * direction
    vec_first[...] = first
    vec_second[...] = second


def vmem(count):
    return [pl.BlockSpec(memory_space=pltpu.VMEM)] * count


def smem(count):
    return [pl.BlockSpec(memory_space=pltpu.SMEM)] * count


def hbm(count):
    return [pl.BlockSpec(memory_space=pltpu.HBM)] * count


def shape(dims, kind=F32):
    return jax.ShapeDtypeStruct(dims, kind)


def per_device(n, dp, canvas, crop_boxes, time_steps, noise_field, step_count, w_in, m_in, v_in,
               conv_w, conv_m, conv_v, temb_w, temb_m, temb_v, attn_w, attn_m, attn_v,
               out_w, out_m, out_v, vectors, vec_m, vec_v):
    images = canvas.shape[0]
    rows_all = images * PIX
    lr = conv_w.shape[1]
    nx = dp // 2
    ny = 1 << ((n.bit_length() - 2) // 2)
    nz = n // ny

    steps = time_steps.astype(F32)
    phase = (steps / 1000.0 + 0.008) / 1.008
    alpha_bar = jnp.cos(phase * (math.pi / 2)) ** 2
    coefs = jnp.stack([jnp.sqrt(alpha_bar), jnp.sqrt(1.0 - alpha_bar)])
    frequency = jnp.exp(-math.log(10000.0) * jnp.arange(TEMB // 2, dtype=F32) / (TEMB // 2))
    angles = steps[:, None] * frequency[None, :]
    embedding = jnp.concatenate([jnp.sin(angles), jnp.cos(angles)], axis=1)
    temb_act = jnp.pad(jax.nn.silu(embedding), ((0, 16 - images), (0, 0))).astype(BF16)
    count_step = step_count[0].astype(F32)
    fixes = jnp.stack([1.0 / (1.0 - BETA_ONE ** count_step), 1.0 / (1.0 - BETA_TWO ** count_step)])

    dma = pltpu.SemaphoreType.DMA
    chunks = 4 * lr // max(lr, 16) + 1
    main, misc_out, misc_vec = pl.pallas_call(
        functools.partial(step_kernel, n, ny, nz, nx, dp, lr, images),
        out_shape=(shape((2, 4 * lr, MAIN), BF16), shape((2, 8, HALF)), shape((2, 32, 128))),
        in_specs=smem(2) + hbm(6) + vmem(3),
        out_specs=vmem(3),
        scratch_shapes=[
            pltpu.VMEM(conv_w.shape, F32), pltpu.VMEM(attn_w.shape, F32), pltpu.VMEM(temb_w.shape, F32),
            pltpu.VMEM(w_in.shape, F32), pltpu.VMEM(out_w.shape, F32), pltpu.VMEM(vectors.shape, F32),
            pltpu.VMEM((n, 4 * lr, KW), BF16), pltpu.VMEM((n, 4 * lr, C), BF16),
            pltpu.VMEM((n, 16, 128), F32), pltpu.VMEM((dp, 8, 128), F32), dma((9,)),
            dma((chunks, n - 1)), dma((chunks, n - 1)), dma((chunks, n - 1)), dma((chunks, n - 1)),
            dma((2, chunks, n - 1)), dma((2, chunks, n - 1)),
            dma((n - 1,)), dma((n - 1,)), dma((dp - 1,)), dma((dp - 1,)),
            pltpu.VMEM((32, 128), F32), pltpu.VMEM((128, 128), F32), pltpu.VMEM((16, HALF), F32),
            pltpu.VMEM((72, C), F32),
            pltpu.VMEM((32, C), F32), pltpu.VMEM((32, C), F32), pltpu.VMEM((2, rows_all, C), F32),
            pltpu.VMEM((6, rows_all, C), F32), pltpu.VMEM((6, rows_all, C), F32),
            pltpu.VMEM((-(-6 * images // 8) * 8, C), F32),
            pltpu.VMEM((rows_all, KW), BF16), pltpu.VMEM((rows_all, KW), BF16),
            pltpu.VMEM((rows_all, KW), BF16), pltpu.VMEM((rows_all, KW), BF16),
            pltpu.VMEM((32, rows_all), BF16), pltpu.VMEM((32, rows_all), F32),
            pltpu.VMEM((2, rows_all, C), BF16),
            pltpu.VMEM((rows_all, C), BF16), pltpu.VMEM((rows_all, C), BF16), pltpu.VMEM((rows_all, C), BF16),
            pltpu.VMEM((images, PIX, PIX), F32), pltpu.VMEM((rows_all, C), BF16),
            pltpu.VMEM((32, C), F32), pltpu.VMEM((4 * lr, LANES + C), F32), pltpu.VMEM((16, C), F32),
        ],
        compiler_params=pltpu.CompilerParams(
            collective_id=1, has_side_effects=True, vmem_limit_bytes=56 * MIB
        ),
        name="step",
    )(crop_boxes, coefs, conv_w, attn_w, temb_w, w_in, out_w, vectors, temb_act, canvas, noise_field)

    state = (w_in, m_in, v_in, conv_w, conv_m, conv_v, temb_w, temb_m, temb_v, attn_w, attn_m, attn_v,
             out_w, out_m, out_v)
    half_main, half_out, half_vec = (4 * lr, MAIN), (8, HALF), (32, 128)
    gmain, gout, gvec, norms = pl.pallas_call(
        functools.partial(reduce_kernel, n, lr, dp, nx),
        out_shape=(shape((2,) + half_main), shape((2,) + half_out), shape((2,) + half_vec),
                   shape((SUM_ROWS, 128))),
        in_specs=smem(1) + vmem(3) + hbm(len(state)),
        out_specs=vmem(4),
        scratch_shapes=[pltpu.VMEM(array.shape, F32) for array in state] + [
            pltpu.VMEM(half_main, BF16), pltpu.VMEM(half_out, F32), pltpu.VMEM(half_vec, F32),
            pltpu.VMEM((nx,) + half_main, BF16), pltpu.VMEM((nx,) + half_out, F32), pltpu.VMEM((nx,) + half_vec, F32),
            pltpu.VMEM((2,) + half_main, BF16), pltpu.VMEM((2,) + half_out, F32), pltpu.VMEM((2,) + half_vec, F32),
            pltpu.VMEM((SUM_ROWS, 128), F32), pltpu.VMEM((n, SUM_ROWS, 128), F32),
            dma((3,)), dma((3,)), dma((3, max(nx - 1, 1))), dma((3, max(nx - 1, 1))), dma((3,)), dma((3,)),
            dma((n - 1,)), dma((n - 1,)), dma((len(state),)),
        ],
        compiler_params=pltpu.CompilerParams(
            collective_id=2, has_side_effects=True, vmem_limit_bytes=40 * MIB
        ),
        name="reduce",
    )(fixes, main, misc_out, misc_vec, *state)

    outs = [shape((12, 2))]
    for array, low in ((w_in, False), (conv_w, True), (temb_w, True), (attn_w, True), (out_w, False), (vectors, False)):
        outs += [shape(array.shape)] * 3
        if low:
            outs.append(shape(array.shape, BF16))
    outs.append(shape(attn_w.shape))
    updated = pl.pallas_call(
        functools.partial(update_kernel, lr),
        out_shape=tuple(outs),
        in_specs=smem(1) + vmem(4 + len(state) + 3),
        out_specs=vmem(len(outs)),
        compiler_params=pltpu.CompilerParams(vmem_limit_bytes=40 * MIB),
        name="update",
    )(fixes, gmain, gout, gvec, norms, *state, vectors, vec_m, vec_v)
    return (gvec[0, LOSS_ROW, 0],) + tuple(updated)


def solution(mesh):
    chan_row = P("chan", None)
    chan_mid = P(None, "chan", None)
    chan_vec = P(None, "chan")
    return jax.shard_map(
        functools.partial(per_device, mesh.shape["chan"], mesh.shape["dp"]),
        mesh=mesh,
        in_specs=(P("dp", None, None, None), P("dp", None), P("dp"), P(None, "dp", None), P())
        + (chan_row,) * 3 + (chan_mid,) * 9 + (P(),) * 3 + (chan_vec,) * 3,
        out_specs=(P(), P()) + (chan_row,) * 3 + (chan_mid,) * 12 + (P(),) * 3 + (chan_vec,) * 3 + (chan_mid,),
        check_vma=False,
    )
```

```python
import functools
import math

import jax
import jax.numpy as jnp
from jax import lax
from jax.experimental import pallas as pl
from jax.experimental.pallas import tpu as pltpu
from jax.sharding import PartitionSpec as P

TEMB = 512
HW = 16
PIX = HW * HW
GSIZE = 8
C = 256
TAPS = 9
KW = C * TAPS
HALF = 128 * TAPS

NORM_EPS = 1e-05
BETA_ONE = 0.9
BETA_TWO = 0.95
ADAM_EPS = 1e-06
DECAY = 0.01
RATE = 0.3
F32 = jnp.float32
BF16 = jnp.bfloat16
HIGH = lax.Precision.HIGHEST
MESH = pl.DeviceIdType.MESH
NN = (((1,), (0,)), ((), ()))
NT = (((1,), (1,)), ((), ()))
TN = (((0,), (0,)), ((), ()))
MIB = 1024 * 1024

XL = (3, 3, 3, 4)
DELAYS = (2, 5, 2)
VEC_ROWS = 22
LOSS_ROW = 24
MAIN = HALF + 128 + 128
SUM_ROWS = 16
CONV, TMB, ATTN = tuple(dict(conv=0, temb=0, attn=0))
HERE, W_IN = tuple(dict(_here=0, w_in=0))
LOG_TEN_THOUSAND = math.log(10000.0)


def dot(a, b, dims, precision=None):
    return lax.dot_general(a, b, dims, precision=precision, preferred_element_type=F32)


def iota(shape, axis):
    return lax.broadcasted_iota(jnp.int32, shape, axis)


def tap_order():
    wanted = (iota((1, HALF), 1) & 127) * TAPS + (iota((1, HALF), 1) >> 7)
    return jnp.where(iota((HALF, 1), 0) == wanted, 1.0, 0.0).astype(BF16)


def flip(value, mask):
    bit = 1
    while bit <= mask:
        if mask & bit:
            value = value + bit * (1 - 2 * ((value // bit) % 2))
        bit *= 2
    return value


def remote(src, dst, send_sem, recv_sem, target):
    return pltpu.make_async_remote_copy(
        src_ref=src, dst_ref=dst, send_sem=send_sem, recv_sem=recv_sem,
        device_id=target, device_id_type=MESH,
    )


def row_sum(value):
    return jnp.sum(value, axis=0, keepdims=True)


def group_mean(row):
    row = jnp.broadcast_to(row, (8, C))
    lane = iota(row.shape, 1)
    step = 1
    while step < GSIZE:
        up = pltpu.roll(row, C - step, 1)
        down = pltpu.roll(row, step, 1)
        row = row + jnp.where((lane & step) == 0, up, down)
        step *= 2
    return row[0:1] * (1.0 / (GSIZE * PIX))


def squares(value):
    return jnp.sum(jnp.sum(value * value, axis=1, keepdims=True), axis=0, keepdims=True)


def matrix_parts(lr):
    parts = []
    for k in range(4):
        for h in range(2):
            parts.append((1 + k, CONV, k, slice(h * HALF, (h + 1) * HALF), h,
                          slice(k * lr, (k + 1) * lr), slice(0, HALF)))
    for k in range(2):
        for j in range(4):
            top = (j % 2) * 2 * lr + k * lr
            parts.append((5 + k, TMB, k, slice(j * 128, (j + 1) * 128), j // 2,
                          slice(top, top + lr), slice(HALF + 128, MAIN)))
    for k in range(4):
        for h in range(2):
            parts.append((7 + k, ATTN, k, slice(h * 128, (h + 1) * 128), h,
                          slice(k * lr, (k + 1) * lr), slice(HALF, HALF + 128)))
    return parts


STATE = tuple(dict(
    w_in=0, m_in=0, v_in=0, conv_w=0, conv_m=0, conv_v=0, temb_w=0, temb_m=0, temb_v=0, attn_w=0, attn_m=0,
    attn_v=0, out_w=0, out_m=0, out_v=0, vectors=0, vec_m=0, vec_v=0,
))
PASSED = tuple(dict(
    in_first=0, in_second=0, conv_first=0, conv_second=0, temb_first=0, temb_second=0, attn_first=0,
    attn_second=0, out_first=0, out_second=0, vec_new=0, vec_first=0, vec_second=0, attn_grad=0,
))
UPDATES = tuple(dict(
    in_update=0, conv_update=0, temb_update=0, attn_update=0, out_update=0,
))
WEIGHTS = tuple(dict(
    w_in=0, conv_w=0, temb_w=0, attn_w=0, out_w=0,
))


class Names:
    def __init__(self, names, refs):
        assert len(names) == len(refs)
        self.__dict__.update(zip(names, refs))


def step_kernel(n, ny, nz, nx, dp, lr, images, names, *refs):
    r = Names(names, refs)
    rows_all = images * PIX
    scale = C ** -0.5
    me = lax.axis_index("chan")
    part = lax.axis_index("dp")
    z, y = me // ny, me % ny
    x, core = part // 2, part % 2
    sibling = (x * 2 + 1 - core, me)

    loads = {}

    def load(i, name):
        src, dst = getattr(r, name + "_hbm"), getattr(r, name)
        loads[name] = pltpu.make_async_copy(src, dst, r.load_sem.at[i])
        loads[name].start()

    for k in range(4):
        loads[k] = pltpu.make_async_copy(r.conv_w_hbm.at[k], r.conv_w.at[k], r.conv_sem.at[k])
        loads[k].start()
    for name in ("vectors", W_IN, "temb_w", "attn_w", "out_w"):
        load(STATE.index(name), name)
    for i, name in enumerate(("canvas", "noise")):
        load(len(STATE) + i, name)
    for i, name in enumerate(STATE):
        if name not in loads and name != "conv_w":
            load(i, name)

    offsets = [(i, j) for i in range(nz) for j in range(ny)][1:]
    place = {o: i for i, o in enumerate(offsets)}

    def chan_at(o):
        return flip(z, o[0]) * ny + flip(y, o[1])

    def next_part(k):
        return lax.rem(part + k, dp)

    barrier = pltpu.get_barrier_semaphore()
    for o in offsets:
        pl.semaphore_signal(barrier, inc=1, device_id=(part, chan_at(o)), device_id_type=MESH)
    for k in range(1, dp):
        pl.semaphore_signal(barrier, inc=1, device_id=(next_part(k), me), device_id_type=MESH)

    core_lanes = KW // 2
    use_x = nx == 2
    chunk_rows = max(lr, 16)
    conv_chunks = 4 * lr // chunk_rows
    chunks = list(range(conv_chunks))
    chunks.insert((conv_chunks + 1) // 2, None)

    def x_lanes(chunk):
        return (XL[chunk % 4]) * 128 if use_x else 0

    def rows_of(chunk):
        return pl.ds(chunk * chunk_rows, chunk_rows)

    attn_x = lr // 2 if use_x and lr >= 32 else 0

    def near_ref(chunk, src, c):
        if chunk is None:
            start = c * 2 * lr + x * attn_x if attn_x else c * 2 * lr
            return r.attn_all.at[src, pl.ds(pl.multiple_of(start, 16), 2 * lr - attn_x), :]
        wide = x_lanes(chunk)
        start = c * core_lanes + x * wide if wide else c * core_lanes
        return r.whole.at[src, rows_of(chunk), pl.ds(pl.multiple_of(start, 128), core_lanes - wide)]

    def x_ref(chunk, src, c, side):
        if chunk is None:
            start = c * 2 * lr + side * (2 * lr - attn_x)
            return r.attn_all.at[src, pl.ds(pl.multiple_of(start, 16), attn_x), :]
        wide = x_lanes(chunk)
        start = c * core_lanes + side * (core_lanes - wide)
        return r.whole.at[src, rows_of(chunk), pl.ds(pl.multiple_of(start, 128), wide)]

    def has_x(chunk):
        return attn_x > 0 if chunk is None else x_lanes(chunk) > 0

    sends = []

    def send(*args):
        copy = remote(*args)
        copy.start()
        sends.append(copy)

    def index(chunk):
        return conv_chunks if chunk is None else chunk

    def send_near(chunk, src, o, target):
        i = index(chunk)
        ref = near_ref(chunk, src, core)
        send(ref, ref, r.near_send.at[i, place[o]], r.near_recv.at[i, place[o]], target)

    def send_core(chunk, src, o, piece):
        i = index(chunk)
        ref = near_ref(chunk, src, core) if piece == 0 else x_ref(chunk, src, core, 1 - x)
        send(ref, ref, r.core_send.at[piece, i, place[o]], r.core_recv.at[piece, i, place[o]], sibling)

    def begin(chunk):
        for i in range(1, nz):
            send_near(chunk, me, (i, 0), (part, chan_at((i, 0))))
        for j in range(1, ny):
            send_near(chunk, me, (0, j), (part, chan_at((0, j))))

    def near_in(chunk, o):
        i = index(chunk)
        src = chan_at(o)
        ref = near_ref(chunk, src, core)
        remote(ref, ref, r.near_send.at[i, place[o]], r.near_recv.at[i, place[o]], (part, src)).wait_recv()
        if o[1] == 0:
            for j in range(1, ny):
                send_near(chunk, src, (o[0], j), (part, chan_at((0, j))))
        if has_x(chunk):
            ref = x_ref(chunk, src, core, x)
            send(ref, ref, r.x_send.at[i, place[o]], r.x_recv.at[i, place[o]], ((1 - x) * 2 + core, me))
        send_core(chunk, src, o, 0)

    def x_in(chunk, o):
        if has_x(chunk):
            i = index(chunk)
            src = chan_at(o)
            ref = x_ref(chunk, src, core, 1 - x)
            remote(ref, ref, r.x_send.at[i, place[o]], r.x_recv.at[i, place[o]], ((1 - x) * 2 + core, me)).wait_recv()
            send_core(chunk, src, o, 1)

    def core_in(chunk, o):
        i = index(chunk)
        src = chan_at(o)
        pieces = [near_ref(chunk, src, 1 - core)]
        if has_x(chunk):
            pieces.append(x_ref(chunk, src, 1 - core, 1 - x))
        for piece, ref in enumerate(pieces):
            remote(ref, ref, r.core_send.at[piece, i, place[o]], r.core_recv.at[piece, i, place[o]], sibling).wait_recv()

    def stage_one(chunk):
        for i in range(1, nz):
            near_in(chunk, (i, 0))

    def stage_two(chunk):
        for j in range(1, ny):
            near_in(chunk, (0, j))
        for i in range(1, nz):
            for j in range(1, ny):
                near_in(chunk, (i, j))

    def stage_three(chunk):
        for o in offsets:
            x_in(chunk, o)

    def stage_four(chunk):
        for o in offsets:
            core_in(chunk, o)

    turn = [0]

    def gather_turn():
        i = turn[0]
        turn[0] += 1
        for stage, delay in ((stage_one, 0), (stage_two, 1), (stage_three, 2), (stage_four, 3)):
            if 0 <= i - delay < len(chunks):
                stage(chunks[i - delay])
            if delay == 0 and 2 <= i + 2 < len(chunks):
                begin(chunks[i + 2])

    def arrived(chunk):
        while turn[0] < chunks.index(chunk) + 4:
            gather_turn()

    order = tap_order()
    r.order[...] = order

    def prepare(convs, extra=None):
        stack = []
        for k in convs:
            loads[k].wait()
            weight = r.conv_w[k].astype(BF16)
            stack += [weight[:, :HALF], weight[:, HALF:]]
        if extra is not None:
            stack.append(extra)
        mixed = dot(jnp.concatenate(stack, axis=0), r.order[...], NN)
        for i, k in enumerate(convs):
            for tap in range(TAPS):
                for h in range(2):
                    lanes = slice(tap * C + h * 128, tap * C + h * 128 + 128)
                    top = (2 * i + h) * lr
                    r.whole[me, k * lr:(k + 1) * lr, lanes] = mixed[top:top + lr, tap * 128:(tap + 1) * 128].astype(BF16)
        return mixed[2 * len(convs) * lr:]

    steps_row = iota((16, C), 0)
    steps_all = jnp.zeros((16, C), F32)
    for b in range(images):
        steps_all = jnp.where(steps_row == b, r.steps[b].astype(F32), steps_all)
    frequency = jnp.exp(-LOG_TEN_THOUSAND * iota((1, C), 1).astype(F32) / (TEMB // 2))
    angles = steps_all * frequency
    for i, wave in enumerate((jnp.sin(angles), jnp.cos(angles))):
        wave = jnp.where(steps_row < images, wave / (1.0 + jnp.exp(-wave)), 0.0)
        r.temb_act[:, i * C:(i + 1) * C] = wave.astype(BF16)

    pl.semaphore_wait(barrier, n + dp - 2)
    prepare((0, 1))
    begin(chunks[0])
    if conv_chunks > 2:
        begin(chunks[1])

    loads["vectors"].wait()
    loads[W_IN].wait()
    loads["temb_w"].wait()
    r.own_rows[...] = jnp.zeros_like(r.own_rows)
    r.own_rows[0:VEC_ROWS, 0:lr] = r.vectors[...]
    for block in range(2):
        shift = dot(r.temb_act[...], r.temb_w[block].astype(BF16), NT)
        for b in range(images):
            row = VEC_ROWS + block * images + b
            r.own_rows[row:row + 1, 0:lr] = (
                shift[b:b + 1, :] + r.vectors[17 + block:18 + block, :]
            ) + r.vectors[13 + 2 * block:14 + 2 * block, :]
    r.in_scr[...] = jnp.zeros_like(r.in_scr)
    r.in_scr[0:lr, 0:27] = r.w_in[...]
    turned = r.in_scr[...].T
    packed = [jnp.zeros((8, 128), F32), jnp.zeros((8, 128), F32)]
    for g in range(4):
        for i, rows in enumerate((r.own_rows[g * 8:g * 8 + 8, :], turned[g * 8:g * 8 + 8, :])):
            packed[i] += rows if g == 0 else pltpu.roll(rows, g * lr, 1)
    r.smalls[me, 0:8, :] = packed[0]
    r.smalls[me, 8:16, :] = packed[1]
    total = jnp.int32(0)
    for b in range(images):
        side = jnp.minimum(jnp.maximum(r.crop[b, 2], 0), HW)
        total += 3 * side * side
    r.counts[part] = jnp.full((8, 128), total, jnp.int32).astype(F32)
    for o in offsets:
        i = place[o]
        send(r.smalls.at[me], r.smalls.at[me], r.small_send.at[i], r.small_recv.at[i], (part, chan_at(o)))
    for i in range(1, dp):
        send(r.counts.at[part], r.counts.at[part], r.count_send.at[i - 1], r.count_recv.at[i - 1], (next_part(i), me))

    loads["attn_w"].wait()
    for k in range(4):
        r.attn_all[me, k * lr:(k + 1) * lr, :] = r.attn_w[k].astype(BF16)
    loads["out_w"].wait()
    r.out_scr[...] = jnp.zeros_like(r.out_scr)
    for h in range(2):
        r.out_scr[h * 8:h * 8 + 3, :] = r.out_w[:, h * HALF:(h + 1) * HALF]
    out_mixed = prepare((2, 3), r.out_scr[...].astype(BF16))
    for tap in range(TAPS):
        for h in range(2):
            r.out_taps[tap * 8:tap * 8 + 8, h * 128:(h + 1) * 128] = out_mixed[
                h * 8:h * 8 + 8, tap * 128:(tap + 1) * 128
            ]
    if conv_chunks <= 2:
        begin(chunks[1])

    lane = iota((1, PIX), 1)
    pix_x, pix_y = lane & (HW - 1), lane >> 4
    size = r.canvas.shape[2]
    loads["canvas"].wait()
    loads["noise"].wait()
    noise_rows, mask_rows, noisy_rows = [], [], []
    for b in range(images):
        phase = (jnp.broadcast_to(r.steps[b].astype(F32), (1, PIX)) / 1000.0 + 0.008) / 1.008
        alpha_bar = jnp.cos(phase * (math.pi / 2)) ** 2
        pick = jnp.where(iota((size, PIX), 0) == r.crop[b, 1] + pix_x, 1.0, 0.0)
        flat = r.canvas[b].reshape(3 * size, size)
        spread = dot(flat, pick, NN, HIGH).reshape(3, size, PIX)
        chosen = iota((size, PIX), 0) == r.crop[b, 0] + pix_y
        clean = jnp.sum(jnp.where(chosen[None], spread, 0.0), axis=1)
        noise_b = r.noise[:, b, :]
        noisy_rows.append(jnp.sqrt(alpha_bar) * clean + jnp.sqrt(1.0 - alpha_bar) * noise_b)
        noise_rows.append(noise_b)
        side = r.crop[b, 2]
        mask_rows.append(jnp.where((pix_x < side) & (pix_y < side), 1.0, 0.0))
    zeros5 = jnp.zeros((5, rows_all), F32)
    noisy = jnp.concatenate([jnp.concatenate(noisy_rows, axis=1), zeros5], axis=0)
    noise_all = jnp.concatenate([jnp.concatenate(noise_rows, axis=1), zeros5], axis=0)
    mask_all = jnp.concatenate(mask_rows, axis=1)

    lane_all = iota((8, rows_all), 1)
    px, py = lane_all & (HW - 1), (lane_all >> 4) & (HW - 1)

    def tap_shift(field, tap):
        dy, dx = tap // 3 - 1, tap % 3 - 1
        move = -(dy * HW + dx) % rows_all
        out = pltpu.roll(field, move, 1) if move else field
        inside = (px + dx >= 0) & (px + dx < HW) & (py + dy >= 0) & (py + dy < HW)
        return jnp.where(inside, out, 0.0)

    noisy = noisy.astype(BF16).astype(F32)
    r.rows_scr[...] = jnp.zeros_like(r.rows_scr)
    for tap in range(TAPS):
        moved = tap_shift(noisy, tap)
        for colour in range(3):
            r.rows_scr[colour * TAPS + tap:colour * TAPS + tap + 1, :] = moved[colour:colour + 1]
    r.taps0[...] = r.rows_scr[...].astype(BF16)

    gather_turn()

    for o in offsets:
        src = chan_at(o)
        remote(r.smalls.at[src], r.smalls.at[src], r.small_send.at[place[o]], r.small_recv.at[place[o]],
               (part, src)).wait_recv()
    for i in range(1, dp):
        p = lax.rem(part - i + dp, dp)
        remote(r.counts.at[p], r.counts.at[p], r.count_send.at[i - 1], r.count_recv.at[i - 1], (p, me)).wait_recv()
    lane_wide = iota((16, C), 1)
    unpacked = [jnp.zeros((16, C), F32) for g in range(4)]
    for j in range(n):
        block = jnp.concatenate([r.smalls[j], jnp.zeros((16, 128), F32)], axis=1)
        for g in range(4):
            piece = jnp.where((lane_wide >= g * lr) & (lane_wide < (g + 1) * lr), block, 0.0)
            move = (j - g) * lr % C
            unpacked[g] += pltpu.roll(piece, move, 1) if move else piece
    for g in range(4):
        r.vec[g * 8:g * 8 + 8, :] = unpacked[g][0:8]
        r.w_in_all[g * 8:g * 8 + 8, :] = unpacked[g][8:16]
    total = r.counts[0, 0:1, 0:1]
    for k in range(1, dp):
        total = total + r.counts[k, 0:1, 0:1]

    def vrow(i):
        return r.vec[i:i + 1, :]

    def span(b):
        return slice(b * PIX, (b + 1) * PIX)

    def conv_weight(k):
        return r.whole[:, k * lr:(k + 1) * lr, :].reshape(C, KW)

    def attn_weight(k):
        return r.attn_all[:, k * lr:(k + 1) * lr, :].reshape(C, C)

    col_x = iota((PIX, C), 0) & (HW - 1)
    blank = jnp.zeros((HW, C), BF16)
    hidden, xhat, dact, rstd, acts = r.hidden, r.xhat, r.dact, r.rstd, r.acts
    cols = (r.col0, r.col1, r.col2, r.col3)

    def norm_fwd(i, value, gain, shift, store):
        for b in range(images):
            image = value[span(b)]
            centred = image - group_mean(row_sum(image))
            inv = lax.rsqrt(group_mean(row_sum(centred * centred)) + NORM_EPS)
            normed = centred * inv
            scaled = normed * gain + shift
            gate = 0.5 * jnp.tanh(0.5 * scaled) + 0.5
            act = scaled * gate
            xhat[i, span(b), :] = normed
            dact[i, span(b), :] = gate + act * (1.0 - gate)
            rstd[i * images + b:i * images + b + 1, :] = inv
            store(b, act)

    def store_cols(ref, b, act):
        left = jnp.where(col_x > 0, pltpu.roll(act, 1, 0), 0.0)
        right = jnp.where(col_x < HW - 1, pltpu.roll(act, PIX - 1, 0), 0.0)
        for dx, moved in enumerate((left, act, right)):
            low = moved.astype(BF16)
            for dy in range(3):
                lanes = slice((3 * dy + dx) * C, (3 * dy + dx + 1) * C)
                base = b * PIX
                if dy == 0:
                    ref[base:base + HW, lanes] = blank
                    ref[base + HW:base + PIX, lanes] = low[:PIX - HW]
                elif dy == 1:
                    ref[base:base + PIX, lanes] = low
                else:
                    ref[base:base + PIX - HW, lanes] = low[HW:]
                    ref[base + PIX - HW:base + PIX, lanes] = blank

    def add_rows(value, first):
        return jnp.concatenate([value[span(b)] + vrow(first + b) for b in range(images)], axis=0)

    def chunk_of(k):
        return k * lr // chunk_rows

    def block_fwd(block, source, target):
        norm_fwd(3 * block, hidden[source], vrow(3 * block), vrow(6 + 3 * block),
                 functools.partial(store_cols, cols[2 * block]))
        arrived(chunk_of(2 * block))
        middle = dot(cols[2 * block][...], conv_weight(2 * block), NT)
        middle = add_rows(middle, VEC_ROWS + block * images)
        norm_fwd(3 * block + 1, middle, vrow(3 * block + 1), vrow(7 + 3 * block),
                 functools.partial(store_cols, cols[2 * block + 1]))
        arrived(chunk_of(2 * block + 1))
        branch = dot(cols[2 * block + 1][...], conv_weight(2 * block + 1), NT)
        hidden[target] = hidden[source] + (branch + vrow(14 + 2 * block))

    def store_act(i):
        def store(b, act):
            acts[i, span(b), :] = act.astype(BF16)
        return store

    hidden[0] = dot(r.taps0[...], r.w_in_all[...].astype(BF16), TN) + vrow(12)
    block_fwd(0, 0, 1)

    norm_fwd(2, hidden[1], vrow(2), vrow(8), store_act(0))
    arrived(None)
    r.q_scr[...] = (dot(acts[0], attn_weight(0), NT) + vrow(19)).astype(BF16)
    r.k_scr[...] = dot(acts[0], attn_weight(1), NT).astype(BF16)
    r.v_scr[...] = (dot(acts[0], attn_weight(2), NT) + vrow(20)).astype(BF16)
    for b in range(images):
        scores = dot(r.q_scr[span(b), :], r.k_scr[span(b), :], NT) * scale
        raised = jnp.exp(scores - jnp.max(scores, axis=1, keepdims=True))
        soft = raised / jnp.sum(raised, axis=1, keepdims=True)
        r.probs[b] = soft
        r.mixed[span(b), :] = dot(soft.astype(BF16), r.v_scr[span(b), :], NN).astype(BF16)
    hidden[0] = hidden[1] + (dot(r.mixed[...], attn_weight(3), NT) + vrow(21))

    block_fwd(1, 0, 1)
    norm_fwd(5, hidden[1], vrow(5), vrow(11), store_act(1))

    out_low = r.out_taps[...].astype(BF16)
    fanned = dot(out_low, acts[1], NT)
    pred = jnp.zeros((8, rows_all), F32)
    for tap in range(TAPS):
        pred += tap_shift(fanned[tap * 8:tap * 8 + 8], tap)
    error = pred - noise_all
    masked = mask_all * error
    inverse = 1.0 / total
    loss = jnp.sum(jnp.sum(masked * error, axis=1, keepdims=True), axis=0, keepdims=True) * inverse
    grad_pred = (2.0 * masked * inverse).astype(BF16).astype(F32)
    spread_pred = jnp.concatenate(
        [tap_shift(grad_pred, TAPS - 1 - tap) for tap in range(TAPS)], axis=0
    ).astype(BF16)
    out_grad = dot(spread_pred, acts[1], NN)

    lanes_attn, lanes_temb = slice(HALF, HALF + 128), slice(HALF + 128, MAIN)

    def region(chunk):
        if chunk == ATTN:
            return slice(0, 4 * lr), lanes_attn
        if chunk == TMB:
            return slice(0, 4 * lr), lanes_temb
        return slice(chunk * chunk_rows, (chunk + 1) * chunk_rows), slice(0, HALF)

    def family(chunk):
        if chunk == "out":
            return (r.out_local, r.out_one, r.out_two, r.out_last), (slice(None), slice(None)), conv_chunks + 2
        i = conv_chunks + (ATTN, TMB).index(chunk) if isinstance(chunk, str) else chunk
        return (r.local, r.one, r.two, r.last), region(chunk), i

    def view(ref, i, where):
        return ref.at[(i,) + where]

    def reduce_one(chunk):
        (local, one, two, last), where, i = family(chunk)
        send(view(local, 1 - core, where), one.at[where], r.one_send.at[i], r.one_recv.at[i], sibling)

    def reduce_two(chunk):
        (local, one, two, last), where, i = family(chunk)
        remote(view(local, 1 - core, where), one.at[where], r.one_send.at[i], r.one_recv.at[i], sibling).wait_recv()
        both = local[(core,) + where].astype(F32) + one[where].astype(F32)
        two[(x,) + where] = both.astype(two.dtype)
        for m in range(1, nx):
            ref = view(two, x, where)
            send(ref, ref, r.two_send.at[i, m - 1], r.two_recv.at[i, m - 1], (lax.rem(x + m, nx) * 2 + core, me))

    def reduce_three(chunk):
        (local, one, two, last), where, i = family(chunk)
        for m in range(1, nx):
            sender = lax.rem(x - m + nx, nx)
            ref = view(two, sender, where)
            remote(ref, ref, r.two_send.at[i, m - 1], r.two_recv.at[i, m - 1], (sender * 2 + core, me)).wait_recv()
        summed = two[(0,) + where].astype(F32)
        for m in range(1, nx):
            summed = summed + two[(m,) + where].astype(F32)
        last[(core,) + where] = summed.astype(last.dtype)
        ref = view(last, core, where)
        send(ref, ref, r.three_send.at[i], r.three_recv.at[i], sibling)

    def reduce_four(chunk):
        (local, one, two, last), where, i = family(chunk)
        ref = view(last, 1 - core, where)
        remote(ref, ref, r.three_send.at[i], r.three_recv.at[i], sibling).wait_recv()

    due = []
    clock = [0]

    def run_due(entry):
        delay = {1: DELAYS[0], 2: DELAYS[1], 3: DELAYS[2]}
        stage, chunk = entry
        (reduce_one, reduce_two, reduce_three, reduce_four)[stage - 1](chunk)
        if stage < 4:
            due.append((clock[0] + delay[stage], (stage + 1, chunk)))

    def tick():
        clock[0] += 1
        for item in [item for item in due if item[0] <= clock[0]]:
            due.remove(item)
            run_due(item[1])

    def ready(chunk):
        run_due((1, chunk))

    def finish(chunk=None):
        while True:
            left = [item for item in due if chunk is None or item[1][1] == chunk]
            if not left:
                return
            item = min(left, key=lambda item: (item[1][0], item[0]))
            due.remove(item)
            run_due(item[1])

    for h in range(2):
        for tap in range(TAPS):
            r.out_local[h, :, tap * 128:(tap + 1) * 128] = out_grad[tap * 8:tap * 8 + 8, h * 128:(h + 1) * 128]
    ready("out")
    grad = dot(spread_pred, out_low, TN)

    gvec = r.gvec
    gvec[...] = jnp.zeros_like(gvec)
    pick_own = jnp.where(iota((lr, C), 1) == iota((lr, C), 0) + me * lr, 1.0, 0.0).astype(BF16)
    hole = jnp.zeros((HW, C), F32)

    def own_rows(low):
        return dot(pick_own, low, NT).astype(BF16)

    def norm_back(i, grad, gain_row):
        outs = []
        gain = vrow(gain_row)
        gain_sum = jnp.zeros((1, C), F32)
        shift_sum = jnp.zeros((1, C), F32)
        for b in range(images):
            slope = grad[span(b)] * dact[i, span(b), :]
            normed = xhat[i, span(b), :]
            shift_b = row_sum(slope)
            gain_b = row_sum(slope * normed)
            mean_one = group_mean(shift_b * gain)
            mean_two = group_mean(gain_b * gain)
            inv = rstd[i * images + b:i * images + b + 1, :]
            outs.append(inv * (slope * gain - mean_one - normed * mean_two))
            gain_sum += gain_b
            shift_sum += shift_b
        gvec[gain_row:gain_row + 1, :] = gain_sum
        gvec[6 + gain_row:7 + gain_row, :] = shift_sum
        return jnp.concatenate(outs, axis=0)

    def conv_back(k, low):
        own = dot(own_rows(low), cols[k][...], NN)
        for h in range(2):
            for tap in range(TAPS):
                r.local[h, k * lr:(k + 1) * lr, tap * 128:(tap + 1) * 128] = own[
                    :, tap * C + h * 128:tap * C + h * 128 + 128
                ].astype(BF16)
        if k * lr % chunk_rows == 0:
            ready(chunk_of(k))
        tick()
        parts = dot(low, conv_weight(k), NN)
        outs = []
        for b in range(images):
            sides = []
            for dx in range(3):
                up = parts[span(b), dx * C:(dx + 1) * C]
                mid = parts[span(b), (3 + dx) * C:(4 + dx) * C]
                down = parts[span(b), (6 + dx) * C:(7 + dx) * C]
                sides.append(
                    mid
                    + jnp.concatenate([up[HW:], hole], axis=0)
                    + jnp.concatenate([hole, down[:PIX - HW]], axis=0)
                )
            left = pltpu.roll(jnp.where(col_x > 0, sides[0], 0.0), PIX - 1, 0)
            right = pltpu.roll(jnp.where(col_x < HW - 1, sides[2], 0.0), 1, 0)
            outs.append(sides[1] + left + right)
        tick()
        return jnp.concatenate(outs, axis=0)

    def block_back(block, grad):
        gvec[14 + 2 * block:15 + 2 * block, :] = row_sum(grad)
        back = conv_back(2 * block + 1, grad.astype(BF16))
        middle = norm_back(3 * block + 1, back, 3 * block + 1)
        r.gsum[...] = jnp.zeros_like(r.gsum)
        for b in range(images):
            r.gsum[b:b + 1, :] = row_sum(middle[span(b)])
        whole_sum = row_sum(r.gsum[...])
        gvec[13 + 2 * block:14 + 2 * block, :] = whole_sum
        gvec[17 + block:18 + block, :] = whole_sum
        own = dot(pick_own, r.gsum[...].astype(BF16), NT).astype(BF16)
        temb = dot(own, r.temb_act[...], NN)
        for j in range(4):
            top = (j % 2) * 2 * lr + block * lr
            r.local[j // 2, top:top + lr, lanes_temb] = temb[:, j * 128:(j + 1) * 128].astype(BF16)
        if block == 0:
            ready(TMB)
        tick()
        back = conv_back(2 * block, middle.astype(BF16))
        return grad + norm_back(3 * block, back, 3 * block)

    grad = norm_back(5, grad, 5)
    tick()
    grad = block_back(1, grad)
    tick()

    gvec[21:22, :] = row_sum(grad)
    low = grad.astype(BF16)

    def attn_own(k, low, field):
        own = dot(own_rows(low), field, NN)
        for h in range(2):
            r.local[h, k * lr:(k + 1) * lr, lanes_attn] = own[:, h * 128:(h + 1) * 128].astype(BF16)

    attn_own(3, low, r.mixed[...])
    mixed_low = dot(low, attn_weight(3), NN).astype(BF16)
    grads_q, grads_k, grads_v = [], [], []
    for b in range(images):
        image = mixed_low[span(b)]
        soft = r.probs[b]
        grad_soft = dot(image, r.v_scr[span(b), :], NT)
        grads_v.append(dot(soft.astype(BF16), image, TN))
        weighed = soft * grad_soft
        slope = (weighed - soft * jnp.sum(weighed, axis=1, keepdims=True)).astype(BF16)
        grads_q.append(scale * dot(slope, r.k_scr[span(b), :], NN))
        grads_k.append(scale * dot(slope, r.q_scr[span(b), :], TN))
    tick()
    back = jnp.zeros((rows_all, C), F32)
    for i, grads in enumerate((grads_q, grads_k, grads_v)):
        full = jnp.concatenate(grads, axis=0)
        if i != 1:
            gvec[19 + i // 2:20 + i // 2, :] = row_sum(full)
        low = full.astype(BF16)
        attn_own(i, low, acts[0])
        back += dot(low, attn_weight(i), NN)
    ready(ATTN)
    tick()
    grad = grad + norm_back(2, back, 2)
    tick()

    grad = block_back(0, grad)
    tick()
    gvec[12:13, :] = row_sum(grad)
    in_grad = dot(own_rows(grad.astype(BF16)), r.taps0[...], NT)

    own_vec = jnp.where(iota((32, 128), 1) < lr, pltpu.roll(gvec[...], lax.rem(C - me * lr, C), 1)[:, 0:128], 0.0)
    own_vec = jnp.where(iota((32, 128), 0) == LOSS_ROW, loss, own_vec)
    own_vec = jnp.where(iota((32, 128), 1) < lr, own_vec, 0.0)
    packed = [jnp.zeros((8, 128), F32), jnp.zeros((8, 128), F32)]
    for g in range(4):
        rows = own_vec[g * 8:g * 8 + 8, :]
        packed[0] += rows if g == 0 else pltpu.roll(rows, g * lr, 1)
    for g in range(lr // 8):
        rows = jnp.concatenate([in_grad[g * 8:g * 8 + 8, :], jnp.zeros((8, 96), F32)], axis=1)
        packed[1] += rows if g == 0 else pltpu.roll(rows, g * 32, 1)
    r.tiny[part, 0:8, :] = packed[0]
    r.tiny[part, 8:16, :] = packed[1]
    for i in range(1, dp):
        send(r.tiny.at[part], r.tiny.at[part], r.tiny_send.at[i - 1], r.tiny_recv.at[i - 1], (next_part(i), me))
    tick()

    for name in STATE:
        if name in loads and name not in ("vectors", W_IN, "temb_w", "attn_w", "out_w"):
            loads[name].wait()
    count = jnp.broadcast_to(r.count_step[0].astype(F32), (1, 128))
    fix_one = (1.0 / (1.0 - jnp.exp(math.log(BETA_ONE) * count)))[:, 0:1]
    fix_two = (1.0 / (1.0 - jnp.exp(math.log(BETA_TWO) * count)))[:, 0:1]

    def adapt(grad, first, second):
        first_new = BETA_ONE * first + (1.0 - BETA_ONE) * grad
        second_new = BETA_TWO * second + (1.0 - BETA_TWO) * grad * grad
        direction = first_new * fix_one / (jnp.sqrt(second_new * fix_two) + ADAM_EPS)
        return first_new, second_new, direction

    sums = {}

    def lamb(number, name, at, grad):
        names = (W_IN, "m_in", "v_in") if name == "in" else (name + "_w", name + "_m", name + "_v")
        weight, first, second = (getattr(r, each)[at] for each in names)
        first, second, direction = adapt(grad, first, second)
        update = direction + DECAY * weight
        getattr(r, name + "_first")[at] = first
        getattr(r, name + "_second")[at] = second
        getattr(r, name + "_update")[at] = update
        pair = (squares(weight), squares(update))
        if number in sums:
            pair = (sums[number][0] + pair[0], sums[number][1] + pair[1])
        sums[number] = pair

    every = slice(None)
    outward = []

    def put(name, k=None):
        src, dst = getattr(r, name), getattr(r, name + "_hbm")
        if k is not None:
            src, dst = src.at[k], dst.at[k]
        copy = pltpu.make_async_copy(src, dst, r.out_sem.at[len(outward)])
        copy.start()
        outward.append(copy)

    def put_all(name, k=None):
        for kind in ("first", "second", "update"):
            put(name + "_" + kind, k)

    def conv_steps(which, natural):
        for number, name, k, lanes, h, rows, held in matrix_parts(lr):
            if name == CONV and chunk_of(k) in which:
                top = h * len(which) * chunk_rows + k * lr - min(which) * chunk_rows
                lamb(number, name, (k, every, lanes), natural[top:top + lr])
                if h == 1:
                    put_all(CONV, k)

    early = list(range(1, conv_chunks))
    for chunk in early + [ATTN, TMB, "out"]:
        finish(chunk)
    stack = [r.last[h, chunk_rows:4 * lr, 0:HALF] for h in range(2)]
    stack += [jnp.concatenate([r.out_last[h], jnp.zeros((8, HALF), F32)], axis=0).astype(BF16) for h in range(2)]
    natural = dot(jnp.concatenate(stack, axis=0), r.order[...], NT)
    conv_steps(early, natural)
    top = 2 * (4 * lr - chunk_rows)
    for h in range(2):
        lamb(11, "out", (every, slice(h * HALF, (h + 1) * HALF)), natural[top + h * 16:top + h * 16 + 3])
    for number, name, k, lanes, h, rows, held in matrix_parts(lr):
        if name != CONV:
            value = r.last[h, rows, held].astype(F32)
            if name == ATTN:
                r.attn_grad[k, :, lanes] = value
            lamb(number, name, (k, every, lanes), value)
    for name in ("out", TMB, ATTN):
        put_all(name)
    put("attn_grad")
    finish()
    natural = dot(jnp.concatenate([r.last[h, 0:chunk_rows, 0:HALF] for h in range(2)], axis=0), r.order[...], NT)
    conv_steps([0], natural)

    for i in range(1, dp):
        p = lax.rem(part - i + dp, dp)
        remote(r.tiny.at[p], r.tiny.at[p], r.tiny_send.at[i - 1], r.tiny_recv.at[i - 1], (p, me)).wait_recv()
    tiny = r.tiny[0]
    for k in range(1, dp):
        tiny = tiny + r.tiny[k]
    for g in range(4):
        rows = tiny[0:8] if g == 0 else pltpu.roll(tiny[0:8], 128 - g * lr, 1)
        r.own_rows[g * 8:g * 8 + 8, :] = rows
    for g in range(lr // 8):
        rows = tiny[8:16] if g == 0 else pltpu.roll(tiny[8:16], 128 - g * 32, 1)
        r.in_scr[g * 8:g * 8 + 8, :] = rows
    lamb(0, "in", (every, every), r.in_scr[0:lr, 0:27])
    put_all("in")

    row = iota((SUM_ROWS, 128), 0)
    lane = iota((SUM_ROWS, 128), 1)
    table = jnp.zeros((SUM_ROWS, 128), F32)
    for number in range(11):
        for side in range(2):
            table = jnp.where((row == number) & (lane == side), sums[number][side], table)
    r.tables[me] = table
    for o in offsets:
        i = place[o]
        send(r.tables.at[me], r.tables.at[me], r.sum_send.at[i], r.sum_recv.at[i], (part, chan_at(o)))
    first, second, direction = adapt(r.own_rows[0:VEC_ROWS, 0:lr], r.vec_m[...], r.vec_v[...])
    r.vec_new[...] = r.vectors[...] - RATE * direction
    r.vec_first[...] = first
    r.vec_second[...] = second
    for name in ("vec_new", "vec_first", "vec_second"):
        put(name)
    for o in offsets:
        src = chan_at(o)
        remote(r.tables.at[src], r.tables.at[src], r.sum_send.at[place[o]], r.sum_recv.at[place[o]],
               (part, src)).wait_recv()
    total = r.tables[0]
    for k in range(1, n):
        total = total + r.tables[k]
    for side in range(2):
        total = jnp.where((row == 11) & (lane == side), sums[11][side], total)
    total = jnp.where((row == 12) & (lane == 0), r.own_rows[LOSS_ROW:LOSS_ROW + 1, 0:1], total)
    r.norms[...] = total
    put("norms")
    for copy in sends:
        copy.wait_send()
    for copy in outward:
        copy.wait()


def update_kernel(names, *refs):
    r = Names(names, refs)
    copies = []

    def copy(src, dst):
        made = pltpu.make_async_copy(src, dst, r.sem.at[len(copies)])
        made.start()
        copies.append(made)
        return made

    copy(r.norms, r.norms_in)
    loads = {}
    for k in range(4):
        loads[(CONV, k)] = [
            copy(getattr(r, name).at[k], getattr(r, name + HERE).at[k]) for name in ("conv_w", "conv_update")
        ]
    for name in ("in", TMB, ATTN, "out"):
        weight = W_IN if name == "in" else name + "_w"
        loads[name] = [copy(getattr(r, each), getattr(r, each + HERE)) for each in (weight, name + "_update")]
    passing = [(name, copy(getattr(r, name), getattr(r, name + HERE))) for name in PASSED]
    copies[0].wait()
    outward = []

    def ratio(number):
        pair = r.norms_in[number:number + 1, 0:2]
        return RATE * jnp.sqrt(pair[:, 0:1] / (pair[:, 1:2] + 1e-06))

    r.norms_here[...] = jnp.sqrt(r.norms_in[...].T[0:2, 0:12])
    outward.append(copy(r.norms_here, r.norms_out))
    r.loss_out[...] = r.norms_in[12:13, 0:1]
    for number, name, k in [(0, "in", None)] + [(1 + k, CONV, k) for k in range(4)] + [
        (5 + k, TMB, k) for k in range(2)
    ] + [(7 + k, ATTN, k) for k in range(4)] + [(11, "out", None)]:
        weight_name = W_IN if name == "in" else name + "_w"
        for wait in loads.pop((name, k) if name == CONV else name, ()):
            wait.wait()
        at = (slice(None), slice(None)) if k is None else (k, slice(None), slice(None))
        here, target = getattr(r, name + HERE), getattr(r, name + "_new_out")
        new = getattr(r, weight_name + HERE)[at] - ratio(number) * getattr(r, name + "_update_here")[at]
        here[at] = new
        last = k in (None, {CONV: k, TMB: 1, ATTN: 3}.get(name))
        if name == CONV:
            outward.append(copy(here.at[k], target.at[k]))
        elif last:
            outward.append(copy(here, target))
        if k is not None:
            low = getattr(r, name + "_low_here")
            low[at] = new.astype(BF16)
            if name == CONV:
                outward.append(copy(low.at[k], getattr(r, name + "_low_out").at[k]))
            elif last:
                outward.append(copy(low, getattr(r, name + "_low_out")))
    for name, made in passing:
        made.wait()
        outward.append(copy(getattr(r, name + HERE), getattr(r, name + "_out")))
    for made in outward:
        made.wait()


def vmem_spec():
    return pl.BlockSpec(memory_space=pltpu.VMEM)


def smem_spec():
    return pl.BlockSpec(memory_space=pltpu.SMEM)


def hbm_spec():
    return pl.BlockSpec(memory_space=pltpu.HBM)


def shape(dims, kind=F32):
    return jax.ShapeDtypeStruct(dims, kind)


def per_device(n, dp, canvas, crop_boxes, time_steps, noise_field, step_count, *state):
    images = canvas.shape[0]
    rows_all = images * PIX
    own = dict(zip(STATE, state))
    lr = own["conv_w"].shape[1]
    nx = dp // 2
    ny = 1 << ((n.bit_length() - 2) // 2)
    nz = n // ny
    dma = pltpu.SemaphoreType.DMA
    chunk_rows = max(lr, 16)
    chunks = 4 * lr // chunk_rows + 1

    made = {}
    for key, name in (("in", W_IN), (CONV, "conv_w"), (TMB, "temb_w"), (ATTN, "attn_w"), ("out", "out_w")):
        for kind in ("first", "second", "update"):
            made[key + "_" + kind] = own[name].shape
    for name in ("vec_new", "vec_first", "vec_second"):
        made[name] = own["vectors"].shape
    made["attn_grad"] = own["attn_w"].shape
    made["norms"] = (SUM_ROWS, 128)

    inputs = ["crop", "steps", "count_step", "canvas_hbm", "noise_hbm"] + [name + "_hbm" for name in STATE]
    scratch = {name: pltpu.VMEM(own[name].shape, F32) for name in STATE}
    wide = max(nx - 1, 1)
    scratch.update(
        canvas=pltpu.VMEM(canvas.shape, F32), noise=pltpu.VMEM(noise_field.shape, F32),
        load_sem=dma((len(STATE) + 2,)), conv_sem=dma((4,)),
        whole=pltpu.VMEM((n, 4 * lr, KW), BF16), attn_all=pltpu.VMEM((n, 4 * lr, C), BF16),
        smalls=pltpu.VMEM((n, 16, 128), F32), counts=pltpu.VMEM((dp, 8, 128), F32),
        near_send=dma((chunks, n - 1)), near_recv=dma((chunks, n - 1)),
        x_send=dma((chunks, n - 1)), x_recv=dma((chunks, n - 1)),
        core_send=dma((2, chunks, n - 1)), core_recv=dma((2, chunks, n - 1)),
        small_send=dma((n - 1,)), small_recv=dma((n - 1,)), count_send=dma((dp - 1,)), count_recv=dma((dp - 1,)),
        order=pltpu.VMEM((HALF, HALF), BF16), temb_act=pltpu.VMEM((16, TEMB), BF16),
        own_rows=pltpu.VMEM((32, 128), F32), in_scr=pltpu.VMEM((128, 128), F32),
        out_scr=pltpu.VMEM((16, HALF), F32), out_taps=pltpu.VMEM((72, C), F32),
        vec=pltpu.VMEM((32, C), F32), w_in_all=pltpu.VMEM((32, C), F32),
        hidden=pltpu.VMEM((2, rows_all, C), F32), xhat=pltpu.VMEM((6, rows_all, C), F32),
        dact=pltpu.VMEM((6, rows_all, C), F32), rstd=pltpu.VMEM((-(-6 * images // 8) * 8, C), F32),
        col0=pltpu.VMEM((rows_all, KW), BF16), col1=pltpu.VMEM((rows_all, KW), BF16),
        col2=pltpu.VMEM((rows_all, KW), BF16), col3=pltpu.VMEM((rows_all, KW), BF16),
        taps0=pltpu.VMEM((32, rows_all), BF16), rows_scr=pltpu.VMEM((32, rows_all), F32),
        acts=pltpu.VMEM((2, rows_all, C), BF16), q_scr=pltpu.VMEM((rows_all, C), BF16),
        k_scr=pltpu.VMEM((rows_all, C), BF16), v_scr=pltpu.VMEM((rows_all, C), BF16),
        probs=pltpu.VMEM((images, PIX, PIX), F32), mixed=pltpu.VMEM((rows_all, C), BF16),
        gvec=pltpu.VMEM((32, C), F32), gsum=pltpu.VMEM((16, C), F32),
        local=pltpu.VMEM((2, 4 * lr, MAIN), BF16), one=pltpu.VMEM((4 * lr, MAIN), BF16),
        two=pltpu.VMEM((nx, 4 * lr, MAIN), BF16), last=pltpu.VMEM((2, 4 * lr, MAIN), BF16),
        out_local=pltpu.VMEM((2, 8, HALF), F32), out_one=pltpu.VMEM((8, HALF), F32),
        out_two=pltpu.VMEM((nx, 8, HALF), F32), out_last=pltpu.VMEM((2, 8, HALF), F32),
        one_send=dma((chunks + 2,)), one_recv=dma((chunks + 2,)),
        two_send=dma((chunks + 2, wide)), two_recv=dma((chunks + 2, wide)),
        three_send=dma((chunks + 2,)), three_recv=dma((chunks + 2,)),
        tiny=pltpu.VMEM((dp, 16, 128), F32), tiny_send=dma((dp - 1,)), tiny_recv=dma((dp - 1,)),
        tables=pltpu.VMEM((n, SUM_ROWS, 128), F32), sum_send=dma((n - 1,)), sum_recv=dma((n - 1,)),
    )
    scratch.update({name: pltpu.VMEM(dims, F32) for name, dims in made.items()})
    scratch["out_sem"] = dma((40,))
    names = inputs + [name + "_hbm" for name in made] + list(scratch)
    results = pl.pallas_call(
        functools.partial(step_kernel, n, ny, nz, nx, dp, lr, images, names),
        out_shape=tuple(shape(dims) for dims in made.values()),
        in_specs=[smem_spec()] * 3 + [hbm_spec()] * (2 + len(STATE)),
        out_specs=tuple(hbm_spec() for _ in made),
        scratch_shapes=list(scratch.values()),
        compiler_params=pltpu.CompilerParams(
            collective_id=1, has_side_effects=True, vmem_limit_bytes=64 * MIB
        ),
        name="step",
    )(crop_boxes, time_steps, step_count, canvas, noise_field, *state)
    results = dict(zip(made, results))

    outs = {"norms_out": shape((2, 12)), "loss_out": shape((1, 1))}
    for name in PASSED:
        outs[name + "_out"] = shape(made[name])
    for key in ("in", CONV, TMB, ATTN, "out"):
        outs[key + "_new_out"] = shape(made[key + "_update"])
    for key in (CONV, TMB, ATTN):
        outs[key + "_low_out"] = shape(made[key + "_update"], BF16)
    held = {name + HERE: pltpu.VMEM(own[name].shape, F32) for name in WEIGHTS}
    held.update({name + HERE: pltpu.VMEM(made[name], F32) for name in UPDATES + PASSED})
    held["norms_here"] = pltpu.VMEM((2, 12), F32)
    held["norms_in"] = pltpu.VMEM((SUM_ROWS, 128), F32)
    for key in ("in", CONV, TMB, ATTN, "out"):
        held[key + HERE] = pltpu.VMEM(made[key + "_update"], F32)
    for key in (CONV, TMB, ATTN):
        held[key + "_low_here"] = pltpu.VMEM(made[key + "_update"], BF16)
    held["sem"] = dma((80,))
    inputs = ["norms"] + list(WEIGHTS) + list(UPDATES) + list(PASSED)
    names = inputs + list(outs) + list(held)
    updated = pl.pallas_call(
        functools.partial(update_kernel, names),
        out_shape=tuple(outs.values()),
        in_specs=[hbm_spec()] * len(inputs),
        out_specs=tuple(vmem_spec() if name == "loss_out" else hbm_spec() for name in outs),
        scratch_shapes=list(held.values()),
        compiler_params=pltpu.CompilerParams(vmem_limit_bytes=64 * MIB),
        name="update",
    )(results["norms"], *[own[name] for name in WEIGHTS], *[results[name] for name in UPDATES + PASSED])
    done = dict(zip(outs, updated))
    final = [done["loss_out"].reshape(()), done["norms_out"].T]
    for key in ("in", CONV, TMB, ATTN, "out"):
        final += [done[key + "_new_out"], done[key + "_first_out"], done[key + "_second_out"]]
        if key + "_low_out" in done:
            final.append(done[key + "_low_out"])
    final += [done["vec_new_out"], done["vec_first_out"], done["vec_second_out"], done["attn_grad_out"]]
    return tuple(final)


def solution(mesh):
    chan_row = P("chan", None)
    chan_mid = P(None, "chan", None)
    chan_vec = P(None, "chan")
    return jax.shard_map(
        functools.partial(per_device, mesh.shape["chan"], mesh.shape["dp"]),
        mesh=mesh,
        in_specs=(P("dp", None, None, None), P("dp", None), P("dp"), P(None, "dp", None), P())
        + (chan_row,) * 3 + (chan_mid,) * 9 + (P(),) * 3 + (chan_vec,) * 3,
        out_specs=(P(), P()) + (chan_row,) * 3 + (chan_mid,) * 12 + (P(),) * 3 + (chan_vec,) * 3 + (chan_mid,),
        check_vma=False,
    )
```

```python
import functools
import math

import jax
import jax.numpy as jnp
from jax import lax
from jax.experimental import pallas as pl
from jax.experimental.pallas import tpu as pltpu
from jax.sharding import PartitionSpec as P

TEMB = 512
HW = 16
PIX = HW * HW
GSIZE = 8
C = 256
TAPS = 9
KW = C * TAPS
HALF = 128 * TAPS

NORM_EPS = 1e-05
BETA_ONE = 0.9
BETA_TWO = 0.95
ADAM_EPS = 1e-06
DECAY = 0.01
RATE = 0.3
F32 = jnp.float32
BF16 = jnp.bfloat16
HIGH = lax.Precision.HIGHEST
MESH = pl.DeviceIdType.MESH
NN = (((1,), (0,)), ((), ()))
NT = (((1,), (1,)), ((), ()))
TN = (((0,), (0,)), ((), ()))
MIB = 1024 * 1024

GROWS = 32
XBIG = 4
XLAST = 2
XTAIL = 1
LEAD = 1
EARLY = 2
IMAGE = 3
LAG_B = 1
LAG_Z = 1.0
LAG_X = 1
LAG_Y = 1
DELAYS = (2, 7, 2)
VEC_ROWS = 22
LOSS_ROW = 24
MAIN = HALF + 128 + 128
SUM_ROWS = 16
CONV, TMB, ATTN = tuple(dict(conv=0, temb=0, attn=0))
HERE, W_IN = tuple(dict(_here=0, w_in=0))
LOG_TEN_THOUSAND = math.log(10000.0)


def dot(a, b, dims, precision=None):
    return lax.dot_general(a, b, dims, precision=precision, preferred_element_type=F32)


def iota(shape, axis):
    return lax.broadcasted_iota(jnp.int32, shape, axis)


def tap_order():
    wanted = (iota((1, HALF), 1) & 127) * TAPS + (iota((1, HALF), 1) >> 7)
    return jnp.where(iota((HALF, 1), 0) == wanted, 1.0, 0.0).astype(BF16)


def flip(value, mask):
    bit = 1
    while bit <= mask:
        if mask & bit:
            value = value + bit * (1 - 2 * ((value // bit) % 2))
        bit *= 2
    return value


def remote(src, dst, send_sem, recv_sem, target):
    return pltpu.make_async_remote_copy(
        src_ref=src, dst_ref=dst, send_sem=send_sem, recv_sem=recv_sem,
        device_id=target, device_id_type=MESH,
    )


def row_sum(value):
    return jnp.sum(value, axis=0, keepdims=True)


def group_mean(row):
    row = jnp.broadcast_to(row, (8, C))
    lane = iota(row.shape, 1)
    step = 1
    while step < GSIZE:
        up = pltpu.roll(row, C - step, 1)
        down = pltpu.roll(row, step, 1)
        row = row + jnp.where((lane & step) == 0, up, down)
        step *= 2
    return row[0:1] * (1.0 / (GSIZE * PIX))


def squares(value):
    return jnp.sum(jnp.sum(value * value, axis=1, keepdims=True), axis=0, keepdims=True)


def matrix_parts(lr):
    parts = []
    for k in range(4):
        for h in range(2):
            parts.append((1 + k, CONV, k, slice(h * HALF, (h + 1) * HALF), h,
                          slice(k * lr, (k + 1) * lr), slice(0, HALF)))
    for k in range(2):
        for j in range(4):
            top = (j % 2) * 2 * lr + k * lr
            parts.append((5 + k, TMB, k, slice(j * 128, (j + 1) * 128), j // 2,
                          slice(top, top + lr), slice(HALF + 128, MAIN)))
    for k in range(4):
        for h in range(2):
            parts.append((7 + k, ATTN, k, slice(h * 128, (h + 1) * 128), h,
                          slice(k * lr, (k + 1) * lr), slice(HALF, HALF + 128)))
    return parts


STATE = tuple(dict(
    w_in=0, m_in=0, v_in=0, conv_w=0, conv_m=0, conv_v=0, temb_w=0, temb_m=0, temb_v=0, attn_w=0, attn_m=0,
    attn_v=0, out_w=0, out_m=0, out_v=0, vectors=0, vec_m=0, vec_v=0,
))
PASSED = tuple(dict(
    in_first=0, in_second=0, conv_first=0, conv_second=0, temb_first=0, temb_second=0, attn_first=0,
    attn_second=0, out_first=0, out_second=0, vec_new=0, vec_first=0, vec_second=0, attn_grad=0,
))
UPDATES = tuple(dict(
    in_update=0, conv_update=0, temb_update=0, attn_update=0, out_update=0,
))
WEIGHTS = tuple(dict(
    w_in=0, conv_w=0, temb_w=0, attn_w=0, out_w=0,
))


class Names:
    def __init__(self, names, refs):
        assert len(names) == len(refs)
        self.__dict__.update(zip(names, refs))


def step_kernel(n, ny, nz, nx, dp, lr, images, names, *refs):
    r = Names(names, refs)
    rows_all = images * PIX
    scale = C ** -0.5
    me = lax.axis_index("chan")
    part = lax.axis_index("dp")
    z, y = me // ny, me % ny
    x, core = part // 2, part % 2
    sibling = (x * 2 + 1 - core, me)

    loads = {}

    def load(i, name):
        src, dst = getattr(r, name + "_hbm"), getattr(r, name)
        loads[name] = pltpu.make_async_copy(src, dst, r.load_sem.at[i])
        loads[name].start()

    for k in range(4):
        loads[k] = pltpu.make_async_copy(r.conv_w_hbm.at[k], r.conv_w.at[k], r.conv_sem.at[k])
        loads[k].start()
    for name in ("vectors", W_IN, "temb_w", "attn_w", "out_w"):
        load(STATE.index(name), name)
    for i, name in enumerate(("canvas", "noise")):
        load(len(STATE) + i, name)
    for i, name in enumerate(STATE):
        if name not in loads and name != "conv_w":
            load(i, name)

    offsets = [(i, j) for i in range(nz) for j in range(ny)][1:]
    place = {o: i for i, o in enumerate(offsets)}

    line = False
    inner = ((z + 1) // 2) % 2

    def z_at(i):
        if line and i >= 2:
            return inner * flip(z, 5 - i) + (1 - inner) * flip(z, i)
        return flip(z, i)

    def chan_at(o):
        return z_at(o[0]) * ny + flip(y, o[1])

    def pair_at(o):
        return flip(z, o[0]) * ny + flip(y, o[1])

    def next_part(k):
        return lax.rem(part + k, dp)

    barrier = pltpu.get_barrier_semaphore()
    for o in offsets:
        pl.semaphore_signal(barrier, inc=1, device_id=(part, chan_at(o)), device_id_type=MESH)
    for k in range(1, dp):
        pl.semaphore_signal(barrier, inc=1, device_id=(next_part(k), me), device_id_type=MESH)

    core_lanes = KW // 2
    use_x = nx == 2
    sum_rows = max(lr, 16)
    sum_chunks = 4 * lr // sum_rows
    gather_rows = min(GROWS, sum_rows)
    conv_chunks = 4 * lr // gather_rows
    chunks = list(range(conv_chunks))
    chunks.insert((conv_chunks + 1) // 2, None)

    def x_lanes(chunk):
        return (XLAST if chunk >= conv_chunks - XTAIL else XBIG) * 128 if use_x else 0

    def rows_of(chunk):
        return pl.ds(chunk * gather_rows, gather_rows)

    attn_x = lr // 2 if use_x and lr >= 32 else 0

    def near_ref(chunk, src, c):
        if chunk is None:
            start = c * 2 * lr + x * attn_x if attn_x else c * 2 * lr
            return r.attn_all.at[src, pl.ds(pl.multiple_of(start, 16), 2 * lr - attn_x), :]
        wide = x_lanes(chunk)
        start = c * core_lanes + x * wide if wide else c * core_lanes
        return r.whole.at[src, rows_of(chunk), pl.ds(pl.multiple_of(start, 128), core_lanes - wide)]

    def x_ref(chunk, src, c, side):
        if chunk is None:
            start = c * 2 * lr + side * (2 * lr - attn_x)
            return r.attn_all.at[src, pl.ds(pl.multiple_of(start, 16), attn_x), :]
        wide = x_lanes(chunk)
        start = c * core_lanes + side * (core_lanes - wide)
        return r.whole.at[src, rows_of(chunk), pl.ds(pl.multiple_of(start, 128), wide)]

    def has_x(chunk):
        return attn_x > 0 if chunk is None else x_lanes(chunk) > 0

    sends = []

    def send(*args):
        copy = remote(*args)
        copy.start()
        sends.append(copy)

    def index(chunk):
        return conv_chunks if chunk is None else chunk

    def send_near(chunk, src, o, target):
        i = index(chunk)
        ref = near_ref(chunk, src, core)
        send(ref, ref, r.near_send.at[i, place[o]], r.near_recv.at[i, place[o]], target)

    def send_core(chunk, src, o, piece):
        i = index(chunk)
        ref = near_ref(chunk, src, core) if piece == 0 else x_ref(chunk, src, core, 1 - x)
        send(ref, ref, r.core_send.at[piece, i, place[o]], r.core_recv.at[piece, i, place[o]], sibling)

    def pass_on(chunk, src, slot, target):
        i = index(chunk)

        @pl.when(inner == 1)
        def _():
            ref = near_ref(chunk, src, core)
            remote(ref, ref, r.pass_send.at[i, slot[0]], r.near_recv.at[i, place[(slot[1], 0)]], (part, target)).start()

    def passed(chunk):
        i = index(chunk)

        @pl.when(inner == 1)
        def _():
            for slot in range(4):
                ref = near_ref(chunk, me, core)
                remote(ref, ref, r.pass_send.at[i, slot], r.near_recv.at[i, 0], (part, me)).wait_send()

    def begin_y(chunk):
        for j in range(1, ny):
            send_near(chunk, me, (0, j), (part, chan_at((0, j))))

    def begin(chunk):
        send_near(chunk, me, (1, 0), (part, chan_at((1, 0))))
        if line:
            pass_on(chunk, me, (0, 2), flip(z, 3) * ny + y)
        else:
            for i in range(2, nz):
                send_near(chunk, me, (i, 0), (part, chan_at((i, 0))))

    def near_in(chunk, o):
        i = index(chunk)
        src = chan_at(o)
        ref = near_ref(chunk, src, core)
        remote(ref, ref, r.near_send.at[i, place[o]], r.near_recv.at[i, place[o]], (part, src)).wait_recv()
        if line and o[1] == 0:
            if o[0] == 1:
                pass_on(chunk, src, (1, 3), flip(z, 3) * ny + y)
            else:
                pass_on(chunk, src, o[:1] * 2, flip(z, 1) * ny + y)
        if o[1] == 0:
            for j in range(1, ny):
                send_near(chunk, src, (o[0], j), (part, chan_at((0, j))))
        if has_x(chunk):
            ref = x_ref(chunk, src, core, x)
            send(ref, ref, r.x_send.at[i, place[o]], r.x_recv.at[i, place[o]], ((1 - x) * 2 + core, me))
        send_core(chunk, src, o, 0)

    def x_in(chunk, o):
        if has_x(chunk):
            i = index(chunk)
            src = chan_at(o)
            ref = x_ref(chunk, src, core, 1 - x)
            remote(ref, ref, r.x_send.at[i, place[o]], r.x_recv.at[i, place[o]], ((1 - x) * 2 + core, me)).wait_recv()
            send_core(chunk, src, o, 1)

    def core_in(chunk, o):
        i = index(chunk)
        src = chan_at(o)
        pieces = [near_ref(chunk, src, 1 - core)]
        if has_x(chunk):
            pieces.append(x_ref(chunk, src, 1 - core, 1 - x))
        for piece, ref in enumerate(pieces):
            remote(ref, ref, r.core_send.at[piece, i, place[o]], r.core_recv.at[piece, i, place[o]], sibling).wait_recv()

    events = []
    for c, chunk in enumerate(chunks):
        if c >= 1:
            events.append((c - LEAD, -1, begin, (chunk,)))
        for i in range(1, nz):
            seen = c + LAG_B + i / (nz - 1) - 0.3
            events.append((seen, c, near_in, (chunk, (i, 0))))
            events.append((seen + LAG_X, c, x_in, (chunk, (i, 0))))
            for j in range(1, ny):
                events.append((seen + LAG_Y, c, near_in, (chunk, (i, j))))
                events.append((seen + LAG_Y + LAG_X, c, x_in, (chunk, (i, j))))
        for j in range(1, ny):
            events.append((LAG_B + c * 0.7, c, near_in, (chunk, (0, j))))
            events.append((LAG_B + c * 0.7 + LAG_X, c, x_in, (chunk, (0, j))))
    events.sort(key=lambda event: event[0])
    here = set()

    def until(time):
        while events and events[0][0] <= time:
            event = events.pop(0)
            event[2](*event[3])

    def arrived(*wanted):
        for chunk in wanted:
            if chunk not in here:
                here.add(chunk)
                until(max([event[0] for event in events if event[1] == chunks.index(chunk)], default=0))
                for o in offsets:
                    core_in(chunk, o)

    def conv_here(k):
        arrived(*range(k * lr // gather_rows, ((k + 1) * lr - 1) // gather_rows + 1))

    order = tap_order()
    r.order[...] = order

    def prepare(convs, extra=None):
        stack = []
        for k in convs:
            loads[k].wait()
            weight = r.conv_w[k].astype(BF16)
            stack += [weight[:, :HALF], weight[:, HALF:]]
        if extra is not None:
            stack.append(extra)
        mixed = dot(jnp.concatenate(stack, axis=0), r.order[...], NN)
        for i, k in enumerate(convs):
            for tap in range(TAPS):
                for h in range(2):
                    lanes = slice(tap * C + h * 128, tap * C + h * 128 + 128)
                    top = (2 * i + h) * lr
                    r.whole[me, k * lr:(k + 1) * lr, lanes] = mixed[top:top + lr, tap * 128:(tap + 1) * 128].astype(BF16)
        return mixed[2 * len(convs) * lr:]

    steps_row = iota((16, C), 0)
    steps_all = jnp.zeros((16, C), F32)
    for b in range(images):
        steps_all = jnp.where(steps_row == b, r.steps[b].astype(F32), steps_all)
    frequency = jnp.exp(-LOG_TEN_THOUSAND * iota((1, C), 1).astype(F32) / (TEMB // 2))
    angles = steps_all * frequency
    for i, wave in enumerate((jnp.sin(angles), jnp.cos(angles))):
        wave = jnp.where(steps_row < images, wave / (1.0 + jnp.exp(-wave)), 0.0)
        r.temb_act[:, i * C:(i + 1) * C] = wave.astype(BF16)

    prepare((0, 1))
    pl.semaphore_wait(barrier, n + dp - 2)
    begin(chunks[0])
    half = [chunk for chunk in chunks[:len(chunks) // 2] if chunk is not None]
    for chunk in half:
        begin_y(chunk)

    loads["vectors"].wait()
    loads[W_IN].wait()
    loads["temb_w"].wait()
    r.own_rows[...] = jnp.zeros_like(r.own_rows)
    r.own_rows[0:VEC_ROWS, 0:lr] = r.vectors[...]
    for block in range(2):
        shift = dot(r.temb_act[...], r.temb_w[block].astype(BF16), NT)
        for b in range(images):
            row = VEC_ROWS + block * images + b
            r.own_rows[row:row + 1, 0:lr] = (
                shift[b:b + 1, :] + r.vectors[17 + block:18 + block, :]
            ) + r.vectors[13 + 2 * block:14 + 2 * block, :]
    r.in_scr[...] = jnp.zeros_like(r.in_scr)
    r.in_scr[0:lr, 0:27] = r.w_in[...]
    turned = r.in_scr[...].T
    packed = [jnp.zeros((8, 128), F32), jnp.zeros((8, 128), F32)]
    for g in range(4):
        for i, rows in enumerate((r.own_rows[g * 8:g * 8 + 8, :], turned[g * 8:g * 8 + 8, :])):
            packed[i] += rows if g == 0 else pltpu.roll(rows, g * lr, 1)
    r.smalls[me, 0:8, :] = packed[0]
    r.smalls[me, 8:16, :] = packed[1]
    total = jnp.int32(0)
    for b in range(images):
        side = jnp.minimum(jnp.maximum(r.crop[b, 2], 0), HW)
        total += 3 * side * side
    r.counts[part] = jnp.full((8, 128), total, jnp.int32).astype(F32)
    for o in offsets:
        i = place[o]
        send(r.smalls.at[me], r.smalls.at[me], r.small_send.at[i], r.small_recv.at[i], (part, pair_at(o)))
    for i in range(1, dp):
        send(r.counts.at[part], r.counts.at[part], r.count_send.at[i - 1], r.count_recv.at[i - 1], (next_part(i), me))

    loads["attn_w"].wait()
    for k in range(4):
        r.attn_all[me, k * lr:(k + 1) * lr, :] = r.attn_w[k].astype(BF16)
    loads["out_w"].wait()
    r.out_scr[...] = jnp.zeros_like(r.out_scr)
    for h in range(2):
        r.out_scr[h * 8:h * 8 + 3, :] = r.out_w[:, h * HALF:(h + 1) * HALF]
    out_mixed = prepare((2, 3), r.out_scr[...].astype(BF16))
    for tap in range(TAPS):
        for h in range(2):
            r.out_taps[tap * 8:tap * 8 + 8, h * 128:(h + 1) * 128] = out_mixed[
                h * 8:h * 8 + 8, tap * 128:(tap + 1) * 128
            ]
    for chunk in chunks:
        if chunk not in half:
            begin_y(chunk)
    until(EARLY)

    lane = iota((1, PIX), 1)
    pix_x, pix_y = lane & (HW - 1), lane >> 4
    size = r.canvas.shape[2]
    loads["canvas"].wait()
    loads["noise"].wait()
    noise_rows, mask_rows, noisy_rows = [], [], []
    for b in range(images):
        phase = (jnp.broadcast_to(r.steps[b].astype(F32), (1, PIX)) / 1000.0 + 0.008) / 1.008
        alpha_bar = jnp.cos(phase * (math.pi / 2)) ** 2
        pick = jnp.where(iota((size, PIX), 0) == r.crop[b, 1] + pix_x, 1.0, 0.0)
        flat = r.canvas[b].reshape(3 * size, size)
        spread = dot(flat, pick, NN, HIGH).reshape(3, size, PIX)
        chosen = iota((size, PIX), 0) == r.crop[b, 0] + pix_y
        clean = jnp.sum(jnp.where(chosen[None], spread, 0.0), axis=1)
        noise_b = r.noise[:, b, :]
        noisy_rows.append(jnp.sqrt(alpha_bar) * clean + jnp.sqrt(1.0 - alpha_bar) * noise_b)
        noise_rows.append(noise_b)
        side = r.crop[b, 2]
        mask_rows.append(jnp.where((pix_x < side) & (pix_y < side), 1.0, 0.0))
    zeros5 = jnp.zeros((5, rows_all), F32)
    noisy = jnp.concatenate([jnp.concatenate(noisy_rows, axis=1), zeros5], axis=0)
    noise_all = jnp.concatenate([jnp.concatenate(noise_rows, axis=1), zeros5], axis=0)
    mask_all = jnp.concatenate(mask_rows, axis=1)

    lane_all = iota((8, rows_all), 1)
    px, py = lane_all & (HW - 1), (lane_all >> 4) & (HW - 1)

    def tap_shift(field, tap):
        dy, dx = tap // 3 - 1, tap % 3 - 1
        move = -(dy * HW + dx) % rows_all
        out = pltpu.roll(field, move, 1) if move else field
        inside = (px + dx >= 0) & (px + dx < HW) & (py + dy >= 0) & (py + dy < HW)
        return jnp.where(inside, out, 0.0)

    noisy = noisy.astype(BF16).astype(F32)
    r.rows_scr[...] = jnp.zeros_like(r.rows_scr)
    for tap in range(TAPS):
        moved = tap_shift(noisy, tap)
        for colour in range(3):
            r.rows_scr[colour * TAPS + tap:colour * TAPS + tap + 1, :] = moved[colour:colour + 1]
    r.taps0[...] = r.rows_scr[...].astype(BF16)

    until(IMAGE)

    for o in offsets:
        src = pair_at(o)
        remote(r.smalls.at[src], r.smalls.at[src], r.small_send.at[place[o]], r.small_recv.at[place[o]],
               (part, src)).wait_recv()
    for i in range(1, dp):
        p = lax.rem(part - i + dp, dp)
        remote(r.counts.at[p], r.counts.at[p], r.count_send.at[i - 1], r.count_recv.at[i - 1], (p, me)).wait_recv()
    lane_wide = iota((16, C), 1)
    unpacked = [jnp.zeros((16, C), F32) for g in range(4)]
    for j in range(n):
        block = jnp.concatenate([r.smalls[j], jnp.zeros((16, 128), F32)], axis=1)
        for g in range(4):
            piece = jnp.where((lane_wide >= g * lr) & (lane_wide < (g + 1) * lr), block, 0.0)
            move = (j - g) * lr % C
            unpacked[g] += pltpu.roll(piece, move, 1) if move else piece
    for g in range(4):
        r.vec[g * 8:g * 8 + 8, :] = unpacked[g][0:8]
        r.w_in_all[g * 8:g * 8 + 8, :] = unpacked[g][8:16]
    total = r.counts[0, 0:1, 0:1]
    for k in range(1, dp):
        total = total + r.counts[k, 0:1, 0:1]

    def vrow(i):
        return r.vec[i:i + 1, :]

    def span(b):
        return slice(b * PIX, (b + 1) * PIX)

    def conv_weight(k):
        return r.whole[:, k * lr:(k + 1) * lr, :].reshape(C, KW)

    def attn_weight(k):
        return r.attn_all[:, k * lr:(k + 1) * lr, :].reshape(C, C)

    col_x = iota((PIX, C), 0) & (HW - 1)
    blank = jnp.zeros((HW, C), BF16)
    hidden, xhat, dact, rstd, acts = r.hidden, r.xhat, r.dact, r.rstd, r.acts
    cols = (r.col0, r.col1, r.col2, r.col3)

    def norm_fwd(i, value, gain, shift, store):
        for b in range(images):
            image = value[span(b)]
            centred = image - group_mean(row_sum(image))
            inv = lax.rsqrt(group_mean(row_sum(centred * centred)) + NORM_EPS)
            normed = centred * inv
            scaled = normed * gain + shift
            gate = 0.5 * jnp.tanh(0.5 * scaled) + 0.5
            act = scaled * gate
            xhat[i, span(b), :] = normed
            dact[i, span(b), :] = gate + act * (1.0 - gate)
            rstd[i * images + b:i * images + b + 1, :] = inv
            store(b, act)

    def store_cols(ref, b, act):
        left = jnp.where(col_x > 0, pltpu.roll(act, 1, 0), 0.0)
        right = jnp.where(col_x < HW - 1, pltpu.roll(act, PIX - 1, 0), 0.0)
        for dx, moved in enumerate((left, act, right)):
            low = moved.astype(BF16)
            for dy in range(3):
                lanes = slice((3 * dy + dx) * C, (3 * dy + dx + 1) * C)
                base = b * PIX
                if dy == 0:
                    ref[base:base + HW, lanes] = blank
                    ref[base + HW:base + PIX, lanes] = low[:PIX - HW]
                elif dy == 1:
                    ref[base:base + PIX, lanes] = low
                else:
                    ref[base:base + PIX - HW, lanes] = low[HW:]
                    ref[base + PIX - HW:base + PIX, lanes] = blank

    def add_rows(value, first):
        return jnp.concatenate([value[span(b)] + vrow(first + b) for b in range(images)], axis=0)

    def chunk_of(k):
        return k * lr // sum_rows

    def block_fwd(block, source, target):
        norm_fwd(3 * block, hidden[source], vrow(3 * block), vrow(6 + 3 * block),
                 functools.partial(store_cols, cols[2 * block]))
        conv_here(2 * block)
        middle = dot(cols[2 * block][...], conv_weight(2 * block), NT)
        middle = add_rows(middle, VEC_ROWS + block * images)
        norm_fwd(3 * block + 1, middle, vrow(3 * block + 1), vrow(7 + 3 * block),
                 functools.partial(store_cols, cols[2 * block + 1]))
        conv_here(2 * block + 1)
        branch = dot(cols[2 * block + 1][...], conv_weight(2 * block + 1), NT)
        hidden[target] = hidden[source] + (branch + vrow(14 + 2 * block))

    def store_act(i):
        def store(b, act):
            acts[i, span(b), :] = act.astype(BF16)
        return store

    hidden[0] = dot(r.taps0[...], r.w_in_all[...].astype(BF16), TN) + vrow(12)
    block_fwd(0, 0, 1)

    norm_fwd(2, hidden[1], vrow(2), vrow(8), store_act(0))
    arrived(None)
    r.q_scr[...] = (dot(acts[0], attn_weight(0), NT) + vrow(19)).astype(BF16)
    r.k_scr[...] = dot(acts[0], attn_weight(1), NT).astype(BF16)
    r.v_scr[...] = (dot(acts[0], attn_weight(2), NT) + vrow(20)).astype(BF16)
    for b in range(images):
        scores = dot(r.q_scr[span(b), :], r.k_scr[span(b), :], NT) * scale
        raised = jnp.exp(scores - jnp.max(scores, axis=1, keepdims=True))
        soft = raised / jnp.sum(raised, axis=1, keepdims=True)
        r.probs[b] = soft
        r.mixed[span(b), :] = dot(soft.astype(BF16), r.v_scr[span(b), :], NN).astype(BF16)
    hidden[0] = hidden[1] + (dot(r.mixed[...], attn_weight(3), NT) + vrow(21))

    block_fwd(1, 0, 1)
    norm_fwd(5, hidden[1], vrow(5), vrow(11), store_act(1))

    out_low = r.out_taps[...].astype(BF16)
    fanned = dot(out_low, acts[1], NT)
    pred = jnp.zeros((8, rows_all), F32)
    for tap in range(TAPS):
        pred += tap_shift(fanned[tap * 8:tap * 8 + 8], tap)
    error = pred - noise_all
    masked = mask_all * error
    inverse = 1.0 / total
    loss = jnp.sum(jnp.sum(masked * error, axis=1, keepdims=True), axis=0, keepdims=True) * inverse
    grad_pred = (2.0 * masked * inverse).astype(BF16).astype(F32)
    spread_pred = jnp.concatenate(
        [tap_shift(grad_pred, TAPS - 1 - tap) for tap in range(TAPS)], axis=0
    ).astype(BF16)
    out_grad = dot(spread_pred, acts[1], NN)

    lanes_attn, lanes_temb = slice(HALF, HALF + 128), slice(HALF + 128, MAIN)

    def region(chunk):
        if chunk == ATTN:
            return slice(0, 4 * lr), lanes_attn
        if chunk == TMB:
            return slice(0, 4 * lr), lanes_temb
        return slice(chunk * sum_rows, (chunk + 1) * sum_rows), slice(0, HALF)

    def family(chunk):
        if chunk == "out":
            return (r.out_local, r.out_one, r.out_two, r.out_last), (slice(None), slice(None)), sum_chunks + 2
        i = sum_chunks + (ATTN, TMB).index(chunk) if isinstance(chunk, str) else chunk
        return (r.local, r.one, r.two, r.last), region(chunk), i

    def view(ref, i, where):
        return ref.at[(i,) + where]

    def reduce_one(chunk):
        (local, one, two, last), where, i = family(chunk)
        send(view(local, 1 - core, where), one.at[where], r.one_send.at[i], r.one_recv.at[i], sibling)

    def reduce_two(chunk):
        (local, one, two, last), where, i = family(chunk)
        remote(view(local, 1 - core, where), one.at[where], r.one_send.at[i], r.one_recv.at[i], sibling).wait_recv()
        both = local[(core,) + where].astype(F32) + one[where].astype(F32)
        two[(x,) + where] = both.astype(two.dtype)
        for m in range(1, nx):
            ref = view(two, x, where)
            send(ref, ref, r.two_send.at[i, m - 1], r.two_recv.at[i, m - 1], (lax.rem(x + m, nx) * 2 + core, me))

    def reduce_three(chunk):
        (local, one, two, last), where, i = family(chunk)
        for m in range(1, nx):
            sender = lax.rem(x - m + nx, nx)
            ref = view(two, sender, where)
            remote(ref, ref, r.two_send.at[i, m - 1], r.two_recv.at[i, m - 1], (sender * 2 + core, me)).wait_recv()
        summed = two[(0,) + where].astype(F32)
        for m in range(1, nx):
            summed = summed + two[(m,) + where].astype(F32)
        last[(core,) + where] = summed.astype(last.dtype)
        ref = view(last, core, where)
        send(ref, ref, r.three_send.at[i], r.three_recv.at[i], sibling)

    def reduce_four(chunk):
        (local, one, two, last), where, i = family(chunk)
        ref = view(last, 1 - core, where)
        remote(ref, ref, r.three_send.at[i], r.three_recv.at[i], sibling).wait_recv()

    due = []
    clock = [0]

    def run_due(entry):
        delay = {1: DELAYS[0], 2: DELAYS[1], 3: DELAYS[2]}
        stage, chunk = entry
        (reduce_one, reduce_two, reduce_three, reduce_four)[stage - 1](chunk)
        if stage < 4:
            due.append((clock[0] + delay[stage], (stage + 1, chunk)))

    def tick():
        clock[0] += 1
        for item in [item for item in due if item[0] <= clock[0]]:
            due.remove(item)
            run_due(item[1])

    def ready(chunk):
        run_due((1, chunk))

    def finish(chunk=None):
        while True:
            left = [item for item in due if chunk is None or item[1][1] == chunk]
            if not left:
                return
            item = min(left, key=lambda item: (item[1][0], item[0]))
            due.remove(item)
            run_due(item[1])

    for h in range(2):
        for tap in range(TAPS):
            r.out_local[h, :, tap * 128:(tap + 1) * 128] = out_grad[tap * 8:tap * 8 + 8, h * 128:(h + 1) * 128]
    ready("out")
    grad = dot(spread_pred, out_low, TN)

    gvec = r.gvec
    gvec[...] = jnp.zeros_like(gvec)
    pick_own = jnp.where(iota((lr, C), 1) == iota((lr, C), 0) + me * lr, 1.0, 0.0).astype(BF16)
    hole = jnp.zeros((HW, C), F32)

    def own_rows(low):
        return dot(pick_own, low, NT).astype(BF16)

    def norm_back(i, grad, gain_row):
        outs = []
        gain = vrow(gain_row)
        gain_sum = jnp.zeros((1, C), F32)
        shift_sum = jnp.zeros((1, C), F32)
        for b in range(images):
            slope = grad[span(b)] * dact[i, span(b), :]
            normed = xhat[i, span(b), :]
            shift_b = row_sum(slope)
            gain_b = row_sum(slope * normed)
            mean_one = group_mean(shift_b * gain)
            mean_two = group_mean(gain_b * gain)
            inv = rstd[i * images + b:i * images + b + 1, :]
            outs.append(inv * (slope * gain - mean_one - normed * mean_two))
            gain_sum += gain_b
            shift_sum += shift_b
        gvec[gain_row:gain_row + 1, :] = gain_sum
        gvec[6 + gain_row:7 + gain_row, :] = shift_sum
        return jnp.concatenate(outs, axis=0)

    def conv_back(k, low):
        own = dot(own_rows(low), cols[k][...], NN)
        for h in range(2):
            for tap in range(TAPS):
                r.local[h, k * lr:(k + 1) * lr, tap * 128:(tap + 1) * 128] = own[
                    :, tap * C + h * 128:tap * C + h * 128 + 128
                ].astype(BF16)
        if k * lr % sum_rows == 0:
            ready(chunk_of(k))
        tick()
        parts = dot(low, conv_weight(k), NN)
        outs = []
        for b in range(images):
            sides = []
            for dx in range(3):
                up = parts[span(b), dx * C:(dx + 1) * C]
                mid = parts[span(b), (3 + dx) * C:(4 + dx) * C]
                down = parts[span(b), (6 + dx) * C:(7 + dx) * C]
                sides.append(
                    mid
                    + jnp.concatenate([up[HW:], hole], axis=0)
                    + jnp.concatenate([hole, down[:PIX - HW]], axis=0)
                )
            left = pltpu.roll(jnp.where(col_x > 0, sides[0], 0.0), PIX - 1, 0)
            right = pltpu.roll(jnp.where(col_x < HW - 1, sides[2], 0.0), 1, 0)
            outs.append(sides[1] + left + right)
        tick()
        return jnp.concatenate(outs, axis=0)

    def block_back(block, grad):
        gvec[14 + 2 * block:15 + 2 * block, :] = row_sum(grad)
        back = conv_back(2 * block + 1, grad.astype(BF16))
        middle = norm_back(3 * block + 1, back, 3 * block + 1)
        r.gsum[...] = jnp.zeros_like(r.gsum)
        for b in range(images):
            r.gsum[b:b + 1, :] = row_sum(middle[span(b)])
        whole_sum = row_sum(r.gsum[...])
        gvec[13 + 2 * block:14 + 2 * block, :] = whole_sum
        gvec[17 + block:18 + block, :] = whole_sum
        own = dot(pick_own, r.gsum[...].astype(BF16), NT).astype(BF16)
        temb = dot(own, r.temb_act[...], NN)
        for j in range(4):
            top = (j % 2) * 2 * lr + block * lr
            r.local[j // 2, top:top + lr, lanes_temb] = temb[:, j * 128:(j + 1) * 128].astype(BF16)
        if block == 0:
            ready(TMB)
        tick()
        back = conv_back(2 * block, middle.astype(BF16))
        return grad + norm_back(3 * block, back, 3 * block)

    grad = norm_back(5, grad, 5)
    tick()
    grad = block_back(1, grad)
    tick()

    gvec[21:22, :] = row_sum(grad)
    low = grad.astype(BF16)

    def attn_own(k, low, field):
        own = dot(own_rows(low), field, NN)
        for h in range(2):
            r.local[h, k * lr:(k + 1) * lr, lanes_attn] = own[:, h * 128:(h + 1) * 128].astype(BF16)

    attn_own(3, low, r.mixed[...])
    mixed_low = dot(low, attn_weight(3), NN).astype(BF16)
    grads_q, grads_k, grads_v = [], [], []
    for b in range(images):
        image = mixed_low[span(b)]
        soft = r.probs[b]
        grad_soft = dot(image, r.v_scr[span(b), :], NT)
        grads_v.append(dot(soft.astype(BF16), image, TN))
        weighed = soft * grad_soft
        slope = (weighed - soft * jnp.sum(weighed, axis=1, keepdims=True)).astype(BF16)
        grads_q.append(scale * dot(slope, r.k_scr[span(b), :], NN))
        grads_k.append(scale * dot(slope, r.q_scr[span(b), :], TN))
    tick()
    back = jnp.zeros((rows_all, C), F32)
    for i, grads in enumerate((grads_q, grads_k, grads_v)):
        full = jnp.concatenate(grads, axis=0)
        if i != 1:
            gvec[19 + i // 2:20 + i // 2, :] = row_sum(full)
        low = full.astype(BF16)
        attn_own(i, low, acts[0])
        back += dot(low, attn_weight(i), NN)
    ready(ATTN)
    tick()
    grad = grad + norm_back(2, back, 2)
    tick()

    grad = block_back(0, grad)
    tick()
    gvec[12:13, :] = row_sum(grad)
    in_grad = dot(own_rows(grad.astype(BF16)), r.taps0[...], NT)

    own_vec = jnp.where(iota((32, 128), 1) < lr, pltpu.roll(gvec[...], lax.rem(C - me * lr, C), 1)[:, 0:128], 0.0)
    own_vec = jnp.where(iota((32, 128), 0) == LOSS_ROW, loss, own_vec)
    own_vec = jnp.where(iota((32, 128), 1) < lr, own_vec, 0.0)
    packed = [jnp.zeros((8, 128), F32), jnp.zeros((8, 128), F32)]
    for g in range(4):
        rows = own_vec[g * 8:g * 8 + 8, :]
        packed[0] += rows if g == 0 else pltpu.roll(rows, g * lr, 1)
    for g in range(lr // 8):
        rows = jnp.concatenate([in_grad[g * 8:g * 8 + 8, :], jnp.zeros((8, 96), F32)], axis=1)
        packed[1] += rows if g == 0 else pltpu.roll(rows, g * 32, 1)
    r.tiny[part, 0:8, :] = packed[0]
    r.tiny[part, 8:16, :] = packed[1]
    for i in range(1, dp):
        send(r.tiny.at[part], r.tiny.at[part], r.tiny_send.at[i - 1], r.tiny_recv.at[i - 1], (next_part(i), me))
    tick()

    for name in STATE:
        if name in loads and name not in ("vectors", W_IN, "temb_w", "attn_w", "out_w"):
            loads[name].wait()
    count = jnp.broadcast_to(r.count_step[0].astype(F32), (1, 128))
    fix_one = (1.0 / (1.0 - jnp.exp(math.log(BETA_ONE) * count)))[:, 0:1]
    fix_two = (1.0 / (1.0 - jnp.exp(math.log(BETA_TWO) * count)))[:, 0:1]

    def adapt(grad, first, second):
        first_new = BETA_ONE * first + (1.0 - BETA_ONE) * grad
        second_new = BETA_TWO * second + (1.0 - BETA_TWO) * grad * grad
        direction = first_new * fix_one / (jnp.sqrt(second_new * fix_two) + ADAM_EPS)
        return first_new, second_new, direction

    sums = {}

    def lamb(number, name, at, grad):
        names = (W_IN, "m_in", "v_in") if name == "in" else (name + "_w", name + "_m", name + "_v")
        weight, first, second = (getattr(r, each)[at] for each in names)
        first, second, direction = adapt(grad, first, second)
        update = direction + DECAY * weight
        getattr(r, name + "_first")[at] = first
        getattr(r, name + "_second")[at] = second
        getattr(r, name + "_update")[at] = update
        pair = (squares(weight), squares(update))
        if number in sums:
            pair = (sums[number][0] + pair[0], sums[number][1] + pair[1])
        sums[number] = pair

    every = slice(None)
    outward = []

    def put(name, k=None):
        src, dst = getattr(r, name), getattr(r, name + "_hbm")
        if k is not None:
            src, dst = src.at[k], dst.at[k]
        copy = pltpu.make_async_copy(src, dst, r.out_sem.at[len(outward)])
        copy.start()
        outward.append(copy)

    def put_all(name, k=None):
        for kind in ("first", "second", "update"):
            put(name + "_" + kind, k)

    def conv_steps(which, natural):
        for number, name, k, lanes, h, rows, held in matrix_parts(lr):
            if name == CONV and chunk_of(k) in which:
                top = h * len(which) * sum_rows + k * lr - min(which) * sum_rows
                lamb(number, name, (k, every, lanes), natural[top:top + lr])
                if h == 1:
                    put_all(CONV, k)

    def push(chunk, stage):
        for item in [item for item in due if item[1][1] == chunk]:
            while item is not None and item[1][0] <= stage:
                due.remove(item)
                run_due(item[1])
                item = next((left for left in due if left[1][1] == chunk), None)

    def whole_parts(which):
        for number, name, k, lanes, h, rows, held in matrix_parts(lr):
            if name == which:
                value = r.last[h, rows, held].astype(F32)
                if name == ATTN:
                    r.attn_grad[k, :, lanes] = value
                lamb(number, name, (k, every, lanes), value)
        put_all(which)

    early = list(range(1, sum_chunks))
    for chunk in early + ["out"]:
        finish(chunk)
    push(0, 2)
    push(TMB, 2)
    stack = [r.last[h, sum_rows:4 * lr, 0:HALF] for h in range(2)]
    stack += [jnp.concatenate([r.out_last[h], jnp.zeros((8, HALF), F32)], axis=0).astype(BF16) for h in range(2)]
    natural = dot(jnp.concatenate(stack, axis=0), r.order[...], NT)
    finish(ATTN)
    whole_parts(ATTN)
    put("attn_grad")
    push(TMB, 3)
    push(0, 3)
    conv_steps(early, natural)
    top = 2 * (4 * lr - sum_rows)
    for h in range(2):
        lamb(11, "out", (every, slice(h * HALF, (h + 1) * HALF)), natural[top + h * 16:top + h * 16 + 3])
    put_all("out")
    finish(TMB)
    whole_parts(TMB)
    finish()
    natural = dot(jnp.concatenate([r.last[h, 0:sum_rows, 0:HALF] for h in range(2)], axis=0), r.order[...], NT)
    conv_steps([0], natural)

    for i in range(1, dp):
        p = lax.rem(part - i + dp, dp)
        remote(r.tiny.at[p], r.tiny.at[p], r.tiny_send.at[i - 1], r.tiny_recv.at[i - 1], (p, me)).wait_recv()
    tiny = r.tiny[0]
    for k in range(1, dp):
        tiny = tiny + r.tiny[k]
    for g in range(4):
        rows = tiny[0:8] if g == 0 else pltpu.roll(tiny[0:8], 128 - g * lr, 1)
        r.own_rows[g * 8:g * 8 + 8, :] = rows
    for g in range(lr // 8):
        rows = tiny[8:16] if g == 0 else pltpu.roll(tiny[8:16], 128 - g * 32, 1)
        r.in_scr[g * 8:g * 8 + 8, :] = rows
    lamb(0, "in", (every, every), r.in_scr[0:lr, 0:27])
    put_all("in")

    row = iota((SUM_ROWS, 128), 0)
    lane = iota((SUM_ROWS, 128), 1)
    table = jnp.zeros((SUM_ROWS, 128), F32)
    for number in range(11):
        for side in range(2):
            table = jnp.where((row == number) & (lane == side), sums[number][side], table)
    r.tables[me] = table
    for o in offsets:
        i = place[o]
        send(r.tables.at[me], r.tables.at[me], r.sum_send.at[i], r.sum_recv.at[i], (part, pair_at(o)))
    first, second, direction = adapt(r.own_rows[0:VEC_ROWS, 0:lr], r.vec_m[...], r.vec_v[...])
    r.vec_new[...] = r.vectors[...] - RATE * direction
    r.vec_first[...] = first
    r.vec_second[...] = second
    for name in ("vec_new", "vec_first", "vec_second"):
        put(name)
    for o in offsets:
        src = pair_at(o)
        remote(r.tables.at[src], r.tables.at[src], r.sum_send.at[place[o]], r.sum_recv.at[place[o]],
               (part, src)).wait_recv()
    total = r.tables[0]
    for k in range(1, n):
        total = total + r.tables[k]
    for side in range(2):
        total = jnp.where((row == 11) & (lane == side), sums[11][side], total)
    total = jnp.where((row == 12) & (lane == 0), r.own_rows[LOSS_ROW:LOSS_ROW + 1, 0:1], total)
    r.norms[...] = total
    put("norms")
    if line:
        for chunk in chunks:
            passed(chunk)
    for copy in sends:
        copy.wait_send()
    for copy in outward:
        copy.wait()


def update_kernel(names, *refs):
    r = Names(names, refs)
    copies = []

    def copy(src, dst):
        made = pltpu.make_async_copy(src, dst, r.sem.at[len(copies)])
        made.start()
        copies.append(made)
        return made

    copy(r.norms, r.norms_in)
    loads = {}
    for k in range(4):
        loads[(CONV, k)] = [
            copy(getattr(r, name).at[k], getattr(r, name + HERE).at[k]) for name in ("conv_w", "conv_update")
        ]
    for name in ("in", TMB, ATTN, "out"):
        weight = W_IN if name == "in" else name + "_w"
        loads[name] = [copy(getattr(r, each), getattr(r, each + HERE)) for each in (weight, name + "_update")]
    passing = [(name, copy(getattr(r, name), getattr(r, name + HERE))) for name in PASSED]
    copies[0].wait()
    outward = []

    def ratio(number):
        pair = r.norms_in[number:number + 1, 0:2]
        return RATE * jnp.sqrt(pair[:, 0:1] / (pair[:, 1:2] + 1e-06))

    r.norms_here[...] = jnp.sqrt(r.norms_in[...].T[0:2, 0:12])
    outward.append(copy(r.norms_here, r.norms_out))
    r.loss_out[...] = r.norms_in[12:13, 0:1]
    for number, name, k in [(0, "in", None)] + [(1 + k, CONV, k) for k in range(4)] + [
        (5 + k, TMB, k) for k in range(2)
    ] + [(7 + k, ATTN, k) for k in range(4)] + [(11, "out", None)]:
        weight_name = W_IN if name == "in" else name + "_w"
        for wait in loads.pop((name, k) if name == CONV else name, ()):
            wait.wait()
        at = (slice(None), slice(None)) if k is None else (k, slice(None), slice(None))
        here, target = getattr(r, name + HERE), getattr(r, name + "_new_out")
        new = getattr(r, weight_name + HERE)[at] - ratio(number) * getattr(r, name + "_update_here")[at]
        here[at] = new
        last = k in (None, {CONV: k, TMB: 1, ATTN: 3}.get(name))
        if name == CONV:
            outward.append(copy(here.at[k], target.at[k]))
        elif last:
            outward.append(copy(here, target))
        if k is not None:
            low = getattr(r, name + "_low_here")
            low[at] = new.astype(BF16)
            if name == CONV:
                outward.append(copy(low.at[k], getattr(r, name + "_low_out").at[k]))
            elif last:
                outward.append(copy(low, getattr(r, name + "_low_out")))
    for name, made in passing:
        made.wait()
        outward.append(copy(getattr(r, name + HERE), getattr(r, name + "_out")))
    for made in outward:
        made.wait()


def vmem_spec():
    return pl.BlockSpec(memory_space=pltpu.VMEM)


def smem_spec():
    return pl.BlockSpec(memory_space=pltpu.SMEM)


def hbm_spec():
    return pl.BlockSpec(memory_space=pltpu.HBM)


def shape(dims, kind=F32):
    return jax.ShapeDtypeStruct(dims, kind)


def per_device(n, dp, canvas, crop_boxes, time_steps, noise_field, step_count, *state):
    images = canvas.shape[0]
    rows_all = images * PIX
    own = dict(zip(STATE, state))
    lr = own["conv_w"].shape[1]
    nx = dp // 2
    ny = 1 << ((n.bit_length() - 2) // 2)
    nz = n // ny
    dma = pltpu.SemaphoreType.DMA
    chunks = 4 * lr // min(GROWS, max(lr, 16)) + 1

    made = {}
    for key, name in (("in", W_IN), (CONV, "conv_w"), (TMB, "temb_w"), (ATTN, "attn_w"), ("out", "out_w")):
        for kind in ("first", "second", "update"):
            made[key + "_" + kind] = own[name].shape
    for name in ("vec_new", "vec_first", "vec_second"):
        made[name] = own["vectors"].shape
    made["attn_grad"] = own["attn_w"].shape
    made["norms"] = (SUM_ROWS, 128)

    inputs = ["crop", "steps", "count_step", "canvas_hbm", "noise_hbm"] + [name + "_hbm" for name in STATE]
    scratch = {name: pltpu.VMEM(own[name].shape, F32) for name in STATE}
    wide = max(nx - 1, 1)
    scratch.update(
        canvas=pltpu.VMEM(canvas.shape, F32), noise=pltpu.VMEM(noise_field.shape, F32),
        load_sem=dma((len(STATE) + 2,)), conv_sem=dma((4,)),
        whole=pltpu.VMEM((n, 4 * lr, KW), BF16), attn_all=pltpu.VMEM((n, 4 * lr, C), BF16),
        smalls=pltpu.VMEM((n, 16, 128), F32), counts=pltpu.VMEM((dp, 8, 128), F32),
        near_send=dma((chunks, n - 1)), pass_send=dma((chunks, 4)), near_recv=dma((chunks, n - 1)),
        x_send=dma((chunks, n - 1)), x_recv=dma((chunks, n - 1)),
        core_send=dma((2, chunks, n - 1)), core_recv=dma((2, chunks, n - 1)),
        small_send=dma((n - 1,)), small_recv=dma((n - 1,)), count_send=dma((dp - 1,)), count_recv=dma((dp - 1,)),
        order=pltpu.VMEM((HALF, HALF), BF16), temb_act=pltpu.VMEM((16, TEMB), BF16),
        own_rows=pltpu.VMEM((32, 128), F32), in_scr=pltpu.VMEM((128, 128), F32),
        out_scr=pltpu.VMEM((16, HALF), F32), out_taps=pltpu.VMEM((72, C), F32),
        vec=pltpu.VMEM((32, C), F32), w_in_all=pltpu.VMEM((32, C), F32),
        hidden=pltpu.VMEM((2, rows_all, C), F32), xhat=pltpu.VMEM((6, rows_all, C), F32),
        dact=pltpu.VMEM((6, rows_all, C), F32), rstd=pltpu.VMEM((-(-6 * images // 8) * 8, C), F32),
        col0=pltpu.VMEM((rows_all, KW), BF16), col1=pltpu.VMEM((rows_all, KW), BF16),
        col2=pltpu.VMEM((rows_all, KW), BF16), col3=pltpu.VMEM((rows_all, KW), BF16),
        taps0=pltpu.VMEM((32, rows_all), BF16), rows_scr=pltpu.VMEM((32, rows_all), F32),
        acts=pltpu.VMEM((2, rows_all, C), BF16), q_scr=pltpu.VMEM((rows_all, C), BF16),
        k_scr=pltpu.VMEM((rows_all, C), BF16), v_scr=pltpu.VMEM((rows_all, C), BF16),
        probs=pltpu.VMEM((images, PIX, PIX), F32), mixed=pltpu.VMEM((rows_all, C), BF16),
        gvec=pltpu.VMEM((32, C), F32), gsum=pltpu.VMEM((16, C), F32),
        local=pltpu.VMEM((2, 4 * lr, MAIN), BF16), one=pltpu.VMEM((4 * lr, MAIN), BF16),
        two=pltpu.VMEM((nx, 4 * lr, MAIN), BF16), last=pltpu.VMEM((2, 4 * lr, MAIN), BF16),
        out_local=pltpu.VMEM((2, 8, HALF), F32), out_one=pltpu.VMEM((8, HALF), F32),
        out_two=pltpu.VMEM((nx, 8, HALF), F32), out_last=pltpu.VMEM((2, 8, HALF), F32),
        one_send=dma((chunks + 2,)), one_recv=dma((chunks + 2,)),
        two_send=dma((chunks + 2, wide)), two_recv=dma((chunks + 2, wide)),
        three_send=dma((chunks + 2,)), three_recv=dma((chunks + 2,)),
        tiny=pltpu.VMEM((dp, 16, 128), F32), tiny_send=dma((dp - 1,)), tiny_recv=dma((dp - 1,)),
        tables=pltpu.VMEM((n, SUM_ROWS, 128), F32), sum_send=dma((n - 1,)), sum_recv=dma((n - 1,)),
    )
    scratch.update({name: pltpu.VMEM(dims, F32) for name, dims in made.items()})
    scratch["out_sem"] = dma((40,))
    names = inputs + [name + "_hbm" for name in made] + list(scratch)
    results = pl.pallas_call(
        functools.partial(step_kernel, n, ny, nz, nx, dp, lr, images, names),
        out_shape=tuple(shape(dims) for dims in made.values()),
        in_specs=[smem_spec()] * 3 + [hbm_spec()] * (2 + len(STATE)),
        out_specs=tuple(hbm_spec() for _ in made),
        scratch_shapes=list(scratch.values()),
        compiler_params=pltpu.CompilerParams(
            collective_id=1, has_side_effects=True, vmem_limit_bytes=64 * MIB
        ),
        name="step",
    )(crop_boxes, time_steps, step_count, canvas, noise_field, *state)
    results = dict(zip(made, results))

    outs = {"norms_out": shape((2, 12)), "loss_out": shape((1, 1))}
    for name in PASSED:
        outs[name + "_out"] = shape(made[name])
    for key in ("in", CONV, TMB, ATTN, "out"):
        outs[key + "_new_out"] = shape(made[key + "_update"])
    for key in (CONV, TMB, ATTN):
        outs[key + "_low_out"] = shape(made[key + "_update"], BF16)
    held = {name + HERE: pltpu.VMEM(own[name].shape, F32) for name in WEIGHTS}
    held.update({name + HERE: pltpu.VMEM(made[name], F32) for name in UPDATES + PASSED})
    held["norms_here"] = pltpu.VMEM((2, 12), F32)
    held["norms_in"] = pltpu.VMEM((SUM_ROWS, 128), F32)
    for key in ("in", CONV, TMB, ATTN, "out"):
        held[key + HERE] = pltpu.VMEM(made[key + "_update"], F32)
    for key in (CONV, TMB, ATTN):
        held[key + "_low_here"] = pltpu.VMEM(made[key + "_update"], BF16)
    held["sem"] = dma((80,))
    inputs = ["norms"] + list(WEIGHTS) + list(UPDATES) + list(PASSED)
    names = inputs + list(outs) + list(held)
    updated = pl.pallas_call(
        functools.partial(update_kernel, names),
        out_shape=tuple(outs.values()),
        in_specs=[hbm_spec()] * len(inputs),
        out_specs=tuple(vmem_spec() if name == "loss_out" else hbm_spec() for name in outs),
        scratch_shapes=list(held.values()),
        compiler_params=pltpu.CompilerParams(vmem_limit_bytes=64 * MIB),
        name="update",
    )(results["norms"], *[own[name] for name in WEIGHTS], *[results[name] for name in UPDATES + PASSED])
    done = dict(zip(outs, updated))
    final = [done["loss_out"].reshape(()), done["norms_out"].T]
    for key in ("in", CONV, TMB, ATTN, "out"):
        final += [done[key + "_new_out"], done[key + "_first_out"], done[key + "_second_out"]]
        if key + "_low_out" in done:
            final.append(done[key + "_low_out"])
    final += [done["vec_new_out"], done["vec_first_out"], done["vec_second_out"], done["attn_grad_out"]]
    return tuple(final)


def solution(mesh):
    chan_row = P("chan", None)
    chan_mid = P(None, "chan", None)
    chan_vec = P(None, "chan")
    return jax.shard_map(
        functools.partial(per_device, mesh.shape["chan"], mesh.shape["dp"]),
        mesh=mesh,
        in_specs=(P("dp", None, None, None), P("dp", None), P("dp"), P(None, "dp", None), P())
        + (chan_row,) * 3 + (chan_mid,) * 9 + (P(),) * 3 + (chan_vec,) * 3,
        out_specs=(P(), P()) + (chan_row,) * 3 + (chan_mid,) * 12 + (P(),) * 3 + (chan_vec,) * 3 + (chan_mid,),
        check_vma=False,
    )
```

```python
import functools
import math

import jax
import jax.numpy as jnp
from jax import lax
from jax.experimental import pallas as pl
from jax.experimental.pallas import tpu as pltpu
from jax.sharding import PartitionSpec as P

TEMB = 512
HW = 16
PIX = HW * HW
GSIZE = 8
C = 256
TAPS = 9
KW = C * TAPS
HALF = 128 * TAPS

NORM_EPS = 1e-05
BETA_ONE = 0.9
BETA_TWO = 0.95
ADAM_EPS = 1e-06
DECAY = 0.01
RATE = 0.3
F32 = jnp.float32
BF16 = jnp.bfloat16
HIGH = lax.Precision.HIGHEST
MESH = pl.DeviceIdType.MESH
NN = (((1,), (0,)), ((), ()))
NT = (((1,), (1,)), ((), ()))
TN = (((0,), (0,)), ((), ()))
MIB = 1024 * 1024

GROWS = 32
XBIG = 4
XLAST = 3
XTAIL = 1
LEAD = 1
EARLY = 2
IMAGE = 3
LAG_B = 1
LAG_Z = 1.0
LAG_X = 1
LAG_Y = 1
DELAYS = (2, 7, 2)
VEC_ROWS = 22
LOSS_ROW = 24
MAIN = HALF + 128 + 128
SUM_ROWS = 16
CONV, TMB, ATTN = tuple(dict(conv=0, temb=0, attn=0))
HERE, W_IN = tuple(dict(_here=0, w_in=0))
LOG_TEN_THOUSAND = math.log(10000.0)


def dot(a, b, dims, precision=None):
    return lax.dot_general(a, b, dims, precision=precision, preferred_element_type=F32)


def iota(shape, axis):
    return lax.broadcasted_iota(jnp.int32, shape, axis)


def tap_order():
    wanted = (iota((1, HALF), 1) & 127) * TAPS + (iota((1, HALF), 1) >> 7)
    return jnp.where(iota((HALF, 1), 0) == wanted, 1.0, 0.0).astype(BF16)


def flip(value, mask):
    bit = 1
    while bit <= mask:
        if mask & bit:
            value = value + bit * (1 - 2 * ((value // bit) % 2))
        bit *= 2
    return value


def remote(src, dst, send_sem, recv_sem, target):
    return pltpu.make_async_remote_copy(
        src_ref=src, dst_ref=dst, send_sem=send_sem, recv_sem=recv_sem,
        device_id=target, device_id_type=MESH,
    )


def row_sum(value):
    return jnp.sum(value, axis=0, keepdims=True)


def group_mean(row):
    row = jnp.broadcast_to(row, (8, C))
    lane = iota(row.shape, 1)
    step = 1
    while step < GSIZE:
        up = pltpu.roll(row, C - step, 1)
        down = pltpu.roll(row, step, 1)
        row = row + jnp.where((lane & step) == 0, up, down)
        step *= 2
    return row[0:1] * (1.0 / (GSIZE * PIX))


def squares(value):
    return jnp.sum(jnp.sum(value * value, axis=1, keepdims=True), axis=0, keepdims=True)


def matrix_parts(lr):
    parts = []
    for k in range(4):
        for h in range(2):
            parts.append((1 + k, CONV, k, slice(h * HALF, (h + 1) * HALF), h,
                          slice(k * lr, (k + 1) * lr), slice(0, HALF)))
    for k in range(2):
        for j in range(4):
            top = (j % 2) * 2 * lr + k * lr
            parts.append((5 + k, TMB, k, slice(j * 128, (j + 1) * 128), j // 2,
                          slice(top, top + lr), slice(HALF + 128, MAIN)))
    for k in range(4):
        for h in range(2):
            parts.append((7 + k, ATTN, k, slice(h * 128, (h + 1) * 128), h,
                          slice(k * lr, (k + 1) * lr), slice(HALF, HALF + 128)))
    return parts


STATE = tuple(dict(
    w_in=0, m_in=0, v_in=0, conv_w=0, conv_m=0, conv_v=0, temb_w=0, temb_m=0, temb_v=0, attn_w=0, attn_m=0,
    attn_v=0, out_w=0, out_m=0, out_v=0, vectors=0, vec_m=0, vec_v=0,
))
PASSED = tuple(dict(
    in_first=0, in_second=0, conv_first=0, conv_second=0, temb_first=0, temb_second=0, attn_first=0,
    attn_second=0, out_first=0, out_second=0, vec_new=0, vec_first=0, vec_second=0, attn_grad=0,
))
UPDATES = tuple(dict(
    in_update=0, conv_update=0, temb_update=0, attn_update=0, out_update=0,
))
WEIGHTS = tuple(dict(
    w_in=0, conv_w=0, temb_w=0, attn_w=0, out_w=0,
))


class Names:
    def __init__(self, names, refs):
        assert len(names) == len(refs)
        self.__dict__.update(zip(names, refs))


def step_kernel(n, ny, nz, nx, dp, lr, images, names, *refs):
    r = Names(names, refs)
    rows_all = images * PIX
    scale = C ** -0.5
    me = lax.axis_index("chan")
    part = lax.axis_index("dp")
    z, y = me // ny, me % ny
    x, core = part // 2, part % 2
    sibling = (x * 2 + 1 - core, me)

    loads = {}

    def load(i, name):
        src, dst = getattr(r, name + "_hbm"), getattr(r, name)
        loads[name] = pltpu.make_async_copy(src, dst, r.load_sem.at[i])
        loads[name].start()

    for k in range(4):
        loads[k] = pltpu.make_async_copy(r.conv_w_hbm.at[k], r.conv_w.at[k], r.conv_sem.at[k])
        loads[k].start()
    for name in ("vectors", W_IN, "temb_w", "attn_w", "out_w"):
        load(STATE.index(name), name)
    for i, name in enumerate(("canvas", "noise")):
        load(len(STATE) + i, name)
    for i, name in enumerate(STATE):
        if name not in loads and name != "conv_w":
            load(i, name)

    offsets = [(i, j) for i in range(nz) for j in range(ny)][1:]
    place = {o: i for i, o in enumerate(offsets)}

    line = False
    inner = ((z + 1) // 2) % 2

    def z_at(i):
        if line and i >= 2:
            return inner * flip(z, 5 - i) + (1 - inner) * flip(z, i)
        return flip(z, i)

    def chan_at(o):
        return z_at(o[0]) * ny + flip(y, o[1])

    def pair_at(o):
        return flip(z, o[0]) * ny + flip(y, o[1])

    def next_part(k):
        return lax.rem(part + k, dp)

    barrier = pltpu.get_barrier_semaphore()
    for o in offsets:
        pl.semaphore_signal(barrier, inc=1, device_id=(part, chan_at(o)), device_id_type=MESH)
    for k in range(1, dp):
        pl.semaphore_signal(barrier, inc=1, device_id=(next_part(k), me), device_id_type=MESH)

    core_lanes = KW // 2
    use_x = nx == 2
    sum_rows = max(lr, 16)
    sum_chunks = 4 * lr // sum_rows
    gather_rows = min(GROWS, sum_rows)
    conv_chunks = 4 * lr // gather_rows
    chunks = list(range(conv_chunks))
    chunks.insert((conv_chunks + 1) // 2, None)

    def x_lanes(chunk):
        return (XLAST if chunk >= conv_chunks - XTAIL else XBIG) * 128 if use_x else 0

    def rows_of(chunk):
        return pl.ds(chunk * gather_rows, gather_rows)

    attn_x = lr // 2 if use_x and lr >= 32 else 0

    def near_ref(chunk, src, c):
        if chunk is None:
            start = c * 2 * lr + x * attn_x if attn_x else c * 2 * lr
            return r.attn_all.at[src, pl.ds(pl.multiple_of(start, 16), 2 * lr - attn_x), :]
        wide = x_lanes(chunk)
        start = c * core_lanes + x * wide if wide else c * core_lanes
        return r.whole.at[src, rows_of(chunk), pl.ds(pl.multiple_of(start, 128), core_lanes - wide)]

    def x_ref(chunk, src, c, side):
        if chunk is None:
            start = c * 2 * lr + side * (2 * lr - attn_x)
            return r.attn_all.at[src, pl.ds(pl.multiple_of(start, 16), attn_x), :]
        wide = x_lanes(chunk)
        start = c * core_lanes + side * (core_lanes - wide)
        return r.whole.at[src, rows_of(chunk), pl.ds(pl.multiple_of(start, 128), wide)]

    def has_x(chunk):
        return attn_x > 0 if chunk is None else x_lanes(chunk) > 0

    sends = []

    def send(*args):
        copy = remote(*args)
        copy.start()
        sends.append(copy)

    def index(chunk):
        return conv_chunks if chunk is None else chunk

    def send_near(chunk, src, o, target):
        i = index(chunk)
        ref = near_ref(chunk, src, core)
        send(ref, ref, r.near_send.at[i, place[o]], r.near_recv.at[i, place[o]], target)

    def send_core(chunk, src, o, piece):
        i = index(chunk)
        ref = near_ref(chunk, src, core) if piece == 0 else x_ref(chunk, src, core, 1 - x)
        send(ref, ref, r.core_send.at[piece, i, place[o]], r.core_recv.at[piece, i, place[o]], sibling)

    def pass_on(chunk, src, slot, target):
        i = index(chunk)

        @pl.when(inner == 1)
        def _():
            ref = near_ref(chunk, src, core)
            remote(ref, ref, r.pass_send.at[i, slot[0]], r.near_recv.at[i, place[(slot[1], 0)]], (part, target)).start()

    def passed(chunk):
        i = index(chunk)

        @pl.when(inner == 1)
        def _():
            for slot in range(4):
                ref = near_ref(chunk, me, core)
                remote(ref, ref, r.pass_send.at[i, slot], r.near_recv.at[i, 0], (part, me)).wait_send()

    def begin_y(chunk):
        for j in range(1, ny):
            send_near(chunk, me, (0, j), (part, chan_at((0, j))))

    def begin(chunk):
        send_near(chunk, me, (1, 0), (part, chan_at((1, 0))))
        if line:
            pass_on(chunk, me, (0, 2), flip(z, 3) * ny + y)
        else:
            for i in range(2, nz):
                send_near(chunk, me, (i, 0), (part, chan_at((i, 0))))

    def near_in(chunk, o):
        i = index(chunk)
        src = chan_at(o)
        ref = near_ref(chunk, src, core)
        remote(ref, ref, r.near_send.at[i, place[o]], r.near_recv.at[i, place[o]], (part, src)).wait_recv()
        if line and o[1] == 0:
            if o[0] == 1:
                pass_on(chunk, src, (1, 3), flip(z, 3) * ny + y)
            else:
                pass_on(chunk, src, o[:1] * 2, flip(z, 1) * ny + y)
        if o[1] == 0:
            for j in range(1, ny):
                send_near(chunk, src, (o[0], j), (part, chan_at((0, j))))
        if has_x(chunk):
            ref = x_ref(chunk, src, core, x)
            send(ref, ref, r.x_send.at[i, place[o]], r.x_recv.at[i, place[o]], ((1 - x) * 2 + core, me))
        send_core(chunk, src, o, 0)

    def x_in(chunk, o):
        if has_x(chunk):
            i = index(chunk)
            src = chan_at(o)
            ref = x_ref(chunk, src, core, 1 - x)
            remote(ref, ref, r.x_send.at[i, place[o]], r.x_recv.at[i, place[o]], ((1 - x) * 2 + core, me)).wait_recv()
            send_core(chunk, src, o, 1)

    def core_in(chunk, o):
        i = index(chunk)
        src = chan_at(o)
        pieces = [near_ref(chunk, src, 1 - core)]
        if has_x(chunk):
            pieces.append(x_ref(chunk, src, 1 - core, 1 - x))
        for piece, ref in enumerate(pieces):
            remote(ref, ref, r.core_send.at[piece, i, place[o]], r.core_recv.at[piece, i, place[o]], sibling).wait_recv()

    events = []
    for c, chunk in enumerate(chunks):
        if c >= 1:
            events.append((c - LEAD, -1, begin, (chunk,)))
        for i in range(1, nz):
            seen = c + LAG_B + i / (nz - 1) - 0.3
            events.append((seen, c, near_in, (chunk, (i, 0))))
            events.append((seen + LAG_X, c, x_in, (chunk, (i, 0))))
            for j in range(1, ny):
                events.append((seen + LAG_Y, c, near_in, (chunk, (i, j))))
                events.append((seen + LAG_Y + LAG_X, c, x_in, (chunk, (i, j))))
        for j in range(1, ny):
            events.append((LAG_B + c * 0.7, c, near_in, (chunk, (0, j))))
            events.append((LAG_B + c * 0.7 + LAG_X, c, x_in, (chunk, (0, j))))
    events.sort(key=lambda event: event[0])
    here = set()

    def until(time):
        while events and events[0][0] <= time:
            event = events.pop(0)
            event[2](*event[3])

    def arrived(*wanted):
        for chunk in wanted:
            if chunk not in here:
                here.add(chunk)
                until(max([event[0] for event in events if event[1] == chunks.index(chunk)], default=0))
                for o in offsets:
                    core_in(chunk, o)

    def conv_here(k):
        arrived(*range(k * lr // gather_rows, ((k + 1) * lr - 1) // gather_rows + 1))

    order = tap_order()
    r.order[...] = order

    def prepare(convs, extra=None):
        stack = []
        for k in convs:
            loads[k].wait()
            weight = r.conv_w[k].astype(BF16)
            stack += [weight[:, :HALF], weight[:, HALF:]]
        if extra is not None:
            stack.append(extra)
        mixed = dot(jnp.concatenate(stack, axis=0), r.order[...], NN)
        for i, k in enumerate(convs):
            for tap in range(TAPS):
                for h in range(2):
                    lanes = slice(tap * C + h * 128, tap * C + h * 128 + 128)
                    top = (2 * i + h) * lr
                    r.whole[me, k * lr:(k + 1) * lr, lanes] = mixed[top:top + lr, tap * 128:(tap + 1) * 128].astype(BF16)
        return mixed[2 * len(convs) * lr:]

    steps_row = iota((16, C), 0)
    steps_all = jnp.zeros((16, C), F32)
    for b in range(images):
        steps_all = jnp.where(steps_row == b, r.steps[b].astype(F32), steps_all)
    frequency = jnp.exp(-LOG_TEN_THOUSAND * iota((1, C), 1).astype(F32) / (TEMB // 2))
    angles = steps_all * frequency
    for i, wave in enumerate((jnp.sin(angles), jnp.cos(angles))):
        wave = jnp.where(steps_row < images, wave / (1.0 + jnp.exp(-wave)), 0.0)
        r.temb_act[:, i * C:(i + 1) * C] = wave.astype(BF16)

    prepare((0, 1))
    pl.semaphore_wait(barrier, n + dp - 2)
    begin(chunks[0])
    half = [chunk for chunk in chunks[:len(chunks) // 2] if chunk is not None]
    for chunk in half:
        begin_y(chunk)

    loads["vectors"].wait()
    loads[W_IN].wait()
    loads["temb_w"].wait()
    r.own_rows[...] = jnp.zeros_like(r.own_rows)
    r.own_rows[0:VEC_ROWS, 0:lr] = r.vectors[...]
    for block in range(2):
        shift = dot(r.temb_act[...], r.temb_w[block].astype(BF16), NT)
        for b in range(images):
            row = VEC_ROWS + block * images + b
            r.own_rows[row:row + 1, 0:lr] = (
                shift[b:b + 1, :] + r.vectors[17 + block:18 + block, :]
            ) + r.vectors[13 + 2 * block:14 + 2 * block, :]
    r.in_scr[...] = jnp.zeros_like(r.in_scr)
    r.in_scr[0:lr, 0:27] = r.w_in[...]
    turned = r.in_scr[...].T
    packed = [jnp.zeros((8, 128), F32), jnp.zeros((8, 128), F32)]
    for g in range(4):
        for i, rows in enumerate((r.own_rows[g * 8:g * 8 + 8, :], turned[g * 8:g * 8 + 8, :])):
            packed[i] += rows if g == 0 else pltpu.roll(rows, g * lr, 1)
    r.smalls[me, 0:8, :] = packed[0]
    r.smalls[me, 8:16, :] = packed[1]
    total = jnp.int32(0)
    for b in range(images):
        side = jnp.minimum(jnp.maximum(r.crop[b, 2], 0), HW)
        total += 3 * side * side
    r.counts[part] = jnp.full((8, 128), total, jnp.int32).astype(F32)
    for o in offsets:
        i = place[o]
        send(r.smalls.at[me], r.smalls.at[me], r.small_send.at[i], r.small_recv.at[i], (part, pair_at(o)))
    for i in range(1, dp):
        send(r.counts.at[part], r.counts.at[part], r.count_send.at[i - 1], r.count_recv.at[i - 1], (next_part(i), me))

    loads["attn_w"].wait()
    for k in range(4):
        r.attn_all[me, k * lr:(k + 1) * lr, :] = r.attn_w[k].astype(BF16)
    loads["out_w"].wait()
    r.out_scr[...] = jnp.zeros_like(r.out_scr)
    for h in range(2):
        r.out_scr[h * 8:h * 8 + 3, :] = r.out_w[:, h * HALF:(h + 1) * HALF]
    out_mixed = prepare((2, 3), r.out_scr[...].astype(BF16))
    for tap in range(TAPS):
        for h in range(2):
            r.out_taps[tap * 8:tap * 8 + 8, h * 128:(h + 1) * 128] = out_mixed[
                h * 8:h * 8 + 8, tap * 128:(tap + 1) * 128
            ]
    for chunk in chunks:
        if chunk not in half:
            begin_y(chunk)
    until(EARLY)

    lane = iota((1, PIX), 1)
    pix_x, pix_y = lane & (HW - 1), lane >> 4
    size = r.canvas.shape[2]
    loads["canvas"].wait()
    loads["noise"].wait()
    noise_rows, mask_rows, noisy_rows = [], [], []
    for b in range(images):
        phase = (jnp.broadcast_to(r.steps[b].astype(F32), (1, PIX)) / 1000.0 + 0.008) / 1.008
        alpha_bar = jnp.cos(phase * (math.pi / 2)) ** 2
        pick = jnp.where(iota((size, PIX), 0) == r.crop[b, 1] + pix_x, 1.0, 0.0)
        flat = r.canvas[b].reshape(3 * size, size)
        spread = dot(flat, pick, NN, HIGH).reshape(3, size, PIX)
        chosen = iota((size, PIX), 0) == r.crop[b, 0] + pix_y
        clean = jnp.sum(jnp.where(chosen[None], spread, 0.0), axis=1)
        noise_b = r.noise[:, b, :]
        noisy_rows.append(jnp.sqrt(alpha_bar) * clean + jnp.sqrt(1.0 - alpha_bar) * noise_b)
        noise_rows.append(noise_b)
        side = r.crop[b, 2]
        mask_rows.append(jnp.where((pix_x < side) & (pix_y < side), 1.0, 0.0))
    zeros5 = jnp.zeros((5, rows_all), F32)
    noisy = jnp.concatenate([jnp.concatenate(noisy_rows, axis=1), zeros5], axis=0)
    noise_all = jnp.concatenate([jnp.concatenate(noise_rows, axis=1), zeros5], axis=0)
    mask_all = jnp.concatenate(mask_rows, axis=1)

    lane_all = iota((8, rows_all), 1)
    px, py = lane_all & (HW - 1), (lane_all >> 4) & (HW - 1)

    def tap_shift(field, tap):
        dy, dx = tap // 3 - 1, tap % 3 - 1
        move = -(dy * HW + dx) % rows_all
        out = pltpu.roll(field, move, 1) if move else field
        inside = (px + dx >= 0) & (px + dx < HW) & (py + dy >= 0) & (py + dy < HW)
        return jnp.where(inside, out, 0.0)

    noisy = noisy.astype(BF16).astype(F32)
    r.rows_scr[...] = jnp.zeros_like(r.rows_scr)
    for tap in range(TAPS):
        moved = tap_shift(noisy, tap)
        for colour in range(3):
            r.rows_scr[colour * TAPS + tap:colour * TAPS + tap + 1, :] = moved[colour:colour + 1]
    r.taps0[...] = r.rows_scr[...].astype(BF16)

    until(IMAGE)

    for o in offsets:
        src = pair_at(o)
        remote(r.smalls.at[src], r.smalls.at[src], r.small_send.at[place[o]], r.small_recv.at[place[o]],
               (part, src)).wait_recv()
    for i in range(1, dp):
        p = lax.rem(part - i + dp, dp)
        remote(r.counts.at[p], r.counts.at[p], r.count_send.at[i - 1], r.count_recv.at[i - 1], (p, me)).wait_recv()
    lane_wide = iota((16, C), 1)
    unpacked = [jnp.zeros((16, C), F32) for g in range(4)]
    for j in range(n):
        block = jnp.concatenate([r.smalls[j], jnp.zeros((16, 128), F32)], axis=1)
        for g in range(4):
            piece = jnp.where((lane_wide >= g * lr) & (lane_wide < (g + 1) * lr), block, 0.0)
            move = (j - g) * lr % C
            unpacked[g] += pltpu.roll(piece, move, 1) if move else piece
    for g in range(4):
        r.vec[g * 8:g * 8 + 8, :] = unpacked[g][0:8]
        r.w_in_all[g * 8:g * 8 + 8, :] = unpacked[g][8:16]
    total = r.counts[0, 0:1, 0:1]
    for k in range(1, dp):
        total = total + r.counts[k, 0:1, 0:1]

    def vrow(i):
        return r.vec[i:i + 1, :]

    def span(b):
        return slice(b * PIX, (b + 1) * PIX)

    def conv_weight(k):
        return r.whole[:, k * lr:(k + 1) * lr, :].reshape(C, KW)

    def attn_weight(k):
        return r.attn_all[:, k * lr:(k + 1) * lr, :].reshape(C, C)

    col_x = iota((PIX, C), 0) & (HW - 1)
    blank = jnp.zeros((HW, C), BF16)
    hidden, xhat, dact, rstd, acts = r.hidden, r.xhat, r.dact, r.rstd, r.acts
    cols = (r.col0, r.col1, r.col2, r.col3)

    def norm_fwd(i, value, gain, shift, store):
        for b in range(images):
            image = value[span(b)]
            centred = image - group_mean(row_sum(image))
            inv = lax.rsqrt(group_mean(row_sum(centred * centred)) + NORM_EPS)
            normed = centred * inv
            scaled = normed * gain + shift
            gate = 0.5 * jnp.tanh(0.5 * scaled) + 0.5
            act = scaled * gate
            xhat[i, span(b), :] = normed
            dact[i, span(b), :] = gate + act * (1.0 - gate)
            rstd[i * images + b:i * images + b + 1, :] = inv
            store(b, act)

    def store_cols(ref, b, act):
        left = jnp.where(col_x > 0, pltpu.roll(act, 1, 0), 0.0)
        right = jnp.where(col_x < HW - 1, pltpu.roll(act, PIX - 1, 0), 0.0)
        for dx, moved in enumerate((left, act, right)):
            low = moved.astype(BF16)
            for dy in range(3):
                lanes = slice((3 * dy + dx) * C, (3 * dy + dx + 1) * C)
                base = b * PIX
                if dy == 0:
                    ref[base:base + HW, lanes] = blank
                    ref[base + HW:base + PIX, lanes] = low[:PIX - HW]
                elif dy == 1:
                    ref[base:base + PIX, lanes] = low
                else:
                    ref[base:base + PIX - HW, lanes] = low[HW:]
                    ref[base + PIX - HW:base + PIX, lanes] = blank

    def add_rows(value, first):
        return jnp.concatenate([value[span(b)] + vrow(first + b) for b in range(images)], axis=0)

    def chunk_of(k):
        return k * lr // sum_rows

    def block_fwd(block, source, target):
        norm_fwd(3 * block, hidden[source], vrow(3 * block), vrow(6 + 3 * block),
                 functools.partial(store_cols, cols[2 * block]))
        conv_here(2 * block)
        middle = dot(cols[2 * block][...], conv_weight(2 * block), NT)
        middle = add_rows(middle, VEC_ROWS + block * images)
        norm_fwd(3 * block + 1, middle, vrow(3 * block + 1), vrow(7 + 3 * block),
                 functools.partial(store_cols, cols[2 * block + 1]))
        conv_here(2 * block + 1)
        branch = dot(cols[2 * block + 1][...], conv_weight(2 * block + 1), NT)
        hidden[target] = hidden[source] + (branch + vrow(14 + 2 * block))

    def store_act(i):
        def store(b, act):
            acts[i, span(b), :] = act.astype(BF16)
        return store

    hidden[0] = dot(r.taps0[...], r.w_in_all[...].astype(BF16), TN) + vrow(12)
    block_fwd(0, 0, 1)

    norm_fwd(2, hidden[1], vrow(2), vrow(8), store_act(0))
    arrived(None)
    r.q_scr[...] = (dot(acts[0], attn_weight(0), NT) + vrow(19)).astype(BF16)
    r.k_scr[...] = dot(acts[0], attn_weight(1), NT).astype(BF16)
    r.v_scr[...] = (dot(acts[0], attn_weight(2), NT) + vrow(20)).astype(BF16)
    for b in range(images):
        scores = dot(r.q_scr[span(b), :], r.k_scr[span(b), :], NT) * scale
        raised = jnp.exp(scores - jnp.max(scores, axis=1, keepdims=True))
        soft = raised / jnp.sum(raised, axis=1, keepdims=True)
        r.probs[b] = soft
        r.mixed[span(b), :] = dot(soft.astype(BF16), r.v_scr[span(b), :], NN).astype(BF16)
    hidden[0] = hidden[1] + (dot(r.mixed[...], attn_weight(3), NT) + vrow(21))

    block_fwd(1, 0, 1)
    norm_fwd(5, hidden[1], vrow(5), vrow(11), store_act(1))

    out_low = r.out_taps[...].astype(BF16)
    fanned = dot(out_low, acts[1], NT)
    pred = jnp.zeros((8, rows_all), F32)
    for tap in range(TAPS):
        pred += tap_shift(fanned[tap * 8:tap * 8 + 8], tap)
    error = pred - noise_all
    masked = mask_all * error
    inverse = 1.0 / total
    loss = jnp.sum(jnp.sum(masked * error, axis=1, keepdims=True), axis=0, keepdims=True) * inverse
    grad_pred = (2.0 * masked * inverse).astype(BF16).astype(F32)
    spread_pred = jnp.concatenate(
        [tap_shift(grad_pred, TAPS - 1 - tap) for tap in range(TAPS)], axis=0
    ).astype(BF16)
    out_grad = dot(spread_pred, acts[1], NN)

    lanes_attn, lanes_temb = slice(HALF, HALF + 128), slice(HALF + 128, MAIN)

    def region(chunk):
        if chunk == ATTN:
            return slice(0, 4 * lr), lanes_attn
        if chunk == TMB:
            return slice(0, 4 * lr), lanes_temb
        return slice(chunk * sum_rows, (chunk + 1) * sum_rows), slice(0, HALF)

    def family(chunk):
        if chunk == "out":
            return (r.out_local, r.out_one, r.out_two, r.out_last), (slice(None), slice(None)), sum_chunks + 2
        i = sum_chunks + (ATTN, TMB).index(chunk) if isinstance(chunk, str) else chunk
        return (r.local, r.one, r.two, r.last), region(chunk), i

    def view(ref, i, where):
        return ref.at[(i,) + where]

    def reduce_one(chunk):
        (local, one, two, last), where, i = family(chunk)
        send(view(local, 1 - core, where), one.at[where], r.one_send.at[i], r.one_recv.at[i], sibling)

    def reduce_two(chunk):
        (local, one, two, last), where, i = family(chunk)
        remote(view(local, 1 - core, where), one.at[where], r.one_send.at[i], r.one_recv.at[i], sibling).wait_recv()
        both = local[(core,) + where].astype(F32) + one[where].astype(F32)
        two[(x,) + where] = both.astype(two.dtype)
        for m in range(1, nx):
            ref = view(two, x, where)
            send(ref, ref, r.two_send.at[i, m - 1], r.two_recv.at[i, m - 1], (lax.rem(x + m, nx) * 2 + core, me))

    def reduce_three(chunk):
        (local, one, two, last), where, i = family(chunk)
        for m in range(1, nx):
            sender = lax.rem(x - m + nx, nx)
            ref = view(two, sender, where)
            remote(ref, ref, r.two_send.at[i, m - 1], r.two_recv.at[i, m - 1], (sender * 2 + core, me)).wait_recv()
        summed = two[(0,) + where].astype(F32)
        for m in range(1, nx):
            summed = summed + two[(m,) + where].astype(F32)
        last[(core,) + where] = summed.astype(last.dtype)
        ref = view(last, core, where)
        send(ref, ref, r.three_send.at[i], r.three_recv.at[i], sibling)

    def reduce_four(chunk):
        (local, one, two, last), where, i = family(chunk)
        ref = view(last, 1 - core, where)
        remote(ref, ref, r.three_send.at[i], r.three_recv.at[i], sibling).wait_recv()

    due = []
    clock = [0]

    def run_due(entry):
        delay = {1: DELAYS[0], 2: DELAYS[1], 3: DELAYS[2]}
        stage, chunk = entry
        (reduce_one, reduce_two, reduce_three, reduce_four)[stage - 1](chunk)
        if stage < 4:
            due.append((clock[0] + delay[stage], (stage + 1, chunk)))

    def tick():
        clock[0] += 1
        for item in [item for item in due if item[0] <= clock[0]]:
            due.remove(item)
            run_due(item[1])

    def ready(chunk):
        run_due((1, chunk))

    def finish(chunk=None):
        while True:
            left = [item for item in due if chunk is None or item[1][1] == chunk]
            if not left:
                return
            item = min(left, key=lambda item: (item[1][0], item[0]))
            due.remove(item)
            run_due(item[1])

    for h in range(2):
        for tap in range(TAPS):
            r.out_local[h, :, tap * 128:(tap + 1) * 128] = out_grad[tap * 8:tap * 8 + 8, h * 128:(h + 1) * 128]
    ready("out")
    grad = dot(spread_pred, out_low, TN)

    gvec = r.gvec
    gvec[...] = jnp.zeros_like(gvec)
    pick_own = jnp.where(iota((lr, C), 1) == iota((lr, C), 0) + me * lr, 1.0, 0.0).astype(BF16)
    hole = jnp.zeros((HW, C), F32)

    def own_rows(low):
        return dot(pick_own, low, NT).astype(BF16)

    def norm_back(i, grad, gain_row):
        outs = []
        gain = vrow(gain_row)
        gain_sum = jnp.zeros((1, C), F32)
        shift_sum = jnp.zeros((1, C), F32)
        for b in range(images):
            slope = grad[span(b)] * dact[i, span(b), :]
            normed = xhat[i, span(b), :]
            shift_b = row_sum(slope)
            gain_b = row_sum(slope * normed)
            mean_one = group_mean(shift_b * gain)
            mean_two = group_mean(gain_b * gain)
            inv = rstd[i * images + b:i * images + b + 1, :]
            outs.append(inv * (slope * gain - mean_one - normed * mean_two))
            gain_sum += gain_b
            shift_sum += shift_b
        gvec[gain_row:gain_row + 1, :] = gain_sum
        gvec[6 + gain_row:7 + gain_row, :] = shift_sum
        return jnp.concatenate(outs, axis=0)

    def conv_back(k, low):
        own = dot(own_rows(low), cols[k][...], NN)
        for h in range(2):
            for tap in range(TAPS):
                r.local[h, k * lr:(k + 1) * lr, tap * 128:(tap + 1) * 128] = own[
                    :, tap * C + h * 128:tap * C + h * 128 + 128
                ].astype(BF16)
        if k * lr % sum_rows == 0:
            ready(chunk_of(k))
        tick()
        parts = dot(low, conv_weight(k), NN)
        outs = []
        for b in range(images):
            sides = []
            for dx in range(3):
                up = parts[span(b), dx * C:(dx + 1) * C]
                mid = parts[span(b), (3 + dx) * C:(4 + dx) * C]
                down = parts[span(b), (6 + dx) * C:(7 + dx) * C]
                sides.append(
                    mid
                    + jnp.concatenate([up[HW:], hole], axis=0)
                    + jnp.concatenate([hole, down[:PIX - HW]], axis=0)
                )
            left = pltpu.roll(jnp.where(col_x > 0, sides[0], 0.0), PIX - 1, 0)
            right = pltpu.roll(jnp.where(col_x < HW - 1, sides[2], 0.0), 1, 0)
            outs.append(sides[1] + left + right)
        tick()
        return jnp.concatenate(outs, axis=0)

    def block_back(block, grad):
        gvec[14 + 2 * block:15 + 2 * block, :] = row_sum(grad)
        back = conv_back(2 * block + 1, grad.astype(BF16))
        middle = norm_back(3 * block + 1, back, 3 * block + 1)
        r.gsum[...] = jnp.zeros_like(r.gsum)
        for b in range(images):
            r.gsum[b:b + 1, :] = row_sum(middle[span(b)])
        whole_sum = row_sum(r.gsum[...])
        gvec[13 + 2 * block:14 + 2 * block, :] = whole_sum
        gvec[17 + block:18 + block, :] = whole_sum
        own = dot(pick_own, r.gsum[...].astype(BF16), NT).astype(BF16)
        temb = dot(own, r.temb_act[...], NN)
        for j in range(4):
            top = (j % 2) * 2 * lr + block * lr
            r.local[j // 2, top:top + lr, lanes_temb] = temb[:, j * 128:(j + 1) * 128].astype(BF16)
        if block == 0:
            ready(TMB)
        tick()
        back = conv_back(2 * block, middle.astype(BF16))
        return grad + norm_back(3 * block, back, 3 * block)

    grad = norm_back(5, grad, 5)
    tick()
    grad = block_back(1, grad)
    tick()

    gvec[21:22, :] = row_sum(grad)
    low = grad.astype(BF16)

    def attn_own(k, low, field):
        own = dot(own_rows(low), field, NN)
        for h in range(2):
            r.local[h, k * lr:(k + 1) * lr, lanes_attn] = own[:, h * 128:(h + 1) * 128].astype(BF16)

    attn_own(3, low, r.mixed[...])
    mixed_low = dot(low, attn_weight(3), NN).astype(BF16)
    grads_q, grads_k, grads_v = [], [], []
    for b in range(images):
        image = mixed_low[span(b)]
        soft = r.probs[b]
        grad_soft = dot(image, r.v_scr[span(b), :], NT)
        grads_v.append(dot(soft.astype(BF16), image, TN))
        weighed = soft * grad_soft
        slope = (weighed - soft * jnp.sum(weighed, axis=1, keepdims=True)).astype(BF16)
        grads_q.append(scale * dot(slope, r.k_scr[span(b), :], NN))
        grads_k.append(scale * dot(slope, r.q_scr[span(b), :], TN))
    tick()
    back = jnp.zeros((rows_all, C), F32)
    for i, grads in enumerate((grads_q, grads_k, grads_v)):
        full = jnp.concatenate(grads, axis=0)
        if i != 1:
            gvec[19 + i // 2:20 + i // 2, :] = row_sum(full)
        low = full.astype(BF16)
        attn_own(i, low, acts[0])
        back += dot(low, attn_weight(i), NN)
    ready(ATTN)
    tick()
    grad = grad + norm_back(2, back, 2)
    tick()

    grad = block_back(0, grad)
    tick()
    gvec[12:13, :] = row_sum(grad)
    in_grad = dot(own_rows(grad.astype(BF16)), r.taps0[...], NT)

    own_vec = jnp.where(iota((32, 128), 1) < lr, pltpu.roll(gvec[...], lax.rem(C - me * lr, C), 1)[:, 0:128], 0.0)
    own_vec = jnp.where(iota((32, 128), 0) == LOSS_ROW, loss, own_vec)
    own_vec = jnp.where(iota((32, 128), 1) < lr, own_vec, 0.0)
    packed = [jnp.zeros((8, 128), F32), jnp.zeros((8, 128), F32)]
    for g in range(4):
        rows = own_vec[g * 8:g * 8 + 8, :]
        packed[0] += rows if g == 0 else pltpu.roll(rows, g * lr, 1)
    for g in range(lr // 8):
        rows = jnp.concatenate([in_grad[g * 8:g * 8 + 8, :], jnp.zeros((8, 96), F32)], axis=1)
        packed[1] += rows if g == 0 else pltpu.roll(rows, g * 32, 1)
    r.tiny[part, 0:8, :] = packed[0]
    r.tiny[part, 8:16, :] = packed[1]
    for i in range(1, dp):
        send(r.tiny.at[part], r.tiny.at[part], r.tiny_send.at[i - 1], r.tiny_recv.at[i - 1], (next_part(i), me))
    tick()

    for name in STATE:
        if name in loads and name not in ("vectors", W_IN, "temb_w", "attn_w", "out_w"):
            loads[name].wait()
    count = jnp.broadcast_to(r.count_step[0].astype(F32), (1, 128))
    fix_one = (1.0 / (1.0 - jnp.exp(math.log(BETA_ONE) * count)))[:, 0:1]
    fix_two = (1.0 / (1.0 - jnp.exp(math.log(BETA_TWO) * count)))[:, 0:1]

    def adapt(grad, first, second):
        first_new = BETA_ONE * first + (1.0 - BETA_ONE) * grad
        second_new = BETA_TWO * second + (1.0 - BETA_TWO) * grad * grad
        direction = first_new * fix_one / (jnp.sqrt(second_new * fix_two) + ADAM_EPS)
        return first_new, second_new, direction

    sums = {}

    def lamb(number, name, at, grad):
        names = (W_IN, "m_in", "v_in") if name == "in" else (name + "_w", name + "_m", name + "_v")
        weight, first, second = (getattr(r, each)[at] for each in names)
        first, second, direction = adapt(grad, first, second)
        update = direction + DECAY * weight
        getattr(r, name + "_first")[at] = first
        getattr(r, name + "_second")[at] = second
        getattr(r, name + "_update")[at] = update
        pair = (squares(weight), squares(update))
        if number in sums:
            pair = (sums[number][0] + pair[0], sums[number][1] + pair[1])
        sums[number] = pair

    every = slice(None)
    outward = []

    def put(name, k=None):
        src, dst = getattr(r, name), getattr(r, name + "_hbm")
        if k is not None:
            src, dst = src.at[k], dst.at[k]
        copy = pltpu.make_async_copy(src, dst, r.out_sem.at[len(outward)])
        copy.start()
        outward.append(copy)

    def put_all(name, k=None):
        for kind in ("first", "second", "update"):
            put(name + "_" + kind, k)

    def conv_steps(which, natural):
        for number, name, k, lanes, h, rows, held in matrix_parts(lr):
            if name == CONV and chunk_of(k) in which:
                top = h * len(which) * sum_rows + k * lr - min(which) * sum_rows
                lamb(number, name, (k, every, lanes), natural[top:top + lr])
                if h == 1:
                    put_all(CONV, k)

    def push(chunk, stage):
        for item in [item for item in due if item[1][1] == chunk]:
            while item is not None and item[1][0] <= stage:
                due.remove(item)
                run_due(item[1])
                item = next((left for left in due if left[1][1] == chunk), None)

    def whole_parts(which):
        for number, name, k, lanes, h, rows, held in matrix_parts(lr):
            if name == which:
                value = r.last[h, rows, held].astype(F32)
                if name == ATTN:
                    r.attn_grad[k, :, lanes] = value
                lamb(number, name, (k, every, lanes), value)
        put_all(which)

    early = list(range(1, sum_chunks))
    for chunk in early + ["out"]:
        finish(chunk)
    push(0, 2)
    push(TMB, 2)
    stack = [r.last[h, sum_rows:4 * lr, 0:HALF] for h in range(2)]
    stack += [jnp.concatenate([r.out_last[h], jnp.zeros((8, HALF), F32)], axis=0).astype(BF16) for h in range(2)]
    natural = dot(jnp.concatenate(stack, axis=0), r.order[...], NT)
    finish(ATTN)
    whole_parts(ATTN)
    put("attn_grad")
    push(TMB, 3)
    push(0, 3)
    conv_steps(early, natural)
    top = 2 * (4 * lr - sum_rows)
    for h in range(2):
        lamb(11, "out", (every, slice(h * HALF, (h + 1) * HALF)), natural[top + h * 16:top + h * 16 + 3])
    put_all("out")
    finish(TMB)
    whole_parts(TMB)
    finish()
    natural = dot(jnp.concatenate([r.last[h, 0:sum_rows, 0:HALF] for h in range(2)], axis=0), r.order[...], NT)
    conv_steps([0], natural)

    for i in range(1, dp):
        p = lax.rem(part - i + dp, dp)
        remote(r.tiny.at[p], r.tiny.at[p], r.tiny_send.at[i - 1], r.tiny_recv.at[i - 1], (p, me)).wait_recv()
    tiny = r.tiny[0]
    for k in range(1, dp):
        tiny = tiny + r.tiny[k]
    for g in range(4):
        rows = tiny[0:8] if g == 0 else pltpu.roll(tiny[0:8], 128 - g * lr, 1)
        r.own_rows[g * 8:g * 8 + 8, :] = rows
    for g in range(lr // 8):
        rows = tiny[8:16] if g == 0 else pltpu.roll(tiny[8:16], 128 - g * 32, 1)
        r.in_scr[g * 8:g * 8 + 8, :] = rows
    lamb(0, "in", (every, every), r.in_scr[0:lr, 0:27])
    put_all("in")

    row = iota((SUM_ROWS, 128), 0)
    lane = iota((SUM_ROWS, 128), 1)
    table = jnp.zeros((SUM_ROWS, 128), F32)
    for number in range(11):
        for side in range(2):
            table = jnp.where((row == number) & (lane == side), sums[number][side], table)
    r.tables[me] = table
    for o in offsets:
        i = place[o]
        send(r.tables.at[me], r.tables.at[me], r.sum_send.at[i], r.sum_recv.at[i], (part, pair_at(o)))
    first, second, direction = adapt(r.own_rows[0:VEC_ROWS, 0:lr], r.vec_m[...], r.vec_v[...])
    r.vec_new[...] = r.vectors[...] - RATE * direction
    r.vec_first[...] = first
    r.vec_second[...] = second
    for name in ("vec_new", "vec_first", "vec_second"):
        put(name)
    for copy in sends[:-len(offsets)]:
        copy.wait_send()
    del sends[:-len(offsets)]
    if line:
        for chunk in chunks:
            passed(chunk)
    for o in offsets:
        src = pair_at(o)
        remote(r.tables.at[src], r.tables.at[src], r.sum_send.at[place[o]], r.sum_recv.at[place[o]],
               (part, src)).wait_recv()
    total = r.tables[0]
    for k in range(1, n):
        total = total + r.tables[k]
    for side in range(2):
        total = jnp.where((row == 11) & (lane == side), sums[11][side], total)
    total = jnp.where((row == 12) & (lane == 0), r.own_rows[LOSS_ROW:LOSS_ROW + 1, 0:1], total)
    r.norms[...] = total
    put("norms")
    for copy in sends:
        copy.wait_send()
    for copy in outward:
        copy.wait()


def update_kernel(names, *refs):
    r = Names(names, refs)
    copies = []

    def copy(src, dst):
        made = pltpu.make_async_copy(src, dst, r.sem.at[len(copies)])
        made.start()
        copies.append(made)
        return made

    copy(r.norms, r.norms_in)
    loads = {}
    for k in range(4):
        loads[(CONV, k)] = [
            copy(getattr(r, name).at[k], getattr(r, name + HERE).at[k]) for name in ("conv_w", "conv_update")
        ]
    for name in ("in", TMB, ATTN, "out"):
        weight = W_IN if name == "in" else name + "_w"
        loads[name] = [copy(getattr(r, each), getattr(r, each + HERE)) for each in (weight, name + "_update")]
    passing = [(name, copy(getattr(r, name), getattr(r, name + HERE))) for name in PASSED]
    copies[0].wait()
    outward = []

    def ratio(number):
        pair = r.norms_in[number:number + 1, 0:2]
        return RATE * jnp.sqrt(pair[:, 0:1] / (pair[:, 1:2] + 1e-06))

    r.norms_here[...] = jnp.sqrt(r.norms_in[...].T[0:2, 0:12])
    outward.append(copy(r.norms_here, r.norms_out))
    r.loss_out[...] = r.norms_in[12:13, 0:1]
    for number, name, k in [(0, "in", None)] + [(1 + k, CONV, k) for k in range(4)] + [
        (5 + k, TMB, k) for k in range(2)
    ] + [(7 + k, ATTN, k) for k in range(4)] + [(11, "out", None)]:
        weight_name = W_IN if name == "in" else name + "_w"
        for wait in loads.pop((name, k) if name == CONV else name, ()):
            wait.wait()
        at = (slice(None), slice(None)) if k is None else (k, slice(None), slice(None))
        here, target = getattr(r, name + HERE), getattr(r, name + "_new_out")
        new = getattr(r, weight_name + HERE)[at] - ratio(number) * getattr(r, name + "_update_here")[at]
        here[at] = new
        last = k in (None, {CONV: k, TMB: 1, ATTN: 3}.get(name))
        if name == CONV:
            outward.append(copy(here.at[k], target.at[k]))
        elif last:
            outward.append(copy(here, target))
        if k is not None:
            low = getattr(r, name + "_low_here")
            low[at] = new.astype(BF16)
            if name == CONV:
                outward.append(copy(low.at[k], getattr(r, name + "_low_out").at[k]))
            elif last:
                outward.append(copy(low, getattr(r, name + "_low_out")))
    for name, made in passing:
        made.wait()
        outward.append(copy(getattr(r, name + HERE), getattr(r, name + "_out")))
    for made in outward:
        made.wait()


def vmem_spec():
    return pl.BlockSpec(memory_space=pltpu.VMEM)


def smem_spec():
    return pl.BlockSpec(memory_space=pltpu.SMEM)


def hbm_spec():
    return pl.BlockSpec(memory_space=pltpu.HBM)


def shape(dims, kind=F32):
    return jax.ShapeDtypeStruct(dims, kind)


def per_device(n, dp, canvas, crop_boxes, time_steps, noise_field, step_count, *state):
    images = canvas.shape[0]
    rows_all = images * PIX
    own = dict(zip(STATE, state))
    lr = own["conv_w"].shape[1]
    nx = dp // 2
    ny = 1 << ((n.bit_length() - 2) // 2)
    nz = n // ny
    dma = pltpu.SemaphoreType.DMA
    chunks = 4 * lr // min(GROWS, max(lr, 16)) + 1

    made = {}
    for key, name in (("in", W_IN), (CONV, "conv_w"), (TMB, "temb_w"), (ATTN, "attn_w"), ("out", "out_w")):
        for kind in ("first", "second", "update"):
            made[key + "_" + kind] = own[name].shape
    for name in ("vec_new", "vec_first", "vec_second"):
        made[name] = own["vectors"].shape
    made["attn_grad"] = own["attn_w"].shape
    made["norms"] = (SUM_ROWS, 128)

    inputs = ["crop", "steps", "count_step", "canvas_hbm", "noise_hbm"] + [name + "_hbm" for name in STATE]
    scratch = {name: pltpu.VMEM(own[name].shape, F32) for name in STATE}
    wide = max(nx - 1, 1)
    scratch.update(
        canvas=pltpu.VMEM(canvas.shape, F32), noise=pltpu.VMEM(noise_field.shape, F32),
        load_sem=dma((len(STATE) + 2,)), conv_sem=dma((4,)),
        whole=pltpu.VMEM((n, 4 * lr, KW), BF16), attn_all=pltpu.VMEM((n, 4 * lr, C), BF16),
        smalls=pltpu.VMEM((n, 16, 128), F32), counts=pltpu.VMEM((dp, 8, 128), F32),
        near_send=dma((chunks, n - 1)), pass_send=dma((chunks, 4)), near_recv=dma((chunks, n - 1)),
        x_send=dma((chunks, n - 1)), x_recv=dma((chunks, n - 1)),
        core_send=dma((2, chunks, n - 1)), core_recv=dma((2, chunks, n - 1)),
        small_send=dma((n - 1,)), small_recv=dma((n - 1,)), count_send=dma((dp - 1,)), count_recv=dma((dp - 1,)),
        order=pltpu.VMEM((HALF, HALF), BF16), temb_act=pltpu.VMEM((16, TEMB), BF16),
        own_rows=pltpu.VMEM((32, 128), F32), in_scr=pltpu.VMEM((128, 128), F32),
        out_scr=pltpu.VMEM((16, HALF), F32), out_taps=pltpu.VMEM((72, C), F32),
        vec=pltpu.VMEM((32, C), F32), w_in_all=pltpu.VMEM((32, C), F32),
        hidden=pltpu.VMEM((2, rows_all, C), F32), xhat=pltpu.VMEM((6, rows_all, C), F32),
        dact=pltpu.VMEM((6, rows_all, C), F32), rstd=pltpu.VMEM((-(-6 * images // 8) * 8, C), F32),
        col0=pltpu.VMEM((rows_all, KW), BF16), col1=pltpu.VMEM((rows_all, KW), BF16),
        col2=pltpu.VMEM((rows_all, KW), BF16), col3=pltpu.VMEM((rows_all, KW), BF16),
        taps0=pltpu.VMEM((32, rows_all), BF16), rows_scr=pltpu.VMEM((32, rows_all), F32),
        acts=pltpu.VMEM((2, rows_all, C), BF16), q_scr=pltpu.VMEM((rows_all, C), BF16),
        k_scr=pltpu.VMEM((rows_all, C), BF16), v_scr=pltpu.VMEM((rows_all, C), BF16),
        probs=pltpu.VMEM((images, PIX, PIX), F32), mixed=pltpu.VMEM((rows_all, C), BF16),
        gvec=pltpu.VMEM((32, C), F32), gsum=pltpu.VMEM((16, C), F32),
        local=pltpu.VMEM((2, 4 * lr, MAIN), BF16), one=pltpu.VMEM((4 * lr, MAIN), BF16),
        two=pltpu.VMEM((nx, 4 * lr, MAIN), BF16), last=pltpu.VMEM((2, 4 * lr, MAIN), BF16),
        out_local=pltpu.VMEM((2, 8, HALF), F32), out_one=pltpu.VMEM((8, HALF), F32),
        out_two=pltpu.VMEM((nx, 8, HALF), F32), out_last=pltpu.VMEM((2, 8, HALF), F32),
        one_send=dma((chunks + 2,)), one_recv=dma((chunks + 2,)),
        two_send=dma((chunks + 2, wide)), two_recv=dma((chunks + 2, wide)),
        three_send=dma((chunks + 2,)), three_recv=dma((chunks + 2,)),
        tiny=pltpu.VMEM((dp, 16, 128), F32), tiny_send=dma((dp - 1,)), tiny_recv=dma((dp - 1,)),
        tables=pltpu.VMEM((n, SUM_ROWS, 128), F32), sum_send=dma((n - 1,)), sum_recv=dma((n - 1,)),
    )
    scratch.update({name: pltpu.VMEM(dims, F32) for name, dims in made.items()})
    scratch["out_sem"] = dma((40,))
    names = inputs + [name + "_hbm" for name in made] + list(scratch)
    results = pl.pallas_call(
        functools.partial(step_kernel, n, ny, nz, nx, dp, lr, images, names),
        out_shape=tuple(shape(dims) for dims in made.values()),
        in_specs=[smem_spec()] * 3 + [hbm_spec()] * (2 + len(STATE)),
        out_specs=tuple(hbm_spec() for _ in made),
        scratch_shapes=list(scratch.values()),
        compiler_params=pltpu.CompilerParams(
            collective_id=1, has_side_effects=True, vmem_limit_bytes=64 * MIB
        ),
        name="step",
    )(crop_boxes, time_steps, step_count, canvas, noise_field, *state)
    results = dict(zip(made, results))

    outs = {"norms_out": shape((2, 12)), "loss_out": shape((1, 1))}
    for name in PASSED:
        outs[name + "_out"] = shape(made[name])
    for key in ("in", CONV, TMB, ATTN, "out"):
        outs[key + "_new_out"] = shape(made[key + "_update"])
    for key in (CONV, TMB, ATTN):
        outs[key + "_low_out"] = shape(made[key + "_update"], BF16)
    held = {name + HERE: pltpu.VMEM(own[name].shape, F32) for name in WEIGHTS}
    held.update({name + HERE: pltpu.VMEM(made[name], F32) for name in UPDATES + PASSED})
    held["norms_here"] = pltpu.VMEM((2, 12), F32)
    held["norms_in"] = pltpu.VMEM((SUM_ROWS, 128), F32)
    for key in ("in", CONV, TMB, ATTN, "out"):
        held[key + HERE] = pltpu.VMEM(made[key + "_update"], F32)
    for key in (CONV, TMB, ATTN):
        held[key + "_low_here"] = pltpu.VMEM(made[key + "_update"], BF16)
    held["sem"] = dma((80,))
    inputs = ["norms"] + list(WEIGHTS) + list(UPDATES) + list(PASSED)
    names = inputs + list(outs) + list(held)
    updated = pl.pallas_call(
        functools.partial(update_kernel, names),
        out_shape=tuple(outs.values()),
        in_specs=[hbm_spec()] * len(inputs),
        out_specs=tuple(vmem_spec() if name == "loss_out" else hbm_spec() for name in outs),
        scratch_shapes=list(held.values()),
        compiler_params=pltpu.CompilerParams(vmem_limit_bytes=64 * MIB),
        name="update",
    )(results["norms"], *[own[name] for name in WEIGHTS], *[results[name] for name in UPDATES + PASSED])
    done = dict(zip(outs, updated))
    final = [done["loss_out"].reshape(()), done["norms_out"].T]
    for key in ("in", CONV, TMB, ATTN, "out"):
        final += [done[key + "_new_out"], done[key + "_first_out"], done[key + "_second_out"]]
        if key + "_low_out" in done:
            final.append(done[key + "_low_out"])
    final += [done["vec_new_out"], done["vec_first_out"], done["vec_second_out"], done["attn_grad_out"]]
    return tuple(final)


def solution(mesh):
    chan_row = P("chan", None)
    chan_mid = P(None, "chan", None)
    chan_vec = P(None, "chan")
    return jax.shard_map(
        functools.partial(per_device, mesh.shape["chan"], mesh.shape["dp"]),
        mesh=mesh,
        in_specs=(P("dp", None, None, None), P("dp", None), P("dp"), P(None, "dp", None), P())
        + (chan_row,) * 3 + (chan_mid,) * 9 + (P(),) * 3 + (chan_vec,) * 3,
        out_specs=(P(), P()) + (chan_row,) * 3 + (chan_mid,) * 12 + (P(),) * 3 + (chan_vec,) * 3 + (chan_mid,),
        check_vma=False,
    )
```
